32 devices in a mesh: pipe: 4 (over y, x), dp: 2 (over core), tensor: 4 (over z).
Axes of the slice: x: 2, y: 2, z: 4, core: 2. Of those that a mesh axis runs over, the one named last changes fastest.
Arguments:
- raw_pages: bfloat16 [4, 2, 1200, 2048], P('pipe', 'dp', 'tensor'), may hold values from -40 to 40
- w_merge: float32 [2048, 1024], P(('pipe', 'dp', 'tensor')), may hold values from -0.125 to 0.125
- merge_gain: float32 [2048], P(('pipe', 'dp', 'tensor')), may hold values from 0.5 to 1.5
- merge_bias: float32 [2048], P(('pipe', 'dp', 'tensor')), may hold values from -1.5 to 1.5
- final_gain: float32 [1024], P(('pipe', 'dp', 'tensor')), may hold values from 0.2 to 2
- final_bias: float32 [1024], P(('pipe', 'dp', 'tensor')), may hold values from -3 to 3
- w_qkv: float32 [4, 1024, 3, 1024], P('pipe', 'dp', None, 'tensor'), may hold values from -0.1875 to 0.1875
- w_proj: float32 [4, 1024, 1024], P('pipe', 'tensor', 'dp'), may hold values from -0.75 to 0.75
- w_fc1: float32 [4, 1024, 4096], P('pipe', 'dp', 'tensor'), may hold values from -0.1875 to 0.1875
- w_fc2: float32 [4, 4096, 1024], P('pipe', 'tensor', 'dp'), may hold values from -0.1875 to 0.1875
- qv_bias: float32 [4, 2, 1024], P('pipe', None, 'tensor'), may hold values from -1.5 to 1.5
- fc1_bias: float32 [4, 4096], P('pipe'), may hold values from -1.5 to 1.5
- rel_table: float32 [4, 361, 32], P('pipe', None, 'tensor'), may hold values from -5 to 5
- ln_gain: float32 [4, 2, 1024], P('pipe'), may hold values from 0.5 to 1.5
- ln_bias: float32 [4, 2, 1024], P('pipe'), may hold values from -1.5 to 1.5
- out_bias: float32 [4, 2, 1024], P('pipe'), may hold values from -1.5 to 1.5
- cotangent: bfloat16 [4, 4, 2, 1200, 1024], P('pipe', None, 'dp', 'tensor'), may hold values from -6 to 6
Outputs:
- hidden_states: bfloat16 [4, 4, 2, 1200, 1024], P('pipe', None, 'dp', 'tensor')
- grad_raw: bfloat16 [4, 2, 1200, 2048], P('pipe', 'dp', 'tensor')
- grad_w_merge: float32 [2048, 1024], P(('pipe', 'dp', 'tensor'))
- grad_merge_gain: float32 [2048], P(('pipe', 'dp', 'tensor'))
- grad_merge_bias: float32 [2048], P(('pipe', 'dp', 'tensor'))
- grad_final_gain: float32 [1024], P(('pipe', 'dp', 'tensor'))
- grad_final_bias: float32 [1024], P(('pipe', 'dp', 'tensor'))
- grad_w_qkv: float32 [4, 1024, 3, 1024], P('pipe', 'dp', None, 'tensor')
- grad_w_proj: float32 [4, 1024, 1024], P('pipe', 'tensor', 'dp')
- grad_w_fc1: float32 [4, 1024, 4096], P('pipe', 'dp', 'tensor')
- grad_w_fc2: float32 [4, 4096, 1024], P('pipe', 'tensor', 'dp')
- grad_qv_bias: float32 [4, 2, 1024], P('pipe', None, 'tensor')
- grad_fc1_bias: float32 [4, 4096], P('pipe')
- grad_rel_table: float32 [4, 361, 32], P('pipe', None, 'tensor')
- grad_ln_gain: float32 [4, 2, 1024], P('pipe')
- grad_ln_bias: float32 [4, 2, 1024], P('pipe')
- grad_out_bias: float32 [4, 2, 1024], P('pipe')
The draws below stay inside these ranges and needn't reach their ends.
All inputs are finite; a program needn't handle non-finite values.
Results may differ from the reference program's by a relative error of at most 0.029.
Values may be sent and summed in bfloat16 or wider, within the bound.
No kernel may reach another device: no remote copies, remote signals or barrier semaphores. Data moves between devices by JAX's collectives and lax.ppermute only.
A program may use at most 192 MiB of HBM per device.

```python
import jax
import jax.numpy as jnp
import numpy as np
from jax import lax

D = 1024
HEADS = 32
HEAD = 32
FF = 4096
MERGE_IN = 2048
WIN = 10
SHIFT = 5
WIN_ROWS = 4
WIN_COLS = 3
GRID_H = 40
GRID_W = 30
TOKENS_PAGE = 1200
TABLE_ROWS = 361
MICRO = 4
PAGES_MB = 2
LAYERS = 4
N_PIPE = 4


def draw_raw_pages(key, part):
    key = jax.random.fold_in(key, 7)
    value_key, column_key, row_key = jax.random.split(key, 3)
    shape_all = (MICRO, PAGES_MB, TOKENS_PAGE, MERGE_IN)
    column_scale = jnp.exp(jax.random.uniform(column_key, (MERGE_IN,), jnp.float32, 0.0, 2.3))
    row_scale = jnp.exp(jax.random.uniform(row_key, (MICRO, PAGES_MB, TOKENS_PAGE, 1), jnp.float32, 0.0, 2.3))
    base_values = jnp.clip(jax.random.normal(value_key, shape_all, jnp.float32), -3.9, 3.9)
    return jnp.clip(0.1 * base_values * column_scale * row_scale, -40.0, 40.0).astype(jnp.bfloat16)


def levels(rng, shape, cuts, smallest, high):
    loudness, own = 1.0, jax.random.fold_in(rng, 6)
    for axis_at, parts in cuts:
        heights = jnp.exp(jax.random.uniform(jax.random.fold_in(own, axis_at), (parts,), jnp.float32, smallest / len(cuts), high / len(cuts)))
        loudness = loudness * jnp.repeat(heights, shape[axis_at] // parts).reshape([-1 if axis == axis_at else 1 for axis in range(len(shape))])
    return loudness


def scatter_about(stream_key, dims, scale, most, cuts=(), kind=jnp.bfloat16):
    array = scale * jax.random.normal(stream_key, dims, jnp.float32)
    if cuts:
        array = array * levels(stream_key, dims, cuts, -0.22, 0.18)
    return jnp.clip(array, -most, most).astype(kind)


def setup_inputs(seed: int = 0) -> dict:
    key_list = jax.random.split(jax.random.key(seed), 18)
    raw_pages = draw_raw_pages(jax.random.fold_in(key_list[17], 71), 0)
    w_merge = scatter_about(key_list[1], (MERGE_IN, D), MERGE_IN ** -0.5, 0.125, ((0, 32),), jnp.float32)
    merge_gain = jnp.clip(1.0 + 0.1 * jax.random.normal(key_list[2], (MERGE_IN,), jnp.float32), 0.5, 1.5)
    merge_bias = scatter_about(key_list[3], (MERGE_IN,), 0.3, 1.5, ((0, 32),), jnp.float32)
    final_gain = jnp.clip(0.2 + 1.8 * jax.random.uniform(key_list[4], (D,), jnp.float32) ** levels(key_list[4], (D,), ((0, 32),), -0.2, 0.2), 0.2, 2.0)
    final_bias = scatter_about(key_list[5], (D,), 0.7, 3.0, ((0, 32),), jnp.float32)
    w_qkv = scatter_about(key_list[6], (LAYERS, D, 3, D), D ** -0.5, 0.1875, ((0, 4), (1, 2), (3, 4)), jnp.float32)
    w_proj = scatter_about(key_list[7], (LAYERS, D, D), (D // 16) ** -0.5, 0.75, ((0, 4), (1, 4), (2, 2)), jnp.float32)
    w_fc1 = scatter_about(key_list[8], (LAYERS, D, FF), D ** -0.5, 0.1875, ((0, 4), (1, 2), (2, 4)), jnp.float32)
    w_fc2 = scatter_about(key_list[9], (LAYERS, FF, D), (FF // 4) ** -0.5, 0.1875, ((0, 4), (1, 4), (2, 2)), jnp.float32)
    qv_bias = scatter_about(key_list[10], (LAYERS, 2, D), 0.3, 1.5, ((0, 4), (2, 4)), jnp.float32)
    fc1_bias = scatter_about(key_list[11], (LAYERS, FF), 0.3, 1.5, ((0, 4),), jnp.float32)
    rel_table = scatter_about(key_list[12], (LAYERS, TABLE_ROWS, HEADS), 1.0, 5.0, ((0, 4), (2, 4)), jnp.float32)
    ln_gain = jnp.clip(1.0 + 0.1 * jax.random.normal(key_list[13], (LAYERS, 2, D), jnp.float32), 0.5, 1.5)
    ln_bias = scatter_about(key_list[14], (LAYERS, 2, D), 0.3, 1.5, ((0, 4),), jnp.float32)
    out_bias = scatter_about(key_list[15], (LAYERS, 2, D), 0.3, 1.5, ((0, 4),), jnp.float32)
    cotangent = scatter_about(key_list[16], (LAYERS, MICRO, PAGES_MB, TOKENS_PAGE, D), 1.0, 6.0, ((0, 4), (2, 2), (3, 4)))
    return {"raw_pages": raw_pages, "w_merge": w_merge, "merge_gain": merge_gain, "merge_bias": merge_bias, "final_gain": final_gain, "final_bias": final_bias, "w_qkv": w_qkv, "w_proj": w_proj, "w_fc1": w_fc1, "w_fc2": w_fc2, "qv_bias": qv_bias, "fc1_bias": fc1_bias, "rel_table": rel_table, "ln_gain": ln_gain, "ln_bias": ln_bias, "out_bias": out_bias, "cotangent": cotangent}


HIGHEST = lax.Precision.HIGHEST
NORM_EPS = 1e-05

@jax.custom_vjp
def low(v):
    return lax.optimization_barrier(v.astype(jnp.bfloat16)).astype(jnp.float32)

@jax.custom_vjp
def low_back(v):
    return v

def low_keep(v):
    return (low(v), None)

def low_pass(kept, grad):
    return (grad,)

def back_keep(v):
    return (v, None)

def back_low(kept, grad):
    return (low(grad),)
low.defvjp(low_keep, low_pass)
low_back.defvjp(back_keep, back_low)

def rel_index(window):
    coords = np.stack(np.meshgrid(np.arange(window), np.arange(window), indexing='ij')).reshape(2, -1)
    offsets = coords[:, :, None] - coords[:, None, :]
    return ((offsets[0] + window - 1) * (2 * window - 1) + offsets[1] + window - 1).reshape(-1)

def shift_mask(grid_rows, grid_cols, window, shift_now):
    region = np.zeros((grid_rows, grid_cols), np.int64)
    region_id = 0
    for span_rows in ((0, grid_rows - window), (grid_rows - window, grid_rows - shift_now), (grid_rows - shift_now, grid_rows)):
        for span_cols in ((0, grid_cols - window), (grid_cols - window, grid_cols - shift_now), (grid_cols - shift_now, grid_cols)):
            region[span_rows[0]:span_rows[1], span_cols[0]:span_cols[1]] = region_id
            region_id += 1
    blocks = region.reshape(grid_rows // window, window, grid_cols // window, window).transpose(0, 2, 1, 3)
    blocks = blocks.reshape(-1, window * window)
    return np.where(blocks[:, :, None] == blocks[:, None, :], 0.0, -100.0).astype(np.float32)

def norm_plain(values):
    row_mean = lax.optimization_barrier(jnp.mean(values, -1, keepdims=True))
    centred = values - row_mean
    variance = lax.optimization_barrier(jnp.mean(centred * centred, -1, keepdims=True))
    return centred * lax.rsqrt(variance + NORM_EPS)

def roll_rows(flat_rows, amount):
    grid_view = flat_rows.reshape(GRID_H, GRID_W, flat_rows.shape[-1])
    return jnp.roll(grid_view, (amount, amount), (0, 1)).reshape(flat_rows.shape)

def split_heads(flat_rows):
    channels = flat_rows.shape[-1]
    grid_view = flat_rows.reshape(WIN_ROWS, WIN, WIN_COLS, WIN, channels).transpose(0, 2, 1, 3, 4)
    return grid_view.reshape(WIN_ROWS * WIN_COLS, WIN * WIN, channels // HEAD, HEAD)

def join_heads(blocks):
    channels = blocks.shape[2] * blocks.shape[3]
    grid_view = blocks.reshape(WIN_ROWS, WIN_COLS, WIN, WIN, channels).transpose(0, 2, 1, 3, 4)
    return grid_view.reshape(GRID_H * GRID_W, channels)

def block_pass(stream, weights, layer_idx):
    w_qkv, w_proj, w_fc1, w_fc2, qv_bias, fc1_bias, rel_table, ln_gain, ln_bias, out_bias = weights
    shift_now = SHIFT * (layer_idx % 2)
    ready_attn = low(norm_plain(stream) * ln_gain[layer_idx, 0] + ln_bias[layer_idx, 0])
    moved = roll_rows(ready_attn, -shift_now)
    qkv_weight = low(w_qkv[layer_idx])
    query_vec = low_back(low(jnp.dot(moved, qkv_weight[:, 0], precision=HIGHEST) + qv_bias[layer_idx, 0]))
    key_vec = low_back(low(jnp.dot(moved, qkv_weight[:, 1], precision=HIGHEST)))
    value_vec = low_back(low(jnp.dot(moved, qkv_weight[:, 2], precision=HIGHEST) + qv_bias[layer_idx, 1]))
    pos_bias = jnp.take(rel_table[layer_idx], rel_index(WIN), axis=0)
    pos_bias = pos_bias.reshape(WIN * WIN, WIN * WIN, HEADS).transpose(2, 0, 1)
    scores = jnp.einsum('nqhd,nkhd->nhqk', split_heads(query_vec), split_heads(key_vec), precision=HIGHEST)
    scores = scores * HEAD ** (-0.5) + pos_bias[None]
    if shift_now:
        scores = scores + jnp.asarray(shift_mask(GRID_H, GRID_W, WIN, SHIFT))[:, None]
    scores = low_back(scores)
    weights_soft = low(jax.nn.softmax(scores, axis=-1))
    attended = jnp.einsum('nhqk,nkhd->nqhd', weights_soft, split_heads(value_vec), precision=HIGHEST)
    attended = low_back(low(attended))
    mixed_flat = roll_rows(join_heads(attended), shift_now)
    branch_attn = low_back(jnp.dot(mixed_flat, low(w_proj[layer_idx]), precision=HIGHEST))
    after_attn = stream + branch_attn + out_bias[layer_idx, 0]
    ready_mlp = low(norm_plain(after_attn) * ln_gain[layer_idx, 1] + ln_bias[layer_idx, 1])
    hidden_pre = low_back(jnp.dot(ready_mlp, low(w_fc1[layer_idx]), precision=HIGHEST) + fc1_bias[layer_idx])
    hidden_act = low(jax.nn.gelu(hidden_pre, approximate=False))
    branch_mlp = low_back(jnp.dot(hidden_act, low(w_fc2[layer_idx]), precision=HIGHEST))
    return after_attn + branch_mlp + out_bias[layer_idx, 1]

def page_forward(one_page, merge_set, block_set):
    w_merge, merge_gain, merge_bias, final_gain, final_bias = merge_set
    merged_in = low(norm_plain(one_page) * low(merge_gain) + low(merge_bias))
    stream = low_back(low(jnp.dot(merged_in, low(w_merge), precision=HIGHEST)))
    section_outs = []
    for layer_idx in range(N_PIPE):
        after_mlp = block_pass(stream, block_set, layer_idx)
        if layer_idx + 1 < N_PIPE:
            section_outs.append(after_mlp)
            stream = low_back(low(after_mlp))
        else:
            section_outs.append(norm_plain(after_mlp) * low(final_gain) + low(final_bias))
    return jnp.stack(section_outs)

def reference(raw_pages, w_merge, merge_gain, merge_bias, final_gain, final_bias, w_qkv, w_proj, w_fc1, w_fc2, qv_bias, fc1_bias, rel_table, ln_gain, ln_bias, out_bias, cotangent):
    page_rows = raw_pages.astype(jnp.float32).reshape(MICRO * PAGES_MB, TOKENS_PAGE, MERGE_IN)
    cot_pages = cotangent.astype(jnp.float32).transpose(1, 2, 0, 3, 4).reshape(MICRO * PAGES_MB, N_PIPE, TOKENS_PAGE, D)
    merge_set = (w_merge, merge_gain, merge_bias, final_gain, final_bias)
    block_set = (w_qkv, w_proj, w_fc1, w_fc2, qv_bias, fc1_bias, rel_table, ln_gain, ln_bias, out_bias)

    def all_pages(pages_in, merge_part, block_part):

        def page_pass(one_page):
            return page_forward(one_page, merge_part, block_part)
        return lax.map(jax.checkpoint(page_pass), pages_in)
    hidden, pull_back = jax.vjp(all_pages, page_rows, merge_set, block_set)
    grad_pages, merge_grads, block_grads = pull_back(cot_pages)
    hidden_out = hidden.reshape(MICRO, PAGES_MB, N_PIPE, TOKENS_PAGE, D).transpose(2, 0, 1, 3, 4).astype(jnp.bfloat16)
    grad_raw = grad_pages.reshape(raw_pages.shape).astype(jnp.bfloat16)
    g_merge, g_mgain, g_mbias, g_fgain, g_fbias = merge_grads
    g_qkv, g_proj, g_fc1, g_fc2, g_qv, g_fc1b, g_table, g_lng, g_lnb, g_outb = block_grads
    return (hidden_out, grad_raw, g_merge, g_mgain, g_mbias, g_fgain, g_fbias, g_qkv, g_proj, g_fc1, g_fc2, g_qv, g_fc1b, g_table, g_lng, g_lnb, g_outb)
```

```python
import functools

import jax
import jax.numpy as jnp
import numpy as np
from jax import lax
from jax.experimental import pallas as pl
from jax.experimental.pallas import tpu as pltpu
from jax.sharding import PartitionSpec as P

D = 1024
HEAD = 32
FF = 4096
WIN = 10
SHIFT = 5
WIN_ROWS = 4
WIN_COLS = 3
NORM_EPS = 1e-05

GRID_W = WIN * WIN_COLS
UNIT = WIN * GRID_W
LINES = SHIFT * GRID_W
HALF = 160
PAD = 112
KEYS = 128
ROWS = WIN_COLS * PAD
PER = 128 // HEAD
GROUPS = D // 128
STACK = PER * PAD
OWN = 2
BLOCKS = 4
DB = D // OWN
TB = D // BLOCKS
FB = FF // BLOCKS
STEP = 16
SUMS = 16
VMEM_BYTES = 60 * 1024 * 1024

F32 = jnp.float32
BF16 = jnp.bfloat16


def rel_parts(window):
    offsets = np.arange(window)[:, None] - np.arange(window)[None, :] + window - 1
    return (offsets.reshape(-1)[None, :] == np.arange(2 * window - 1)[:, None]).astype(np.float32)


def shift_mask(grid_rows, grid_cols, window, shift_now):
    region = np.zeros((grid_rows, grid_cols), np.int64)
    region_id = 0
    for span_rows in (
        (0, grid_rows - window),
        (grid_rows - window, grid_rows - shift_now),
        (grid_rows - shift_now, grid_rows),
    ):
        for span_cols in (
            (0, grid_cols - window),
            (grid_cols - window, grid_cols - shift_now),
            (grid_cols - shift_now, grid_cols),
        ):
            region[span_rows[0] : span_rows[1], span_cols[0] : span_cols[1]] = region_id
            region_id += 1
    blocks = region.reshape(grid_rows // window, window, grid_cols // window, window).transpose(
        0, 2, 1, 3
    )
    blocks = blocks.reshape(-1, window * window)
    return np.where(blocks[:, :, None] == blocks[:, None, :], 0.0, -100.0).astype(np.float32)


def window_order(shift_now):
    order = np.zeros((ROWS, 2 * HALF), np.float32)
    for win in range(WIN_COLS):
        for row in range(WIN):
            for col in range(WIN):
                source_col = (win * WIN + col + shift_now) % GRID_W
                source = (row // SHIFT) * HALF + (row % SHIFT) * GRID_W + source_col
                order[win * PAD + row * WIN + col, source] = 1.0
    return order


def norm_stats(values):
    row_mean = jnp.mean(values, -1, keepdims=True)
    centred = values - row_mean
    rstd_rows = lax.rsqrt(jnp.mean(centred * centred, -1, keepdims=True) + NORM_EPS)
    return (centred * rstd_rows, rstd_rows)


def norm_back(normed, rstd_rows, grad_normed):
    return rstd_rows * (
        grad_normed
        - jnp.mean(grad_normed, -1, keepdims=True)
        - normed * jnp.mean(grad_normed * normed, -1, keepdims=True)
    )


def dot_nn(left, right):
    return lax.dot_general(left, right, (((1,), (0,)), ((), ())), preferred_element_type=F32)


def dot_nt(left, right):
    return lax.dot_general(left, right, (((1,), (1,)), ((), ())), preferred_element_type=F32)


def dot_tn(left, right):
    return lax.dot_general(left, right, (((0,), (0,)), ((), ())), preferred_element_type=F32)


def row_chunks(body, carry=None):
    def step(index, state):
        return body(pl.ds(pl.multiple_of(index * STEP, STEP), STEP), state)

    return lax.fori_loop(0, ROWS // STEP, step, carry)


def fold8(values):
    return jnp.sum(values.reshape(values.shape[0] // 8, 8, values.shape[1]), 0)


def head_masks():
    lane_head = lax.broadcasted_iota(jnp.int32, (1, 128), 1) // HEAD
    return [(lane_head == head).astype(F32) for head in range(PER)]


def spread_heads(tile, masks):
    return jnp.concatenate([(tile * mask.astype(BF16)) for mask in masks], 0)


def pick_heads(stacked, masks):
    total = stacked[:PAD] * masks[0]
    for head in range(1, PER):
        total = total + stacked[head * PAD : (head + 1) * PAD] * masks[head]
    return total


def group_columns(group):
    return (group // 2) * (3 * TB) + (group % 2) * 128


def lanes(start, size):
    return pl.ds(pl.multiple_of(start, 128), size)


def forward_kernel(
    flags,
    recv_a,
    recv_b,
    firsts,
    perm_in,
    perm_out,
    mask,
    vecs,
    bias_qkv,
    bias_fc1,
    bias_pos,
    w_qkv,
    w_proj,
    w_fc1,
    w_fc2,
    *refs,
):
    (x_all, qkv_all, probs_all, mixed_all, mid_all, rattn_all, rmlp_all, act_all, slope_all) = refs[11:20]
    out_all, hid_all = refs[20:22]
    send = refs[22]
    (
        v_qkv,
        v_proj,
        v_fc1,
        v_fc2,
        v_pos,
        rin,
        xf,
        xb,
        rattn,
        qkv,
        probs,
        mixed,
        mid,
        rmlp,
        act,
        slope,
        total,
        final,
        outb,
        outs,
        sem_w,
        sem_in,
        sem_out,
    ) = refs[23:]
    valid = flags[0]
    slot = flags[1]
    is_first = flags[2]
    is_last = flags[3]

    @pl.when(valid == 1)
    def _():
        def w_copy(kind, block):
            source, target = ((w_qkv, v_qkv), (w_fc1, v_fc1), (w_fc2, v_fc2))[kind]
            return pltpu.make_async_copy(
                source.at[:, block], target.at[:, block], sem_w.at[kind * BLOCKS + block]
            )

        def proj_copy():
            return pltpu.make_async_copy(w_proj, v_proj, sem_w.at[3 * BLOCKS])

        def pos_copy():
            return pltpu.make_async_copy(bias_pos, v_pos, sem_w.at[3 * BLOCKS + 1])

        @pl.when(is_first == 1)
        def _():
            pltpu.make_async_copy(
                firsts.at[slot, 0], rin.at[pl.ds(0, HALF)], sem_in.at[0]
            ).start()
            pltpu.make_async_copy(
                firsts.at[slot, 1], rin.at[pl.ds(HALF, HALF)], sem_in.at[1]
            ).start()

        @pl.when(is_first == 0)
        def _():
            pltpu.make_async_copy(recv_a, rin.at[pl.ds(0, HALF)], sem_in.at[0]).start()
            pltpu.make_async_copy(recv_b, rin.at[pl.ds(HALF, HALF)], sem_in.at[1]).start()

        for block in range(BLOCKS):
            w_copy(0, block).start()
        pos_copy().start()
        proj_copy().start()
        for block in range(BLOCKS):
            w_copy(1, block).start()
        for block in range(BLOCKS):
            w_copy(2, block).start()
        pltpu.make_async_copy(recv_a, rin.at[pl.ds(0, HALF)], sem_in.at[0]).wait()
        pltpu.make_async_copy(recv_b, rin.at[pl.ds(HALF, HALF)], sem_in.at[1]).wait()

        xf[...] = dot_nn(perm_in[...], rin[...])

        def first_norm(rows, state):
            values = xf[rows, :]
            hat, _ = norm_stats(values)
            rattn[rows, :] = (hat * vecs[0:1, :] + vecs[2:3, :]).astype(BF16)
            xb[rows, :] = values.astype(BF16)
            return state

        row_chunks(first_norm)
        saves = [
            pltpu.make_async_copy(rattn, rattn_all.at[slot], sem_out.at[0]),
            pltpu.make_async_copy(xb, x_all.at[slot], sem_out.at[1]),
        ]
        saves[0].start()
        saves[1].start()
        qkv[pl.ds(ROWS, 16), :] = jnp.zeros((16, 3 * D), BF16)

        def qkv_block(block, state):
            w_copy(0, block).wait()
            out = dot_nn(rattn[:, :DB], v_qkv[0, block])
            out = out + dot_nn(rattn[:, DB:], v_qkv[1, block])
            columns = lanes(block * 3 * TB, 3 * TB)
            qkv[pl.ds(0, ROWS), columns] = (out + bias_qkv[:, columns]).astype(BF16)
            return state

        lax.fori_loop(0, BLOCKS, qkv_block, None)
        save_qkv = pltpu.make_async_copy(
            qkv.at[pl.ds(0, ROWS)], qkv_all.at[slot], sem_out.at[2]
        )
        save_qkv.start()
        pos_copy().wait()
        masks = head_masks()

        def attend(win, group):
            base = pl.multiple_of(win * PAD, 16)
            column = group_columns(group)
            query = qkv[pl.ds(base, PAD), lanes(column, 128)]
            key = qkv[pl.ds(base, KEYS), lanes(column + TB, 128)]
            value = qkv[pl.ds(base, KEYS), lanes(column + 2 * TB, 128)]
            scores = dot_nt(spread_heads(query, masks), key)
            scores = scores * HEAD**-0.5 + v_pos[group]
            scores = scores + jnp.concatenate([mask[win]] * PER, 0)
            top = jnp.max(scores, -1, keepdims=True)
            powers = jnp.exp(scores - top)
            low = (powers / jnp.sum(powers, -1, keepdims=True)).astype(BF16)
            probs[win * GROUPS + group] = low
            mixed[pl.ds(base, PAD), lanes(group * 128, 128)] = pick_heads(
                dot_nn(low, value), masks
            ).astype(BF16)

        def attend_pair(index, state):
            win = index // (GROUPS // 2)
            pair = index % (GROUPS // 2)
            attend(win, pair * 2)
            attend(win, pair * 2 + 1)
            return state

        lax.fori_loop(0, WIN_COLS * GROUPS // 2, attend_pair, None)
        saves.append(pltpu.make_async_copy(probs, probs_all.at[slot], sem_out.at[3]))
        saves[-1].start()
        saves.append(pltpu.make_async_copy(mixed, mixed_all.at[slot], sem_out.at[4]))
        saves[-1].start()
        proj_copy().wait()
        for own in range(OWN):
            columns = slice(own * DB, (own + 1) * DB)
            out = xf[:, columns] + vecs[4:5, columns]
            for block in range(BLOCKS):
                out = out + dot_nn(mixed[:, block * TB : (block + 1) * TB], v_proj[own, block])
            mid[:, columns] = out
        saves.append(pltpu.make_async_copy(mid, mid_all.at[slot], sem_out.at[5]))
        saves[-1].start()

        def second_norm(rows, state):
            hat, _ = norm_stats(mid[rows, :])
            rmlp[rows, :] = (hat * vecs[1:2, :] + vecs[3:4, :]).astype(BF16)
            total[rows, :] = mid[rows, :] + vecs[5:6, :]
            return state

        row_chunks(second_norm)
        saves.append(pltpu.make_async_copy(rmlp, rmlp_all.at[slot], sem_out.at[6]))
        saves[-1].start()

        def hidden_block(block, state):
            w_copy(1, block).wait()
            columns = lanes(block * FB, FB)
            pre = dot_nn(rmlp[:, :DB], v_fc1[0, block]) + dot_nn(rmlp[:, DB:], v_fc1[1, block])
            pre = pre + bias_fc1[:, columns]
            chance = 0.5 + 0.5 * lax.erf(pre * np.float32(0.5**0.5))
            slope[:, columns] = (
                chance + pre * (np.float32((2 * np.pi) ** -0.5) * jnp.exp(-0.5 * pre * pre))
            ).astype(BF16)
            act[:, columns] = (pre * chance).astype(BF16)
            w_copy(2, block).wait()
            for own in range(OWN):
                half = slice(own * DB, (own + 1) * DB)
                total[:, half] += dot_nn(act[:, columns], v_fc2[own, block])
            return state

        lax.fori_loop(0, BLOCKS, hidden_block, None)
        saves.append(pltpu.make_async_copy(act, act_all.at[slot], sem_out.at[7]))
        saves[-1].start()
        saves.append(pltpu.make_async_copy(slope, slope_all.at[slot], sem_out.at[8]))
        saves[-1].start()

        def finish(rows, state):
            values = total[rows, :]
            hat, _ = norm_stats(values)
            shown = jnp.where(is_last == 1, hat * vecs[6:7, :] + vecs[7:8, :], values)
            outb[rows, :] = shown.astype(BF16)
            return state

        row_chunks(finish)
        saves.append(pltpu.make_async_copy(total, out_all.at[slot], sem_out.at[9]))
        saves[-1].start()
        outs[...] = dot_nn(perm_out[...], outb[...]).astype(BF16)
        for half in range(2):
            rows = pl.ds(half * HALF, HALF)
            saves.append(
                pltpu.make_async_copy(outs.at[rows], send.at[half], sem_out.at[10 + half])
            )
            saves[-1].start()
            saves.append(
                pltpu.make_async_copy(outs.at[rows], hid_all.at[slot, half], sem_out.at[12 + half])
            )
            saves[-1].start()
        save_qkv.wait()
        for save in saves:
            save.wait()


def backward_kernel(
    flags,
    recv_a,
    recv_b,
    cots,
    perm_in,
    perm_out,
    vecs,
    w_qkv,
    w_proj,
    w_fc1,
    w_fc2,
    probs_all,
    mid_all,
    out_all,
    *refs,
):
    x_all, qkv_all, slope_all, dbm_all, dx_all, sums_all, dpos_all = refs[7:14]
    send = refs[14]
    (
        v_qkv,
        v_proj,
        v_fc1,
        v_fc2,
        rin,
        rcot,
        xb,
        qkv,
        probs,
        mid,
        last,
        slope,
        grad,
        back,
        dbm,
        dba,
        dmix,
        dqkv,
        dpos,
        sums,
        outs,
        sem_w,
        sem_in,
        sem_out,
    ) = refs[15:]
    valid = flags[0]
    slot = flags[1]
    is_last = flags[3]

    @pl.when(valid == 1)
    def _():
        def w_copy(kind, block):
            source, target = ((w_fc2, v_fc2), (w_fc1, v_fc1), (w_qkv, v_qkv))[kind]
            return pltpu.make_async_copy(
                source.at[:, block], target.at[:, block], sem_w.at[kind * BLOCKS + block]
            )

        def proj_copy():
            return pltpu.make_async_copy(w_proj, v_proj, sem_w.at[3 * BLOCKS])

        def load(index):
            source, target = (
                (cots.at[slot, 0], rcot.at[pl.ds(0, HALF)]),
                (cots.at[slot, 1], rcot.at[pl.ds(HALF, HALF)]),
                (recv_a, rin.at[pl.ds(0, HALF)]),
                (recv_b, rin.at[pl.ds(HALF, HALF)]),
                (out_all.at[slot], last),
                (slope_all.at[slot], slope),
                (mid_all.at[slot], mid),
                (qkv_all.at[slot], qkv.at[pl.ds(0, ROWS)]),
                (probs_all.at[slot], probs),
                (x_all.at[slot], xb),
                (dpos_all, dpos),
            )[index]
            return pltpu.make_async_copy(source, target, sem_in.at[index])

        for index in range(5):
            load(index).start()
        w_copy(0, 0).start()
        load(5).start()
        w_copy(1, 0).start()
        for block in range(1, BLOCKS):
            w_copy(0, block).start()
            w_copy(1, block).start()
        load(6).start()
        proj_copy().start()
        load(7).start()
        load(8).start()
        for block in range(BLOCKS):
            w_copy(2, block).start()
        load(9).start()
        load(10).start()
        for index in range(5):
            load(index).wait()
        sums[...] = jnp.zeros_like(sums)
        grad[...] = dot_nn(perm_in[...], rcot[...])

        @pl.when(is_last == 1)
        def _():
            def final_norm(rows, state):
                cot = grad[rows, :]
                hat, rstd = norm_stats(last[rows, :])
                grad[rows, :] = norm_back(hat, rstd, cot * vecs[6:7, :])
                return (state[0] + fold8(cot * hat), state[1] + fold8(cot))

            zero = jnp.zeros((8, D), F32)
            gain, shift = row_chunks(final_norm, (zero, zero))
            sums[6:7, :] = jnp.sum(gain, 0, keepdims=True)
            sums[7:8, :] = jnp.sum(shift, 0, keepdims=True)

        @pl.when(is_last == 0)
        def _():
            grad[...] += dot_nn(perm_in[...], rin[...])

        def enter(rows, state):
            values = grad[rows, :]
            dbm[rows, :] = values.astype(BF16)
            back[rows, :] = jnp.zeros((STEP, D), F32)
            return state + fold8(values)

        out_sum = row_chunks(enter, jnp.zeros((8, D), F32))
        sums[5:6, :] = jnp.sum(out_sum, 0, keepdims=True)
        saves = [pltpu.make_async_copy(dbm, dbm_all.at[slot], sem_out.at[0])]
        saves[0].start()
        load(5).wait()

        def hidden_block(block, state):
            columns = lanes(block * FB, FB)
            w_copy(0, block).wait()
            dact = dot_nt(dbm[:, :DB], v_fc2[0, block]) + dot_nt(dbm[:, DB:], v_fc2[1, block])
            dpre = (dact * slope[:, columns].astype(F32)).astype(BF16)
            slope[:, columns] = dpre
            sums[pl.ds(8 + block, 1), :] = jnp.sum(dpre.astype(F32), 0, keepdims=True)
            w_copy(1, block).wait()
            for own in range(OWN):
                half = slice(own * DB, (own + 1) * DB)
                back[:, half] += dot_nt(slope[:, columns], v_fc1[own, block])
            return state

        lax.fori_loop(0, BLOCKS, hidden_block, None)
        saves.append(pltpu.make_async_copy(slope, slope_all.at[slot], sem_out.at[1]))
        saves[-1].start()
        load(6).wait()

        def mlp_norm(rows, state):
            hat, rstd = norm_stats(mid[rows, :])
            ready = back[rows, :]
            values = grad[rows, :] + norm_back(hat, rstd, ready * vecs[1:2, :])
            grad[rows, :] = values
            dba[rows, :] = values.astype(BF16)
            back[rows, :] = jnp.zeros((STEP, D), F32)
            return (state[0] + fold8(ready * hat), state[1] + fold8(ready), state[2] + fold8(values))

        zero = jnp.zeros((8, D), F32)
        gain, shift, out_sum = row_chunks(mlp_norm, (zero, zero, zero))
        sums[1:2, :] = jnp.sum(gain, 0, keepdims=True)
        sums[3:4, :] = jnp.sum(shift, 0, keepdims=True)
        sums[4:5, :] = jnp.sum(out_sum, 0, keepdims=True)
        load(9).wait()
        saves.append(pltpu.make_async_copy(dba, x_all.at[slot], sem_out.at[2]))
        saves[-1].start()
        proj_copy().wait()
        for block in range(BLOCKS):
            out = dot_nt(dba[:, :DB], v_proj[0, block]) + dot_nt(dba[:, DB:], v_proj[1, block])
            dmix[:, block * TB : (block + 1) * TB] = out.astype(BF16)
        load(7).wait()
        load(8).wait()
        load(10).wait()
        qkv[pl.ds(ROWS, 16), :] = jnp.zeros((16, 3 * D), BF16)
        masks = head_masks()

        def attend_back(group, state):
            column = group_columns(group)
            for win in range(WIN_COLS):
                base = win * PAD
                query = qkv[pl.ds(base, PAD), lanes(column, 128)]
                key = qkv[pl.ds(base, KEYS), lanes(column + TB, 128)]
                value = qkv[pl.ds(base, KEYS), lanes(column + 2 * TB, 128)]
                low = probs[win * GROUPS + group]
                dout = spread_heads(dmix[pl.ds(base, PAD), lanes(group * 128, 128)], masks)
                dprob = dot_nt(dout, value)
                weight = low.astype(F32)
                dscore = weight * (dprob - jnp.sum(dprob * weight, -1, keepdims=True))
                dscore = dscore.astype(BF16)
                dpos[group] += dscore.astype(F32)
                dquery = pick_heads(dot_nn(dscore, key), masks) * HEAD**-0.5
                dkey = dot_tn(dscore, spread_heads(query, masks)) * HEAD**-0.5
                dvalue = dot_tn(low, dout)
                dqkv[pl.ds(base, PAD), lanes(column, 128)] = dquery.astype(BF16)
                dqkv[pl.ds(base, PAD), lanes(column + TB, 128)] = dkey[:PAD].astype(BF16)
                dqkv[pl.ds(base, PAD), lanes(column + 2 * TB, 128)] = dvalue[:PAD].astype(BF16)
            return state

        lax.fori_loop(0, GROUPS, attend_back, None)
        saves.append(pltpu.make_async_copy(dqkv, qkv_all.at[slot], sem_out.at[3]))
        saves[-1].start()
        saves.append(pltpu.make_async_copy(dpos, dpos_all, sem_out.at[4]))
        saves[-1].start()

        def ready_block(block, state):
            columns = lanes(block * 3 * TB, 3 * TB)
            w_copy(2, block).wait()
            for own in range(OWN):
                half = slice(own * DB, (own + 1) * DB)
                back[:, half] += dot_nt(dqkv[:, columns], v_qkv[own, block])
            return state

        lax.fori_loop(0, BLOCKS, ready_block, None)
        for part in range(3):
            columns = slice(part * D, (part + 1) * D)
            sums[12 + part : 13 + part, :] = jnp.sum(dqkv[:, columns].astype(F32), 0, keepdims=True)

        def attn_norm(rows, state):
            hat, rstd = norm_stats(xb[rows, :].astype(F32))
            ready = back[rows, :]
            values = grad[rows, :] + norm_back(hat, rstd, ready * vecs[0:1, :])
            xb[rows, :] = values.astype(BF16)
            return (state[0] + fold8(ready * hat), state[1] + fold8(ready))

        gain, shift = row_chunks(attn_norm, (zero, zero))
        sums[0:1, :] = jnp.sum(gain, 0, keepdims=True)
        sums[2:3, :] = jnp.sum(shift, 0, keepdims=True)
        saves.append(pltpu.make_async_copy(sums, sums_all.at[slot], sem_out.at[5]))
        saves[-1].start()
        outs[...] = dot_nn(perm_out[...], xb[...]).astype(BF16)
        for half in range(2):
            rows = pl.ds(half * HALF, HALF)
            saves.append(
                pltpu.make_async_copy(outs.at[rows], send.at[half], sem_out.at[6 + half])
            )
            saves[-1].start()
            saves.append(
                pltpu.make_async_copy(outs.at[rows], dx_all.at[slot, half], sem_out.at[8 + half])
            )
            saves[-1].start()
        for save in saves:
            save.wait()


def any_specs(count):
    return [pl.BlockSpec(memory_space=pl.ANY)] * count


def vmem_specs(count):
    return [pl.BlockSpec(memory_space=pltpu.VMEM)] * count


def shapes_of(arrays):
    return [jax.ShapeDtypeStruct(array.shape, array.dtype) for array in arrays]


WEIGHT_SCRATCH = [
    pltpu.VMEM((OWN, BLOCKS, DB, 3 * TB), BF16),
    pltpu.VMEM((OWN, BLOCKS, TB, DB), BF16),
    pltpu.VMEM((OWN, BLOCKS, DB, FB), BF16),
    pltpu.VMEM((OWN, BLOCKS, FB, DB), BF16),
]


def layer_forward(flags, recv_a, recv_b, firsts, tables, weights, stacks):
    inputs = (flags, recv_a, recv_b, firsts) + tuple(tables) + tuple(weights) + tuple(stacks)
    first_stack = len(inputs) - len(stacks)
    wide = lambda dtype: pltpu.VMEM((ROWS, D), dtype)
    results = pl.pallas_call(
        forward_kernel,
        out_shape=shapes_of(stacks) + [jax.ShapeDtypeStruct((2, HALF, D), BF16)],
        in_specs=[pl.BlockSpec(memory_space=pltpu.SMEM)]
        + any_specs(3)
        + vmem_specs(6)
        + any_specs(5 + len(stacks)),
        out_specs=any_specs(len(stacks) + 1),
        scratch_shapes=WEIGHT_SCRATCH
        + [
            pltpu.VMEM((GROUPS, STACK, KEYS), F32),
            pltpu.VMEM((2 * HALF, D), BF16),
            wide(F32),
            wide(BF16),
            wide(BF16),
            pltpu.VMEM((ROWS + 16, 3 * D), BF16),
            pltpu.VMEM((WIN_COLS * GROUPS, STACK, KEYS), BF16),
            wide(BF16),
            wide(F32),
            wide(BF16),
            pltpu.VMEM((ROWS, FF), BF16),
            pltpu.VMEM((ROWS, FF), BF16),
            wide(F32),
            wide(F32),
            wide(BF16),
            pltpu.VMEM((2 * HALF, D), BF16),
            pltpu.SemaphoreType.DMA((3 * BLOCKS + 2,)),
            pltpu.SemaphoreType.DMA((2,)),
            pltpu.SemaphoreType.DMA((14,)),
        ],
        input_output_aliases={first_stack + index: index for index in range(len(stacks))},
        compiler_params=pltpu.CompilerParams(vmem_limit_bytes=VMEM_BYTES),
        cost_estimate=pl.CostEstimate(
            flops=24 * ROWS * D * D, bytes_accessed=40 * 1024 * 1024, transcendentals=ROWS * FF
        ),
        name="layer_forward",
    )(*inputs)
    return results[-1], tuple(results[:-1])


def layer_backward(flags, recv_a, recv_b, cots, tables, weights, saved, stacks):
    inputs = (
        (flags, recv_a, recv_b, cots) + tuple(tables) + tuple(weights) + tuple(saved) + tuple(stacks)
    )
    first_stack = len(inputs) - len(stacks)
    wide = lambda dtype: pltpu.VMEM((ROWS, D), dtype)
    results = pl.pallas_call(
        backward_kernel,
        out_shape=shapes_of(stacks) + [jax.ShapeDtypeStruct((2, HALF, D), BF16)],
        in_specs=[pl.BlockSpec(memory_space=pltpu.SMEM)]
        + any_specs(3)
        + vmem_specs(3)
        + any_specs(4 + len(saved) + len(stacks)),
        out_specs=any_specs(len(stacks) + 1),
        scratch_shapes=WEIGHT_SCRATCH
        + [
            pltpu.VMEM((2 * HALF, D), BF16),
            pltpu.VMEM((2 * HALF, D), BF16),
            wide(BF16),
            pltpu.VMEM((ROWS + 16, 3 * D), BF16),
            pltpu.VMEM((WIN_COLS * GROUPS, STACK, KEYS), BF16),
            wide(F32),
            wide(F32),
            pltpu.VMEM((ROWS, FF), BF16),
            wide(F32),
            wide(F32),
            wide(BF16),
            wide(BF16),
            wide(BF16),
            pltpu.VMEM((ROWS, 3 * D), BF16),
            pltpu.VMEM((GROUPS, STACK, KEYS), F32),
            pltpu.VMEM((SUMS, D), F32),
            pltpu.VMEM((2 * HALF, D), BF16),
            pltpu.SemaphoreType.DMA((3 * BLOCKS + 1,)),
            pltpu.SemaphoreType.DMA((11,)),
            pltpu.SemaphoreType.DMA((10,)),
        ],
        input_output_aliases={first_stack + index: index for index in range(len(stacks))},
        compiler_params=pltpu.CompilerParams(vmem_limit_bytes=VMEM_BYTES),
        cost_estimate=pl.CostEstimate(
            flops=24 * ROWS * D * D, bytes_accessed=50 * 1024 * 1024, transcendentals=0
        ),
        name="layer_backward",
    )(*inputs)
    return results[-1], tuple(results[:-1])


def on_device(
    raw_pages,
    w_merge,
    merge_gain,
    merge_bias,
    final_gain,
    final_bias,
    w_qkv,
    w_proj,
    w_fc1,
    w_fc2,
    qv_bias,
    fc1_bias,
    rel_table,
    ln_gain,
    ln_bias,
    out_bias,
    cotangent,
):
    section_now = lax.axis_index("pipe")
    section_count = lax.axis_size("pipe")
    dp_now = lax.axis_index("dp")
    dp_count = lax.axis_size("dp")
    tensor_now = lax.axis_index("tensor")
    tensor_count = lax.axis_size("tensor")
    copies = tensor_count // WIN_ROWS
    unit_now = tensor_now // copies
    all_axes = ("pipe", "dp", "tensor")
    group_axes = ("dp", "tensor")
    is_first = section_now == 0
    is_last = section_now == section_count - 1
    is_odd = section_now % 2 == 1
    owned, _, rows_here, merge_in = raw_pages.shape
    micro_count = cotangent.shape[1]
    own_width = D // dp_count

    def section_pairs(step, moves):
        pairs = []
        for section in range(section_count):
            if 0 <= section + step < section_count:
                for tensor in range(tensor_count):
                    target = (tensor + copies * moves[section % 2]) % tensor_count
                    pairs.append(
                        (section * tensor_count + tensor, (section + step) * tensor_count + target)
                    )
        return pairs

    def odd_pairs(move):
        return [
            (
                section * tensor_count + tensor,
                section * tensor_count + (tensor + copies * move) % tensor_count,
            )
            for section in range(1, section_count, 2)
            for tensor in range(tensor_count)
        ]

    def hop(halves, step):
        to_a = lax.ppermute(halves[1], ("pipe", "tensor"), section_pairs(step, (0, 1)))
        to_b = lax.ppermute(halves[0], ("pipe", "tensor"), section_pairs(step, (-1, 0)))
        return to_a, to_b

    def whole_unit(rows, axis):
        if copies == 1:
            return rows
        rows = lax.all_gather(rows, "tensor", axis=axis, tiled=True)
        return lax.dynamic_slice_in_dim(rows, unit_now * UNIT, UNIT, axis)

    def own_part(rows, axis):
        if copies == 1:
            return rows
        return lax.dynamic_slice_in_dim(
            rows, (tensor_now % copies) * rows_here, rows_here, axis
        )

    def gather_rows(values, axes):
        size = values.shape[0]
        tile = 8 * 128
        rows = jnp.pad(values, (0, -size % tile)).reshape(-1, 128)
        rows = lax.all_gather(rows, axes, axis=0, tiled=True)
        return rows.reshape(-1, size + -size % tile)[:, :size]

    def to_halves(rows):
        rows = rows.reshape(rows.shape[:-2] + (2, LINES, D))
        pads = [(0, 0)] * (rows.ndim - 2) + [(0, HALF - LINES), (0, 0)]
        return jnp.pad(rows, pads)

    def from_halves(halves):
        rows = halves[..., :LINES, :]
        return rows.reshape(rows.shape[:-3] + (UNIT, D))

    share = w_merge.shape[0]
    small = jnp.concatenate((merge_gain, merge_bias, final_gain, final_bias)).astype(BF16)
    merge_weight = lax.all_gather(w_merge.astype(BF16), all_axes, axis=0, tiled=True)
    small_all = lax.all_gather(small, all_axes, axis=0)
    fshare = final_gain.shape[0]
    merge_scale = small_all[:, :share].reshape(-1).astype(F32)
    merge_shift = small_all[:, share : 2 * share].reshape(-1).astype(F32)
    final_scale = small_all[:, 2 * share : 2 * share + fshare].reshape(-1).astype(F32)
    final_shift = small_all[:, 2 * share + fshare :].reshape(-1).astype(F32)

    def gather(weight):
        return lax.all_gather(weight.astype(BF16), group_axes, axis=0)

    split = (dp_count, tensor_count)
    qkv_weight = gather(w_qkv[0].reshape(own_width, -1))
    proj_weight = gather(w_proj[0])
    fc1_weight = gather(w_fc1[0])
    fc2_weight = gather(w_fc2[0])
    if split == (OWN, BLOCKS):
        qkv_weight = qkv_weight.reshape(OWN, BLOCKS, DB, 3 * TB)
        proj_weight = proj_weight.reshape(OWN, BLOCKS, TB, DB)
        fc1_weight = fc1_weight.reshape(OWN, BLOCKS, DB, FB)
        fc2_weight = fc2_weight.reshape(OWN, BLOCKS, FB, DB)
    else:
        qkv_weight = qkv_weight.reshape(split + (own_width, 3, -1)).transpose(0, 2, 3, 1, 4)
        qkv_weight = qkv_weight.reshape(OWN, DB, 3, BLOCKS, TB).transpose(0, 3, 1, 2, 4)
        qkv_weight = qkv_weight.reshape(OWN, BLOCKS, DB, 3 * TB)
        proj_weight = proj_weight.reshape(split + (-1, own_width)).transpose(1, 2, 0, 3)
        proj_weight = proj_weight.reshape(BLOCKS, TB, OWN, DB).transpose(2, 0, 1, 3)
        fc1_weight = fc1_weight.reshape(split + (own_width, -1)).transpose(0, 2, 1, 3)
        fc1_weight = fc1_weight.reshape(OWN, DB, BLOCKS, FB).transpose(0, 2, 1, 3)
        fc2_weight = fc2_weight.reshape(split + (-1, own_width)).transpose(1, 2, 0, 3)
        fc2_weight = fc2_weight.reshape(BLOCKS, FB, OWN, DB).transpose(2, 0, 1, 3)
    weights = (qkv_weight, proj_weight, fc1_weight, fc2_weight)

    heads_here = rel_table.shape[2]
    head_set = jnp.concatenate((qv_bias[0].reshape(-1), rel_table[0].reshape(-1)))
    head_set = gather_rows(head_set, "tensor")
    qv_all = head_set[:, : qv_bias.shape[1] * qv_bias.shape[2]].reshape(tensor_count, 2, -1)
    qv_all = qv_all.transpose(1, 0, 2).reshape(2, BLOCKS, TB)
    bias_qkv = jnp.stack((qv_all[0], jnp.zeros_like(qv_all[0]), qv_all[1]), 1).reshape(1, 3 * D)
    table_all = head_set[:, qv_bias.shape[1] * qv_bias.shape[2] :]
    table_all = table_all.reshape(tensor_count, 2 * WIN - 1, 2 * WIN - 1, heads_here)
    table_all = table_all.transpose(0, 3, 1, 2).reshape(D // HEAD, 2 * WIN - 1, 2 * WIN - 1)
    offsets = jnp.asarray(rel_parts(WIN))
    spread = jnp.einsum("huv,vy->huy", table_all, offsets, precision=lax.Precision.HIGHEST)
    spread = jnp.einsum("huy,ux->hxy", spread, offsets, precision=lax.Precision.HIGHEST)
    spread = spread.reshape(D // HEAD, WIN, WIN, WIN, WIN).transpose(0, 1, 3, 2, 4)
    spread = spread.reshape(D // HEAD, WIN * WIN, WIN * WIN)
    bias_pos = jnp.pad(spread, ((0, 0), (0, PAD - WIN * WIN), (0, 0)))
    bias_pos = jnp.pad(
        bias_pos, ((0, 0), (0, 0), (0, KEYS - WIN * WIN)), constant_values=-1e30
    ).reshape(GROUPS, STACK, KEYS)

    mask_all = np.zeros((WIN_ROWS, WIN_COLS, PAD, KEYS), np.float32)
    mask_all[:, :, : WIN * WIN, : WIN * WIN] = shift_mask(
        WIN * WIN_ROWS, GRID_W, WIN, SHIFT
    ).reshape(WIN_ROWS, WIN_COLS, WIN * WIN, WIN * WIN)
    mask_here = lax.dynamic_index_in_dim(jnp.asarray(mask_all, BF16), unit_now, 0, keepdims=False)
    mask_here = mask_here.astype(F32) * is_odd.astype(F32)
    orders = np.stack((window_order(0), window_order(SHIFT)))
    parity = section_now % 2
    perm_in = lax.dynamic_index_in_dim(jnp.asarray(orders, BF16), parity, 0, keepdims=False)
    perm_out = lax.dynamic_index_in_dim(
        jnp.asarray(orders.transpose(0, 2, 1), BF16), parity, 0, keepdims=False
    )
    vecs = jnp.concatenate(
        (ln_gain[0], ln_bias[0], out_bias[0], final_scale[None], final_shift[None])
    )
    forward_tables = (perm_in, perm_out, mask_here, vecs, bias_qkv, fc1_bias, bias_pos)
    backward_tables = (perm_in, perm_out, vecs)

    raw_rows = raw_pages.reshape(owned * rows_here, merge_in).astype(F32)
    raw_hat, raw_rstd = norm_stats(raw_rows)
    merged_in = (raw_hat * merge_scale + merge_shift).astype(BF16)
    merged = dot_nn(merged_in, merge_weight).astype(BF16).reshape(owned, rows_here, D)
    merged = to_halves(whole_unit(merged, 1))
    first_list = [merged]
    for section in range(1, section_count):
        first_list.append(lax.ppermute(merged, "pipe", [(section, 0)]))
    firsts = jnp.concatenate(first_list, 0)

    cots = to_halves(whole_unit(cotangent[0, :, 0], 1))
    cots_next = lax.ppermute(cots[:, 0], ("pipe", "tensor"), odd_pairs(-1))
    cots = jnp.where(is_odd, jnp.stack((cots[:, 1], cots_next), 1), cots)

    tick_count = micro_count + 2 * (section_count - 1)

    def flags_at(start, tick_now):
        slot_now = tick_now - 2 * start
        is_valid = (slot_now >= 0) & (slot_now < micro_count)
        slot = jnp.clip(slot_now, 0, micro_count - 1)
        return jnp.stack([flag.astype(jnp.int32) for flag in (is_valid, slot, is_first, is_last)])

    def stack_of(shape, dtype):
        return jnp.zeros((micro_count,) + shape, dtype)

    def forward_tick(tick_now, state):
        outgoing, recv_a, recv_b, stacks = state
        next_a, next_b = hop(outgoing, 1)
        outgoing, stacks = layer_forward(
            flags_at(section_now, tick_now), recv_a, recv_b, firsts, forward_tables, weights, stacks
        )
        return outgoing, next_a, next_b, stacks

    empty = jnp.zeros((2, HALF, D), BF16)
    stacks = (
        stack_of((ROWS, D), BF16),
        stack_of((ROWS, 3 * D), BF16),
        stack_of((WIN_COLS * GROUPS, STACK, KEYS), BF16),
        stack_of((ROWS, D), BF16),
        stack_of((ROWS, D), F32),
        stack_of((ROWS, D), BF16),
        stack_of((ROWS, D), BF16),
        stack_of((ROWS, FF), BF16),
        stack_of((ROWS, FF), BF16),
        stack_of((ROWS, D), F32),
        stack_of((2, HALF, D), BF16),
    )
    state = lax.fori_loop(0, tick_count, forward_tick, (empty, empty[0], empty[1], stacks))
    (
        x_all,
        qkv_all,
        probs_all,
        mixed_all,
        mid_all,
        rattn_all,
        rmlp_all,
        act_all,
        slope_all,
        out_all,
        hid_all,
    ) = state[3]
    hid_before = lax.ppermute(hid_all[:, 1], ("pipe", "tensor"), odd_pairs(1))
    shown = jnp.where(is_odd, jnp.stack((hid_before, hid_all[:, 0]), 1), hid_all)
    shown = own_part(from_halves(shown), 1)

    def backward_tick(tick_now, state):
        outgoing, recv_a, recv_b, stacks = state
        next_a, next_b = hop(outgoing, -1)
        outgoing, stacks = layer_backward(
            flags_at(section_count - 1 - section_now, tick_now),
            recv_a,
            recv_b,
            cots,
            backward_tables,
            weights,
            (probs_all, mid_all, out_all),
            stacks,
        )
        return outgoing, next_a, next_b, stacks

    stacks = (
        x_all,
        qkv_all,
        slope_all,
        stack_of((ROWS, D), BF16),
        stack_of((2, HALF, D), BF16),
        stack_of((SUMS, D), F32),
        jnp.zeros((GROUPS, STACK, KEYS), F32),
    )
    state = lax.fori_loop(0, tick_count, backward_tick, (empty, empty[0], empty[1], stacks))
    dba_all, dqkv_all, dpre_all, dbm_all, dx_all, sums_all, dpos = state[3]

    def weight_gradient(left, right):
        left = left.reshape(micro_count * ROWS, -1)
        right = right.reshape(micro_count * ROWS, D)

        def part(target):
            return dot_tn(
                left, lax.dynamic_slice_in_dim(right, target * own_width, own_width, 1)
            )

        total = None
        for step in range(1, dp_count):
            pairs = [(index, (index + step) % dp_count) for index in range(dp_count)]
            moved = lax.ppermute(
                part((dp_now + step) % dp_count).astype(BF16), "dp", pairs
            ).astype(F32)
            total = moved if total is None else total + moved
        mine = part(dp_now)
        total = mine if total is None else mine + total
        return total / copies

    def over_tensor(total):
        return lax.psum_scatter(total.astype(BF16), "tensor", scatter_dimension=0, tiled=True)

    g_fc2 = over_tensor(weight_gradient(act_all, dbm_all)).astype(F32)
    g_fc1 = over_tensor(weight_gradient(dpre_all, rmlp_all)).astype(F32).T
    g_qkv = weight_gradient(dqkv_all, rattn_all)
    if copies > 1:
        g_qkv = g_qkv.reshape(BLOCKS, 3, copies, TB // copies, own_width)
        g_qkv = g_qkv.transpose(0, 2, 1, 3, 4).reshape(3 * D, own_width)
    g_qkv = over_tensor(g_qkv).astype(F32).T.reshape(own_width, 3, D // tensor_count)
    g_proj = over_tensor(weight_gradient(mixed_all, dba_all)).astype(F32)

    sums = jnp.sum(sums_all, 0)
    dpos = dpos.reshape(D // HEAD, PAD, KEYS)[:, : WIN * WIN, : WIN * WIN]
    dpos = dpos.reshape(D // HEAD, WIN, WIN, WIN, WIN).transpose(0, 1, 3, 2, 4)
    dpos = dpos.reshape(D // HEAD, WIN * WIN, WIN * WIN)
    dtable = jnp.einsum("hxy,vy->hxv", dpos, offsets, precision=lax.Precision.HIGHEST)
    dtable = jnp.einsum("hxv,ux->huv", dtable, offsets, precision=lax.Precision.HIGHEST)
    local_sums = jnp.concatenate((sums[:15].reshape(-1), dtable.reshape(-1)))
    local_sums = jnp.sum(gather_rows(local_sums, group_axes), 0) / copies
    sums = local_sums[: 15 * D].reshape(15, D)
    dtable = local_sums[15 * D :].reshape(tensor_count, heads_here, -1)
    g_table = lax.dynamic_index_in_dim(dtable, tensor_now, 0, keepdims=False).T
    dqv = sums[12:15].reshape(BLOCKS, 3, TB)[:, 0::2].transpose(1, 0, 2).reshape(2, D)
    g_qv = lax.dynamic_slice_in_dim(
        dqv, tensor_now * (D // tensor_count), D // tensor_count, 1
    )

    own_grads = dx_all[:owned]
    for section in range(1, section_count):
        moved = lax.ppermute(
            dx_all[section * owned : (section + 1) * owned], "pipe", [(0, section)]
        )
        own_grads = jnp.where(section_now == section, moved, own_grads)
    grad_merged = own_part(from_halves(own_grads), 1).reshape(owned * rows_here, D)
    g_merge = dot_tn(merged_in, grad_merged).astype(BF16)
    grad_unit = dot_nt(grad_merged, merge_weight)
    merge_sums = jnp.stack((jnp.sum(grad_unit * raw_hat, 0), jnp.sum(grad_unit, 0)))
    grad_raw = norm_back(raw_hat, raw_rstd, grad_unit * merge_scale)
    grad_raw = grad_raw.reshape(raw_pages.shape).astype(BF16)
    for axis in all_axes:
        g_merge = lax.psum_scatter(g_merge, axis, scatter_dimension=0, tiled=True)
    final_sums = jnp.sum(sums_all, 0)[6:8] * is_last.astype(F32) / copies
    edge = jnp.concatenate((merge_sums.reshape(-1), final_sums.reshape(-1)))
    edge = jnp.sum(gather_rows(edge, all_axes), 0)
    place = (section_now * dp_count + dp_now) * tensor_count + tensor_now
    edge_parts = []
    start = 0
    for size, width in ((merge_in, share), (merge_in, share), (D, fshare), (D, fshare)):
        edge_parts.append(lax.dynamic_slice_in_dim(edge, start + place * width, width))
        start += size
    return (
        shown[None, :, None],
        grad_raw,
        g_merge.astype(F32),
        *edge_parts,
        g_qkv[None],
        g_proj[None],
        g_fc1[None],
        g_fc2[None],
        g_qv[None],
        sums[8:12].reshape(1, FF),
        g_table[None],
        sums[0:2][None],
        sums[2:4][None],
        sums[4:6][None],
    )


def solution(mesh):
    return jax.shard_map(
        on_device,
        mesh=mesh,
        in_specs=(
            P("pipe", "dp", "tensor", None),
            P(("pipe", "dp", "tensor"), None),
            P(("pipe", "dp", "tensor")),
            P(("pipe", "dp", "tensor")),
            P(("pipe", "dp", "tensor")),
            P(("pipe", "dp", "tensor")),
            P("pipe", "dp", None, "tensor"),
            P("pipe", "tensor", "dp"),
            P("pipe", "dp", "tensor"),
            P("pipe", "tensor", "dp"),
            P("pipe", None, "tensor"),
            P("pipe", None),
            P("pipe", None, "tensor"),
            P("pipe", None, None),
            P("pipe", None, None),
            P("pipe", None, None),
            P("pipe", None, "dp", "tensor", None),
        ),
        out_specs=(
            P("pipe", None, "dp", "tensor", None),
            P("pipe", "dp", "tensor", None),
            P(("pipe", "dp", "tensor"), None),
            P(("pipe", "dp", "tensor")),
            P(("pipe", "dp", "tensor")),
            P(("pipe", "dp", "tensor")),
            P(("pipe", "dp", "tensor")),
            P("pipe", "dp", None, "tensor"),
            P("pipe", "tensor", "dp"),
            P("pipe", "dp", "tensor"),
            P("pipe", "tensor", "dp"),
            P("pipe", None, "tensor"),
            P("pipe", None),
            P("pipe", None, "tensor"),
            P("pipe", None, None),
            P("pipe", None, None),
            P("pipe", None, None),
        ),
        check_vma=False,
    )
```

```python
import functools

import jax
import jax.numpy as jnp
import numpy as np
from jax import lax
from jax.experimental import pallas as pl
from jax.experimental.pallas import tpu as pltpu
from jax.sharding import PartitionSpec as P

D = 1024
HEAD = 32
FF = 4096
WIN = 10
SHIFT = 5
WIN_ROWS = 4
WIN_COLS = 3
NORM_EPS = 1e-05

GRID_W = WIN * WIN_COLS
UNIT = WIN * GRID_W
LINES = SHIFT * GRID_W
HALF = 160
PAD = 112
KEYS = 128
ROWS = WIN_COLS * PAD
PER = 128 // HEAD
GROUPS = D // 128
STACK = PER * PAD
OWN = 2
BLOCKS = 4
DB = D // OWN
TB = D // BLOCKS
FB = FF // BLOCKS
STEP = PAD
SUMS = 16
VMEM_BYTES = 60 * 1024 * 1024

F32 = jnp.float32
BF16 = jnp.bfloat16


def rel_parts(window):
    offsets = np.arange(window)[:, None] - np.arange(window)[None, :] + window - 1
    return (offsets.reshape(-1)[None, :] == np.arange(2 * window - 1)[:, None]).astype(np.float32)


def shift_mask(grid_rows, grid_cols, window, shift_now):
    region = np.zeros((grid_rows, grid_cols), np.int64)
    region_id = 0
    for span_rows in (
        (0, grid_rows - window),
        (grid_rows - window, grid_rows - shift_now),
        (grid_rows - shift_now, grid_rows),
    ):
        for span_cols in (
            (0, grid_cols - window),
            (grid_cols - window, grid_cols - shift_now),
            (grid_cols - shift_now, grid_cols),
        ):
            region[span_rows[0] : span_rows[1], span_cols[0] : span_cols[1]] = region_id
            region_id += 1
    blocks = region.reshape(grid_rows // window, window, grid_cols // window, window).transpose(
        0, 2, 1, 3
    )
    blocks = blocks.reshape(-1, window * window)
    return np.where(blocks[:, :, None] == blocks[:, None, :], 0.0, -100.0).astype(np.float32)


def window_order(shift_now):
    order = np.zeros((ROWS, 2 * HALF), np.float32)
    for win in range(WIN_COLS):
        for row in range(WIN):
            for col in range(WIN):
                source_col = (win * WIN + col + shift_now) % GRID_W
                source = (row // SHIFT) * HALF + (row % SHIFT) * GRID_W + source_col
                order[win * PAD + row * WIN + col, source] = 1.0
    return order


def norm_stats(values):
    row_mean = jnp.mean(values, -1, keepdims=True)
    centred = values - row_mean
    rstd_rows = lax.rsqrt(jnp.mean(centred * centred, -1, keepdims=True) + NORM_EPS)
    return (centred * rstd_rows, rstd_rows)


def norm_back(normed, rstd_rows, grad_normed):
    return rstd_rows * (
        grad_normed
        - jnp.mean(grad_normed, -1, keepdims=True)
        - normed * jnp.mean(grad_normed * normed, -1, keepdims=True)
    )


def dot_nn(left, right):
    return lax.dot_general(left, right, (((1,), (0,)), ((), ())), preferred_element_type=F32)


def dot_nt(left, right):
    return lax.dot_general(left, right, (((1,), (1,)), ((), ())), preferred_element_type=F32)


def dot_tn(left, right):
    return lax.dot_general(left, right, (((0,), (0,)), ((), ())), preferred_element_type=F32)


def row_chunks(body, carry=None):
    def step(index, state):
        return body(pl.ds(pl.multiple_of(index * STEP, STEP), STEP), state)

    return lax.fori_loop(0, ROWS // STEP, step, carry)


def fold8(values):
    return jnp.sum(values.reshape(values.shape[0] // 8, 8, values.shape[1]), 0)


def head_masks():
    lane_head = lax.broadcasted_iota(jnp.int32, (1, 128), 1) // HEAD
    return [(lane_head == head).astype(F32) for head in range(PER)]


def spread_heads(tile, masks):
    return jnp.concatenate([(tile * mask.astype(BF16)) for mask in masks], 0)


def pick_heads(stacked, masks):
    total = stacked[:PAD] * masks[0]
    for head in range(1, PER):
        total = total + stacked[head * PAD : (head + 1) * PAD] * masks[head]
    return total


def group_columns(group):
    return (group // 2) * (3 * TB) + (group % 2) * 128


def lanes(start, size):
    return pl.ds(pl.multiple_of(start, 128), size)


def forward_kernel(
    flags,
    recv_a,
    recv_b,
    firsts,
    perm_in,
    perm_out,
    mask,
    vecs,
    bias_qkv,
    bias_fc1,
    bias_pos,
    w_qkv,
    w_proj,
    w_fc1,
    w_fc2,
    *refs,
):
    (x_all, qkv_all, probs_all, mixed_all, mid_all, rattn_all, rmlp_all, act_all, slope_all) = refs[11:20]
    out_all, hid_all = refs[20:22]
    sends = refs[22:24]
    (
        v_qkv,
        v_proj,
        v_fc1,
        v_fc2,
        v_pos,
        rin,
        xf,
        xb,
        rattn,
        qkv,
        probs,
        mixed,
        mid,
        rmlp,
        act,
        slope,
        total,
        final,
        outb,
        outs,
        sem_w,
        sem_in,
        sem_out,
        sem_h,
    ) = refs[24:]
    valid = flags[0]
    slot = flags[1]
    is_first = flags[2]
    is_last = flags[3]

    @pl.when(valid == 1)
    def _():
        def w_copy(kind, block):
            source, target = ((w_qkv, v_qkv), (w_fc1, v_fc1), (w_fc2, v_fc2))[kind]
            return pltpu.make_async_copy(
                source.at[:, block], target.at[:, block], sem_w.at[kind * BLOCKS + block]
            )

        def proj_copy():
            return pltpu.make_async_copy(w_proj, v_proj, sem_w.at[3 * BLOCKS])

        def pos_copy():
            return pltpu.make_async_copy(bias_pos, v_pos, sem_w.at[3 * BLOCKS + 1])

        @pl.when(is_first == 1)
        def _():
            pltpu.make_async_copy(
                firsts.at[slot, 0], rin.at[pl.ds(0, HALF)], sem_in.at[0]
            ).start()
            pltpu.make_async_copy(
                firsts.at[slot, 1], rin.at[pl.ds(HALF, HALF)], sem_in.at[1]
            ).start()

        @pl.when(is_first == 0)
        def _():
            pltpu.make_async_copy(recv_a, rin.at[pl.ds(0, HALF)], sem_in.at[0]).start()
            pltpu.make_async_copy(recv_b, rin.at[pl.ds(HALF, HALF)], sem_in.at[1]).start()

        for block in range(BLOCKS):
            w_copy(0, block).start()
        pltpu.make_async_copy(recv_a, rin.at[pl.ds(0, HALF)], sem_in.at[0]).wait()
        pltpu.make_async_copy(recv_b, rin.at[pl.ds(HALF, HALF)], sem_in.at[1]).wait()

        xf[...] = dot_nn(perm_in[...], rin[...])

        def first_norm(rows, state):
            values = xf[rows, :]
            hat, _ = norm_stats(values)
            rattn[rows, :] = (hat * vecs[0:1, :] + vecs[2:3, :]).astype(BF16)
            xb[rows, :] = values.astype(BF16)
            return state

        row_chunks(first_norm)
        saves = [
            pltpu.make_async_copy(rattn, rattn_all.at[slot], sem_out.at[0]),
            pltpu.make_async_copy(xb, x_all.at[slot], sem_out.at[1]),
        ]
        saves[0].start()
        saves[1].start()
        qkv[pl.ds(ROWS, 16), :] = jnp.zeros((16, 3 * D), BF16)

        pos_copy().start()
        proj_copy().start()

        def qkv_block(block, state):
            w_copy(0, block).wait()
            w_copy(1, block).start()
            out = dot_nn(rattn[:, :DB], v_qkv[0, block])
            out = out + dot_nn(rattn[:, DB:], v_qkv[1, block])
            columns = lanes(block * 3 * TB, 3 * TB)
            qkv[pl.ds(0, ROWS), columns] = (out + bias_qkv[:, columns]).astype(BF16)
            return state

        lax.fori_loop(0, BLOCKS, qkv_block, None)
        save_qkv = pltpu.make_async_copy(
            qkv.at[pl.ds(0, ROWS)], qkv_all.at[slot], sem_out.at[2]
        )
        save_qkv.start()
        for block in range(BLOCKS):
            w_copy(2, block).start()
        pos_copy().wait()
        masks = head_masks()

        def attend(win, group):
            base = pl.multiple_of(win * PAD, 16)
            column = group_columns(group)
            query = qkv[pl.ds(base, PAD), lanes(column, 128)]
            key = qkv[pl.ds(base, KEYS), lanes(column + TB, 128)]
            value = qkv[pl.ds(base, KEYS), lanes(column + 2 * TB, 128)]
            scores = dot_nt(spread_heads(query, masks), key)
            scores = scores * HEAD**-0.5 + v_pos[group]
            scores = scores + jnp.concatenate([mask[win]] * PER, 0)
            top = jnp.max(scores, -1, keepdims=True)
            powers = jnp.exp(scores - top)
            low = (powers * (1.0 / jnp.sum(powers, -1, keepdims=True))).astype(BF16)
            probs[win * GROUPS + group] = low
            mixed[pl.ds(base, PAD), lanes(group * 128, 128)] = pick_heads(
                dot_nn(low, value), masks
            ).astype(BF16)

        def attend_window(win, state):
            for group in range(GROUPS):
                attend(win, group)
            return state

        lax.fori_loop(0, WIN_COLS, attend_window, None)
        saves.append(pltpu.make_async_copy(probs, probs_all.at[slot], sem_out.at[3]))
        saves[-1].start()
        saves.append(pltpu.make_async_copy(mixed, mixed_all.at[slot], sem_out.at[4]))
        saves[-1].start()
        proj_copy().wait()
        for own in range(OWN):
            columns = slice(own * DB, (own + 1) * DB)
            out = xf[:, columns] + vecs[4:5, columns]
            for block in range(BLOCKS):
                out = out + dot_nn(mixed[:, block * TB : (block + 1) * TB], v_proj[own, block])
            mid[:, columns] = out
        saves.append(pltpu.make_async_copy(mid, mid_all.at[slot], sem_out.at[5]))
        saves[-1].start()

        def second_norm(rows, state):
            hat, _ = norm_stats(mid[rows, :])
            rmlp[rows, :] = (hat * vecs[1:2, :] + vecs[3:4, :]).astype(BF16)
            total[rows, :] = mid[rows, :] + vecs[5:6, :]
            return state

        row_chunks(second_norm)
        saves.append(pltpu.make_async_copy(rmlp, rmlp_all.at[slot], sem_out.at[6]))
        saves[-1].start()

        def hidden_saves(block):
            columns = lanes(block * FB, FB)
            return [
                pltpu.make_async_copy(
                    source.at[:, columns], target.at[slot, :, columns], sem_h.at[kind * BLOCKS + block]
                )
                for kind, (source, target) in enumerate(((act, act_all), (slope, slope_all)))
            ]

        def hidden_block(block, state):
            w_copy(1, block).wait()
            columns = lanes(block * FB, FB)
            pre = dot_nn(rmlp[:, :DB], v_fc1[0, block]) + dot_nn(rmlp[:, DB:], v_fc1[1, block])
            pre = pre + bias_fc1[:, columns]
            chance = 0.5 + 0.5 * lax.erf(pre * np.float32(0.5**0.5))
            slope[:, columns] = (
                chance + pre * (np.float32((2 * np.pi) ** -0.5) * jnp.exp(-0.5 * pre * pre))
            ).astype(BF16)
            act[:, columns] = (pre * chance).astype(BF16)
            for save in hidden_saves(block):
                save.start()
            w_copy(2, block).wait()
            for own in range(OWN):
                half = slice(own * DB, (own + 1) * DB)
                total[:, half] += dot_nn(act[:, columns], v_fc2[own, block])
            return state

        lax.fori_loop(0, BLOCKS, hidden_block, None)

        def finish(rows, state):
            values = total[rows, :]
            hat, _ = norm_stats(values)
            shown = jnp.where(is_last == 1, hat * vecs[6:7, :] + vecs[7:8, :], values)
            outb[rows, :] = shown.astype(BF16)
            return state

        row_chunks(finish)
        save_out = pltpu.make_async_copy(total, out_all.at[slot], sem_out.at[9])

        @pl.when(is_last == 1)
        def _():
            save_out.start()

        outs[...] = dot_nn(perm_out[...], outb[...]).astype(BF16)
        for half in range(2):
            rows = pl.ds(half * HALF, HALF)
            saves.append(
                pltpu.make_async_copy(outs.at[rows], sends[half], sem_out.at[10 + half])
            )
            saves[-1].start()
            saves.append(
                pltpu.make_async_copy(outs.at[rows], hid_all.at[slot, half], sem_out.at[12 + half])
            )
            saves[-1].start()
        save_qkv.wait()
        for block in range(BLOCKS):
            saves.extend(hidden_saves(block))
        for save in saves:
            save.wait()

        @pl.when(is_last == 1)
        def _():
            save_out.wait()


def backward_kernel(
    flags,
    recv_a,
    recv_b,
    cots,
    perm_in,
    perm_out,
    vecs,
    w_qkv,
    w_proj,
    w_fc1,
    w_fc2,
    probs_all,
    mid_all,
    out_all,
    *refs,
):
    x_all, qkv_all, slope_all, dbm_all, dx_all, sums_all, dpos_all = refs[7:14]
    sends = refs[14:16]
    (
        v_qkv,
        v_proj,
        v_fc1,
        v_fc2,
        rin,
        rcot,
        xb,
        qkv,
        probs,
        mid,
        last,
        slope,
        grad,
        back,
        dbm,
        dba,
        dmix,
        dqkv,
        dpos,
        sums,
        outs,
        sem_w,
        sem_in,
        sem_out,
        sem_h,
    ) = refs[16:]
    valid = flags[0]
    slot = flags[1]
    is_last = flags[3]

    @pl.when(valid == 1)
    def _():
        def w_copy(kind, block):
            source, target = ((w_fc2, v_fc2), (w_fc1, v_fc1), (w_qkv, v_qkv))[kind]
            return pltpu.make_async_copy(
                source.at[:, block], target.at[:, block], sem_w.at[kind * BLOCKS + block]
            )

        def proj_copy():
            return pltpu.make_async_copy(w_proj, v_proj, sem_w.at[3 * BLOCKS])

        def load(index):
            source, target = (
                (cots.at[slot, 0], rcot.at[pl.ds(0, HALF)]),
                (cots.at[slot, 1], rcot.at[pl.ds(HALF, HALF)]),
                (recv_a, rin.at[pl.ds(0, HALF)]),
                (recv_b, rin.at[pl.ds(HALF, HALF)]),
                (out_all.at[slot], last),
                (slope_all.at[slot], slope),
                (mid_all.at[slot], mid),
                (qkv_all.at[slot], qkv.at[pl.ds(0, ROWS)]),
                (probs_all.at[slot], probs),
                (x_all.at[slot], xb),
                (dpos_all, dpos),
            )[index]
            return pltpu.make_async_copy(source, target, sem_in.at[index])

        for index in range(4):
            load(index).start()

        @pl.when(is_last == 1)
        def _():
            load(4).start()

        w_copy(0, 0).start()
        load(5).start()
        w_copy(1, 0).start()
        for index in range(4):
            load(index).wait()
        sums[...] = jnp.zeros_like(sums)
        grad[...] = dot_nn(perm_in[...], rcot[...])

        @pl.when(is_last == 1)
        def _():
            load(4).wait()

            def final_norm(rows, state):
                cot = grad[rows, :]
                hat, rstd = norm_stats(last[rows, :])
                grad[rows, :] = norm_back(hat, rstd, cot * vecs[6:7, :])
                return (state[0] + fold8(cot * hat), state[1] + fold8(cot))

            zero = jnp.zeros((8, D), F32)
            gain, shift = row_chunks(final_norm, (zero, zero))
            sums[6:7, :] = jnp.sum(gain, 0, keepdims=True)
            sums[7:8, :] = jnp.sum(shift, 0, keepdims=True)

        @pl.when(is_last == 0)
        def _():
            grad[...] += dot_nn(perm_in[...], rin[...])

        def enter(rows, state):
            values = grad[rows, :]
            dbm[rows, :] = values.astype(BF16)
            back[rows, :] = jnp.zeros((STEP, D), F32)
            return state + fold8(values)

        out_sum = row_chunks(enter, jnp.zeros((8, D), F32))
        sums[5:6, :] = jnp.sum(out_sum, 0, keepdims=True)
        saves = [pltpu.make_async_copy(dbm, dbm_all.at[slot], sem_out.at[0])]
        saves[0].start()
        load(5).wait()

        def hidden_save(block):
            columns = lanes(block * FB, FB)
            return pltpu.make_async_copy(
                slope.at[:, columns], slope_all.at[slot, :, columns], sem_h.at[block]
            )

        def hidden_block(block, state):
            columns = lanes(block * FB, FB)
            w_copy(0, block).wait()

            @pl.when(block < BLOCKS - 1)
            def _():
                w_copy(0, block + 1).start()
                w_copy(1, block + 1).start()

            @pl.when(block == BLOCKS - 1)
            def _():
                load(6).start()
                proj_copy().start()
                load(7).start()
                load(8).start()

            dact = dot_nt(dbm[:, :DB], v_fc2[0, block]) + dot_nt(dbm[:, DB:], v_fc2[1, block])
            dpre = (dact * slope[:, columns].astype(F32)).astype(BF16)
            slope[:, columns] = dpre
            hidden_save(block).start()
            sums[pl.ds(8 + block, 1), :] = jnp.sum(dpre.astype(F32), 0, keepdims=True)
            w_copy(1, block).wait()
            for own in range(OWN):
                half = slice(own * DB, (own + 1) * DB)
                back[:, half] += dot_nt(slope[:, columns], v_fc1[own, block])
            return state

        lax.fori_loop(0, BLOCKS, hidden_block, None)
        for block in range(BLOCKS):
            w_copy(2, block).start()
        load(9).start()

        @pl.when(slot > 0)
        def _():
            load(10).start()

        load(6).wait()

        def mlp_norm(rows, state):
            hat, rstd = norm_stats(mid[rows, :])
            ready = back[rows, :]
            values = grad[rows, :] + norm_back(hat, rstd, ready * vecs[1:2, :])
            grad[rows, :] = values
            dba[rows, :] = values.astype(BF16)
            back[rows, :] = jnp.zeros((STEP, D), F32)
            return (state[0] + fold8(ready * hat), state[1] + fold8(ready), state[2] + fold8(values))

        zero = jnp.zeros((8, D), F32)
        gain, shift, out_sum = row_chunks(mlp_norm, (zero, zero, zero))
        sums[1:2, :] = jnp.sum(gain, 0, keepdims=True)
        sums[3:4, :] = jnp.sum(shift, 0, keepdims=True)
        sums[4:5, :] = jnp.sum(out_sum, 0, keepdims=True)
        load(9).wait()
        saves.append(pltpu.make_async_copy(dba, x_all.at[slot], sem_out.at[2]))
        saves[-1].start()
        proj_copy().wait()
        for block in range(BLOCKS):
            out = dot_nt(dba[:, :DB], v_proj[0, block]) + dot_nt(dba[:, DB:], v_proj[1, block])
            dmix[:, block * TB : (block + 1) * TB] = out.astype(BF16)
        load(7).wait()
        load(8).wait()

        @pl.when(slot > 0)
        def _():
            load(10).wait()

        @pl.when(slot == 0)
        def _():
            dpos[...] = jnp.zeros_like(dpos)

        qkv[pl.ds(ROWS, 16), :] = jnp.zeros((16, 3 * D), BF16)
        masks = head_masks()

        def attend_back(group, state):
            column = group_columns(group)
            for win in range(WIN_COLS):
                base = win * PAD
                query = qkv[pl.ds(base, PAD), lanes(column, 128)]
                key = qkv[pl.ds(base, KEYS), lanes(column + TB, 128)]
                value = qkv[pl.ds(base, KEYS), lanes(column + 2 * TB, 128)]
                low = probs[win * GROUPS + group]
                dout = spread_heads(dmix[pl.ds(base, PAD), lanes(group * 128, 128)], masks)
                dprob = dot_nt(dout, value)
                weight = low.astype(F32)
                dscore = weight * (dprob - jnp.sum(dprob * weight, -1, keepdims=True))
                dscore = dscore.astype(BF16)
                dpos[group] += dscore.astype(F32)
                dquery = pick_heads(dot_nn(dscore, key), masks) * HEAD**-0.5
                dkey = dot_tn(dscore, spread_heads(query, masks)) * HEAD**-0.5
                dvalue = dot_tn(low, dout)
                dqkv[pl.ds(base, PAD), lanes(column, 128)] = dquery.astype(BF16)
                dqkv[pl.ds(base, PAD), lanes(column + TB, 128)] = dkey[:PAD].astype(BF16)
                dqkv[pl.ds(base, PAD), lanes(column + 2 * TB, 128)] = dvalue[:PAD].astype(BF16)
            return state

        def attend_back_pair(pair, state):
            return attend_back(2 * pair + 1, attend_back(2 * pair, state))

        lax.fori_loop(0, GROUPS // 2, attend_back_pair, None)
        saves.append(pltpu.make_async_copy(dqkv, qkv_all.at[slot], sem_out.at[3]))
        saves[-1].start()
        saves.append(pltpu.make_async_copy(dpos, dpos_all, sem_out.at[4]))
        saves[-1].start()

        def ready_block(block, state):
            columns = lanes(block * 3 * TB, 3 * TB)
            w_copy(2, block).wait()
            for own in range(OWN):
                half = slice(own * DB, (own + 1) * DB)
                back[:, half] += dot_nt(dqkv[:, columns], v_qkv[own, block])
            return state

        lax.fori_loop(0, BLOCKS, ready_block, None)
        for part in range(3):
            columns = slice(part * D, (part + 1) * D)
            sums[12 + part : 13 + part, :] = jnp.sum(dqkv[:, columns].astype(F32), 0, keepdims=True)

        def attn_norm(rows, state):
            hat, rstd = norm_stats(xb[rows, :].astype(F32))
            ready = back[rows, :]
            values = grad[rows, :] + norm_back(hat, rstd, ready * vecs[0:1, :])
            xb[rows, :] = values.astype(BF16)
            return (state[0] + fold8(ready * hat), state[1] + fold8(ready))

        gain, shift = row_chunks(attn_norm, (zero, zero))
        sums[0:1, :] = jnp.sum(gain, 0, keepdims=True)
        sums[2:3, :] = jnp.sum(shift, 0, keepdims=True)
        saves.append(pltpu.make_async_copy(sums, sums_all.at[slot], sem_out.at[5]))
        saves[-1].start()
        outs[...] = dot_nn(perm_out[...], xb[...]).astype(BF16)
        for half in range(2):
            rows = pl.ds(half * HALF, HALF)
            saves.append(
                pltpu.make_async_copy(outs.at[rows], sends[half], sem_out.at[6 + half])
            )
            saves[-1].start()
            saves.append(
                pltpu.make_async_copy(outs.at[rows], dx_all.at[slot, half], sem_out.at[8 + half])
            )
            saves[-1].start()
        for block in range(BLOCKS):
            saves.append(hidden_save(block))
        for save in saves:
            save.wait()


def any_specs(count):
    return [pl.BlockSpec(memory_space=pl.ANY)] * count


def vmem_specs(count):
    return [pl.BlockSpec(memory_space=pltpu.VMEM)] * count


def shapes_of(arrays):
    return [jax.ShapeDtypeStruct(array.shape, array.dtype) for array in arrays]


WEIGHT_SCRATCH = [
    pltpu.VMEM((OWN, BLOCKS, DB, 3 * TB), BF16),
    pltpu.VMEM((OWN, BLOCKS, TB, DB), BF16),
    pltpu.VMEM((OWN, BLOCKS, DB, FB), BF16),
    pltpu.VMEM((OWN, BLOCKS, FB, DB), BF16),
]


def layer_forward(flags, recv_a, recv_b, firsts, tables, weights, stacks):
    inputs = (flags, recv_a, recv_b, firsts) + tuple(tables) + tuple(weights) + tuple(stacks)
    first_stack = len(inputs) - len(stacks)
    wide = lambda dtype: pltpu.VMEM((ROWS, D), dtype)
    results = pl.pallas_call(
        forward_kernel,
        out_shape=shapes_of(stacks) + [jax.ShapeDtypeStruct((HALF, D), BF16)] * 2,
        in_specs=[pl.BlockSpec(memory_space=pltpu.SMEM)]
        + any_specs(3)
        + vmem_specs(6)
        + any_specs(5 + len(stacks)),
        out_specs=any_specs(len(stacks) + 2),
        scratch_shapes=WEIGHT_SCRATCH
        + [
            pltpu.VMEM((GROUPS, STACK, KEYS), F32),
            pltpu.VMEM((2 * HALF, D), BF16),
            wide(F32),
            wide(BF16),
            wide(BF16),
            pltpu.VMEM((ROWS + 16, 3 * D), BF16),
            pltpu.VMEM((WIN_COLS * GROUPS, STACK, KEYS), BF16),
            wide(BF16),
            wide(F32),
            wide(BF16),
            pltpu.VMEM((ROWS, FF), BF16),
            pltpu.VMEM((ROWS, FF), BF16),
            wide(F32),
            wide(F32),
            wide(BF16),
            pltpu.VMEM((2 * HALF, D), BF16),
            pltpu.SemaphoreType.DMA((3 * BLOCKS + 2,)),
            pltpu.SemaphoreType.DMA((2,)),
            pltpu.SemaphoreType.DMA((14,)),
            pltpu.SemaphoreType.DMA((2 * BLOCKS,)),
        ],
        input_output_aliases={first_stack + index: index for index in range(len(stacks))},
        compiler_params=pltpu.CompilerParams(vmem_limit_bytes=VMEM_BYTES),
        cost_estimate=pl.CostEstimate(
            flops=24 * ROWS * D * D, bytes_accessed=40 * 1024 * 1024, transcendentals=ROWS * FF
        ),
        name="layer_forward",
    )(*inputs)
    return results[-2:], tuple(results[:-2])


def layer_backward(flags, recv_a, recv_b, cots, tables, weights, saved, stacks):
    inputs = (
        (flags, recv_a, recv_b, cots) + tuple(tables) + tuple(weights) + tuple(saved) + tuple(stacks)
    )
    first_stack = len(inputs) - len(stacks)
    wide = lambda dtype: pltpu.VMEM((ROWS, D), dtype)
    results = pl.pallas_call(
        backward_kernel,
        out_shape=shapes_of(stacks) + [jax.ShapeDtypeStruct((HALF, D), BF16)] * 2,
        in_specs=[pl.BlockSpec(memory_space=pltpu.SMEM)]
        + any_specs(3)
        + vmem_specs(3)
        + any_specs(4 + len(saved) + len(stacks)),
        out_specs=any_specs(len(stacks) + 2),
        scratch_shapes=WEIGHT_SCRATCH
        + [
            pltpu.VMEM((2 * HALF, D), BF16),
            pltpu.VMEM((2 * HALF, D), BF16),
            wide(BF16),
            pltpu.VMEM((ROWS + 16, 3 * D), BF16),
            pltpu.VMEM((WIN_COLS * GROUPS, STACK, KEYS), BF16),
            wide(F32),
            wide(F32),
            pltpu.VMEM((ROWS, FF), BF16),
            wide(F32),
            wide(F32),
            wide(BF16),
            wide(BF16),
            wide(BF16),
            pltpu.VMEM((ROWS, 3 * D), BF16),
            pltpu.VMEM((GROUPS, STACK, KEYS), F32),
            pltpu.VMEM((SUMS, D), F32),
            pltpu.VMEM((2 * HALF, D), BF16),
            pltpu.SemaphoreType.DMA((3 * BLOCKS + 1,)),
            pltpu.SemaphoreType.DMA((11,)),
            pltpu.SemaphoreType.DMA((10,)),
            pltpu.SemaphoreType.DMA((BLOCKS,)),
        ],
        input_output_aliases={first_stack + index: index for index in range(len(stacks))},
        compiler_params=pltpu.CompilerParams(vmem_limit_bytes=VMEM_BYTES),
        cost_estimate=pl.CostEstimate(
            flops=24 * ROWS * D * D, bytes_accessed=50 * 1024 * 1024, transcendentals=0
        ),
        name="layer_backward",
    )(*inputs)
    return results[-2:], tuple(results[:-2])


def on_device(
    raw_pages,
    w_merge,
    merge_gain,
    merge_bias,
    final_gain,
    final_bias,
    w_qkv,
    w_proj,
    w_fc1,
    w_fc2,
    qv_bias,
    fc1_bias,
    rel_table,
    ln_gain,
    ln_bias,
    out_bias,
    cotangent,
):
    section_now = lax.axis_index("pipe")
    section_count = lax.axis_size("pipe")
    dp_now = lax.axis_index("dp")
    dp_count = lax.axis_size("dp")
    tensor_now = lax.axis_index("tensor")
    tensor_count = lax.axis_size("tensor")
    copies = tensor_count // WIN_ROWS
    unit_now = tensor_now // copies
    all_axes = ("pipe", "dp", "tensor")
    group_axes = ("dp", "tensor")
    is_first = section_now == 0
    is_last = section_now == section_count - 1
    is_odd = section_now % 2 == 1
    owned, _, rows_here, merge_in = raw_pages.shape
    micro_count = cotangent.shape[1]
    own_width = D // dp_count

    def section_pairs(sections, step, moves):
        pairs = []
        for section in sections:
            for tensor in range(tensor_count):
                target = (tensor + copies * moves[section % 2]) % tensor_count
                pairs.append(
                    (section * tensor_count + tensor, (section + step) * tensor_count + target)
                )
        return pairs

    def odd_pairs(move):
        return [
            (
                section * tensor_count + tensor,
                section * tensor_count + (tensor + copies * move) % tensor_count,
            )
            for section in range(1, section_count, 2)
            for tensor in range(tensor_count)
        ]

    def hop(halves, sections, step):
        axes = ("pipe", "tensor")
        to_a = lax.ppermute(halves[1], axes, section_pairs(sections, step, (0, 1)))
        to_b = lax.ppermute(halves[0], axes, section_pairs(sections, step, (-1, 0)))
        return to_a, to_b

    def shares_summed(values, axis):
        count = lax.axis_size(axis)
        index = lax.axis_index(axis)
        blocks = values.reshape((count, values.shape[0] // count) + values.shape[1:])
        total = lax.dynamic_index_in_dim(blocks, index, 0, keepdims=False).astype(F32)
        for step in range(1, count):
            block = lax.dynamic_index_in_dim(blocks, (index + step) % count, 0, keepdims=False)
            pairs = [(source, (source + step) % count) for source in range(count)]
            total = total + lax.ppermute(block, axis, pairs).astype(F32)
        return total

    def summed(values, axis):
        count = lax.axis_size(axis)
        step = 1
        while step < count:
            pairs = [(source, source ^ step) for source in range(count)]
            values = values + lax.ppermute(values, axis, pairs)
            step *= 2
        return values

    def whole_unit(rows, axis):
        if copies == 1:
            return rows
        rows = lax.all_gather(rows, "tensor", axis=axis, tiled=True)
        return lax.dynamic_slice_in_dim(rows, unit_now * UNIT, UNIT, axis)

    def own_part(rows, axis):
        if copies == 1:
            return rows
        return lax.dynamic_slice_in_dim(
            rows, (tensor_now % copies) * rows_here, rows_here, axis
        )

    def gather_rows(values, axes):
        size = values.shape[0]
        tile = 8 * 128
        rows = jnp.pad(values, (0, -size % tile)).reshape(-1, 128)
        rows = lax.all_gather(rows, axes, axis=0, tiled=True)
        return rows.reshape(-1, size + -size % tile)[:, :size]

    def to_halves(rows):
        rows = rows.reshape(rows.shape[:-2] + (2, LINES, D))
        pads = [(0, 0)] * (rows.ndim - 2) + [(0, HALF - LINES), (0, 0)]
        return jnp.pad(rows, pads)

    def from_halves(halves):
        rows = halves[..., :LINES, :]
        return rows.reshape(rows.shape[:-3] + (UNIT, D))

    share = w_merge.shape[0]
    fshare = final_gain.shape[0]
    small = jnp.concatenate((merge_gain, merge_bias, final_gain, final_bias))
    small = jnp.pad(small, (0, 8 * D - small.shape[0])).reshape(8, D)
    packed = jnp.concatenate((w_merge, small)).astype(BF16)
    packed = lax.all_gather(packed, group_axes, axis=0)
    parts = [packed]
    for step in range(1, section_count):
        pairs = [(source, (source + step) % section_count) for source in range(section_count)]
        parts.append(lax.ppermute(packed, "pipe", pairs))
    parts = parts[::-1]
    packed = lax.dynamic_slice_in_dim(
        jnp.concatenate(parts + parts[:-1]),
        (section_count - 1 - section_now) * packed.shape[0],
        section_count * packed.shape[0],
    )
    merge_weight = packed[:, :share].reshape(merge_in, D)
    small_all = packed[:, share]
    merge_scale = small_all[:, :share].reshape(-1).astype(F32)
    merge_shift = small_all[:, share : 2 * share].reshape(-1).astype(F32)
    final_scale = small_all[:, 2 * share : 2 * share + fshare].reshape(-1).astype(F32)
    final_shift = small_all[:, 2 * share + fshare : 2 * (share + fshare)].reshape(-1).astype(F32)

    def gather(weight):
        return lax.all_gather(weight.astype(BF16), group_axes, axis=0)

    split = (dp_count, tensor_count)
    qkv_weight = gather(w_qkv[0].reshape(own_width, -1))
    proj_weight = gather(w_proj[0])
    fc1_weight = gather(w_fc1[0])
    fc2_weight = gather(w_fc2[0])
    if split == (OWN, BLOCKS):
        qkv_weight = qkv_weight.reshape(OWN, BLOCKS, DB, 3 * TB)
        proj_weight = proj_weight.reshape(OWN, BLOCKS, TB, DB)
        fc1_weight = fc1_weight.reshape(OWN, BLOCKS, DB, FB)
        fc2_weight = fc2_weight.reshape(OWN, BLOCKS, FB, DB)
    else:
        qkv_weight = qkv_weight.reshape(split + (own_width, 3, -1)).transpose(0, 2, 3, 1, 4)
        qkv_weight = qkv_weight.reshape(OWN, DB, 3, BLOCKS, TB).transpose(0, 3, 1, 2, 4)
        qkv_weight = qkv_weight.reshape(OWN, BLOCKS, DB, 3 * TB)
        proj_weight = proj_weight.reshape(split + (-1, own_width)).transpose(1, 2, 0, 3)
        proj_weight = proj_weight.reshape(BLOCKS, TB, OWN, DB).transpose(2, 0, 1, 3)
        fc1_weight = fc1_weight.reshape(split + (own_width, -1)).transpose(0, 2, 1, 3)
        fc1_weight = fc1_weight.reshape(OWN, DB, BLOCKS, FB).transpose(0, 2, 1, 3)
        fc2_weight = fc2_weight.reshape(split + (-1, own_width)).transpose(1, 2, 0, 3)
        fc2_weight = fc2_weight.reshape(BLOCKS, FB, OWN, DB).transpose(2, 0, 1, 3)
    weights = (qkv_weight, proj_weight, fc1_weight, fc2_weight)

    heads_here = rel_table.shape[2]
    head_set = jnp.concatenate((qv_bias[0].reshape(-1), rel_table[0].reshape(-1)))
    head_set = gather_rows(head_set, "tensor")
    qv_all = head_set[:, : qv_bias.shape[1] * qv_bias.shape[2]].reshape(tensor_count, 2, -1)
    qv_all = qv_all.transpose(1, 0, 2).reshape(2, BLOCKS, TB)
    bias_qkv = jnp.stack((qv_all[0], jnp.zeros_like(qv_all[0]), qv_all[1]), 1).reshape(1, 3 * D)
    table_all = head_set[:, qv_bias.shape[1] * qv_bias.shape[2] :]
    table_all = table_all.reshape(tensor_count, 2 * WIN - 1, 2 * WIN - 1, heads_here)
    table_all = table_all.transpose(0, 3, 1, 2).reshape(D // HEAD, 2 * WIN - 1, 2 * WIN - 1)
    offsets = jnp.asarray(rel_parts(WIN))
    spread = jnp.einsum("huv,vy->huy", table_all, offsets, precision=lax.Precision.HIGHEST)
    spread = jnp.einsum("huy,ux->hxy", spread, offsets, precision=lax.Precision.HIGHEST)
    spread = spread.reshape(D // HEAD, WIN, WIN, WIN, WIN).transpose(0, 1, 3, 2, 4)
    spread = spread.reshape(D // HEAD, WIN * WIN, WIN * WIN)
    bias_pos = jnp.pad(spread, ((0, 0), (0, PAD - WIN * WIN), (0, 0)))
    bias_pos = jnp.pad(
        bias_pos, ((0, 0), (0, 0), (0, KEYS - WIN * WIN)), constant_values=-1e30
    ).reshape(GROUPS, STACK, KEYS)

    mask_all = np.zeros((WIN_ROWS, WIN_COLS, PAD, KEYS), np.float32)
    mask_all[:, :, : WIN * WIN, : WIN * WIN] = shift_mask(
        WIN * WIN_ROWS, GRID_W, WIN, SHIFT
    ).reshape(WIN_ROWS, WIN_COLS, WIN * WIN, WIN * WIN)
    mask_here = lax.dynamic_index_in_dim(jnp.asarray(mask_all, BF16), unit_now, 0, keepdims=False)
    mask_here = mask_here.astype(F32) * is_odd.astype(F32)
    orders = np.stack((window_order(0), window_order(SHIFT)))
    parity = section_now % 2
    perm_in = lax.dynamic_index_in_dim(jnp.asarray(orders, BF16), parity, 0, keepdims=False)
    perm_out = lax.dynamic_index_in_dim(
        jnp.asarray(orders.transpose(0, 2, 1), BF16), parity, 0, keepdims=False
    )
    vecs = jnp.concatenate(
        (ln_gain[0], ln_bias[0], out_bias[0], final_scale[None], final_shift[None])
    )
    forward_tables = (perm_in, perm_out, mask_here, vecs, bias_qkv, fc1_bias, bias_pos)
    backward_tables = (perm_in, perm_out, vecs)

    raw_rows = raw_pages.reshape(owned * rows_here, merge_in).astype(F32)
    raw_hat, raw_rstd = norm_stats(raw_rows)
    merged_in = (raw_hat * merge_scale + merge_shift).astype(BF16)
    merged = dot_nn(merged_in, merge_weight).astype(BF16).reshape(owned, rows_here, D)
    merged = to_halves(whole_unit(merged, 1))
    first_list = [merged]
    for section in range(1, section_count):
        first_list.append(lax.ppermute(merged, "pipe", [(section, 0)]))
    firsts = jnp.concatenate(first_list, 0)

    cots = to_halves(whole_unit(cotangent[0, :, 0], 1))
    cots_next = lax.ppermute(cots[:, 0], ("pipe", "tensor"), odd_pairs(-1))
    cots = jnp.where(is_odd, jnp.stack((cots[:, 1], cots_next), 1), cots)

    tick_count = micro_count + 2 * (section_count - 1)

    def flags_at(start, tick_now):
        slot_now = tick_now - 2 * start
        is_valid = (slot_now >= 0) & (slot_now < micro_count)
        slot = jnp.clip(slot_now, 0, micro_count - 1)
        return jnp.stack([flag.astype(jnp.int32) for flag in (is_valid, slot, is_first, is_last)])

    def busy(starts, tick_now):
        return [
            section
            for section, start in enumerate(starts)
            if 0 <= tick_now - 2 * start < micro_count
        ]

    def stacks_of(*kinds):
        return pl.pallas_call(
            lambda *refs: None,
            out_shape=[jax.ShapeDtypeStruct(shape, dtype) for shape, dtype in kinds],
            out_specs=any_specs(len(kinds)),
        )()

    def of_micro(shape, dtype):
        return ((micro_count,) + shape, dtype)

    *stacks, empty_a, empty_b = stacks_of(
        of_micro((ROWS, D), BF16),
        of_micro((ROWS, 3 * D), BF16),
        of_micro((WIN_COLS * GROUPS, STACK, KEYS), BF16),
        of_micro((ROWS, D), BF16),
        of_micro((ROWS, D), F32),
        of_micro((ROWS, D), BF16),
        of_micro((ROWS, D), BF16),
        of_micro((ROWS, FF), BF16),
        of_micro((ROWS, FF), BF16),
        of_micro((ROWS, D), F32),
        of_micro((2, HALF, D), BF16),
        ((HALF, D), BF16),
        ((HALF, D), BF16),
    )
    starts = list(range(section_count))
    recv = (empty_a, empty_b)
    for tick_now in range(tick_count):
        senders = [section for section in busy(starts, tick_now - 1) if section < section_count - 1]
        coming = hop(outgoing, senders, 1) if senders else (empty_a, empty_b)
        outgoing, stacks = layer_forward(
            flags_at(section_now, tick_now), *recv, firsts, forward_tables, weights, stacks
        )
        recv = coming
    (
        x_all,
        qkv_all,
        probs_all,
        mixed_all,
        mid_all,
        rattn_all,
        rmlp_all,
        act_all,
        slope_all,
        out_all,
        hid_all,
    ) = stacks
    hid_before = lax.ppermute(hid_all[:, 1], ("pipe", "tensor"), odd_pairs(1))

    stacks = (
        x_all,
        qkv_all,
        slope_all,
        *stacks_of(
            of_micro((ROWS, D), BF16),
            of_micro((2, HALF, D), BF16),
            of_micro((SUMS, D), F32),
            ((GROUPS, STACK, KEYS), F32),
        ),
    )
    starts = starts[::-1]
    recv = (empty_a, empty_b)
    for tick_now in range(tick_count):
        senders = [section for section in busy(starts, tick_now - 1) if section > 0]
        coming = hop(outgoing, senders, -1) if senders else (empty_a, empty_b)
        flags = flags_at(section_count - 1 - section_now, tick_now)
        if tick_now == tick_count // 2:
            flags, hid_before = lax.optimization_barrier((flags, hid_before))
        outgoing, stacks = layer_backward(
            flags,
            *recv,
            cots,
            backward_tables,
            weights,
            (probs_all, mid_all, out_all),
            stacks,
        )
        recv = coming
    dba_all, dqkv_all, dpre_all, dbm_all, dx_all, sums_all, dpos = stacks
    shown = jnp.where(is_odd, jnp.stack((hid_before, hid_all[:, 0]), 1), hid_all)
    shown = own_part(from_halves(shown), 1)

    def weight_gradient(left, right):
        left = left.reshape(micro_count * ROWS, -1)
        right = right.reshape(micro_count * ROWS, D)

        def part(target):
            return dot_tn(
                left, lax.dynamic_slice_in_dim(right, target * own_width, own_width, 1)
            )

        total = None
        for step in range(1, dp_count):
            pairs = [(index, (index + step) % dp_count) for index in range(dp_count)]
            moved = lax.ppermute(
                part((dp_now + step) % dp_count).astype(BF16), "dp", pairs
            ).astype(F32)
            total = moved if total is None else total + moved
        mine = part(dp_now)
        total = mine if total is None else mine + total
        return total / copies

    def over_tensor(total):
        return lax.psum_scatter(total.astype(BF16), "tensor", scatter_dimension=0, tiled=True)

    g_proj = over_tensor(weight_gradient(mixed_all, dba_all)).astype(F32)
    g_fc2 = over_tensor(weight_gradient(act_all, dbm_all)).astype(F32)
    g_fc1 = over_tensor(weight_gradient(dpre_all, rmlp_all)).astype(F32).T
    g_qkv = weight_gradient(dqkv_all, rattn_all)
    if copies > 1:
        g_qkv = g_qkv.reshape(BLOCKS, 3, copies, TB // copies, own_width)
        g_qkv = g_qkv.transpose(0, 2, 1, 3, 4).reshape(3 * D, own_width)
    g_qkv = over_tensor(g_qkv).astype(F32).T.reshape(own_width, 3, D // tensor_count)

    own_grads = dx_all[:owned]
    for section in range(1, section_count):
        moved = lax.ppermute(
            dx_all[section * owned : (section + 1) * owned], "pipe", [(0, section)]
        )
        own_grads = jnp.where(section_now == section, moved, own_grads)
    grad_merged = own_part(from_halves(own_grads), 1).reshape(owned * rows_here, D)
    g_merge = dot_tn(merged_in, grad_merged)
    g_merge = g_merge.reshape(section_count, dp_count, tensor_count, share, D)
    g_merge = shares_summed(g_merge.transpose(1, 0, 2, 3, 4).astype(BF16), "dp")[0]
    g_merge = shares_summed(g_merge.astype(BF16), "pipe")[0]
    g_merge = shares_summed(g_merge.astype(BF16), "tensor")[0]
    grad_unit = dot_nt(grad_merged, merge_weight)
    merge_sums = jnp.stack((jnp.sum(grad_unit * raw_hat, 0), jnp.sum(grad_unit, 0)))
    grad_raw = norm_back(raw_hat, raw_rstd, grad_unit * merge_scale)
    grad_raw = grad_raw.reshape(raw_pages.shape).astype(BF16)

    sums = jnp.sum(sums_all, 0) / copies
    dpos = dpos.reshape(D // HEAD, PAD, KEYS)[:, : WIN * WIN, : WIN * WIN]
    dpos = dpos.reshape(D // HEAD, WIN, WIN, WIN, WIN).transpose(0, 1, 3, 2, 4)
    dpos = dpos.reshape(D // HEAD, WIN * WIN, WIN * WIN) / copies
    dtable = jnp.einsum("hxy,vy->hxv", dpos, offsets, precision=lax.Precision.HIGHEST)
    dtable = jnp.einsum("hxv,ux->huv", dtable, offsets, precision=lax.Precision.HIGHEST)
    final_sums = sums[6:8] * is_last.astype(F32)
    every = jnp.concatenate((merge_sums.reshape(-1), final_sums.reshape(-1)))
    vector = jnp.concatenate((every, sums.reshape(-1), dtable.reshape(-1)))
    size = vector.shape[0]
    vector = jnp.pad(vector, (0, -size % D)).reshape(-1, 128)
    for axis in group_axes:
        vector = summed(vector, axis)
    edge_rows = every.shape[0] // 128
    edge = summed(vector[:edge_rows], "pipe").reshape(-1)
    local_sums = vector[edge_rows:].reshape(-1)
    sums = local_sums[: SUMS * D].reshape(SUMS, D)
    dtable = local_sums[SUMS * D : SUMS * D + dtable.size].reshape(tensor_count, heads_here, -1)
    g_table = lax.dynamic_index_in_dim(dtable, tensor_now, 0, keepdims=False).T
    dqv = sums[12:15].reshape(BLOCKS, 3, TB)[:, 0::2].transpose(1, 0, 2).reshape(2, D)
    g_qv = lax.dynamic_slice_in_dim(
        dqv, tensor_now * (D // tensor_count), D // tensor_count, 1
    )
    place = (section_now * dp_count + dp_now) * tensor_count + tensor_now
    edge_parts = []
    start = 0
    for size, width in ((merge_in, share), (merge_in, share), (D, fshare), (D, fshare)):
        edge_parts.append(lax.dynamic_slice_in_dim(edge, start + place * width, width))
        start += size
    return (
        shown[None, :, None],
        grad_raw,
        g_merge,
        *edge_parts,
        g_qkv[None],
        g_proj[None],
        g_fc1[None],
        g_fc2[None],
        g_qv[None],
        sums[8:12].reshape(1, FF),
        g_table[None],
        sums[0:2][None],
        sums[2:4][None],
        sums[4:6][None],
    )


def solution(mesh):
    return jax.shard_map(
        on_device,
        mesh=mesh,
        in_specs=(
            P("pipe", "dp", "tensor", None),
            P(("pipe", "dp", "tensor"), None),
            P(("pipe", "dp", "tensor")),
            P(("pipe", "dp", "tensor")),
            P(("pipe", "dp", "tensor")),
            P(("pipe", "dp", "tensor")),
            P("pipe", "dp", None, "tensor"),
            P("pipe", "tensor", "dp"),
            P("pipe", "dp", "tensor"),
            P("pipe", "tensor", "dp"),
            P("pipe", None, "tensor"),
            P("pipe", None),
            P("pipe", None, "tensor"),
            P("pipe", None, None),
            P("pipe", None, None),
            P("pipe", None, None),
            P("pipe", None, "dp", "tensor", None),
        ),
        out_specs=(
            P("pipe", None, "dp", "tensor", None),
            P("pipe", "dp", "tensor", None),
            P(("pipe", "dp", "tensor"), None),
            P(("pipe", "dp", "tensor")),
            P(("pipe", "dp", "tensor")),
            P(("pipe", "dp", "tensor")),
            P(("pipe", "dp", "tensor")),
            P("pipe", "dp", None, "tensor"),
            P("pipe", "tensor", "dp"),
            P("pipe", "dp", "tensor"),
            P("pipe", "tensor", "dp"),
            P("pipe", None, "tensor"),
            P("pipe", None),
            P("pipe", None, "tensor"),
            P("pipe", None, None),
            P("pipe", None, None),
            P("pipe", None, None),
        ),
        check_vma=False,
    )
```

```python
import functools

import jax
import jax.numpy as jnp
import numpy as np
from jax import lax
from jax.experimental import pallas as pl
from jax.experimental.pallas import tpu as pltpu
from jax.sharding import PartitionSpec as P

D = 1024
HEAD = 32
FF = 4096
WIN = 10
SHIFT = 5
WIN_ROWS = 4
WIN_COLS = 3
NORM_EPS = 1e-05

GRID_W = WIN * WIN_COLS
UNIT = WIN * GRID_W
LINES = SHIFT * GRID_W
HALF = 160
PAD = 112
KEYS = 128
ROWS = WIN_COLS * PAD
PER = 128 // HEAD
GROUPS = D // 128
STACK = PER * PAD
OWN = 2
BLOCKS = 4
DB = D // OWN
TB = D // BLOCKS
FB = FF // BLOCKS
STEP = PAD
SUMS = 16
VMEM_BYTES = 60 * 1024 * 1024

F32 = jnp.float32
BF16 = jnp.bfloat16


def rel_parts(window):
    offsets = np.arange(window)[:, None] - np.arange(window)[None, :] + window - 1
    return (offsets.reshape(-1)[None, :] == np.arange(2 * window - 1)[:, None]).astype(np.float32)


def shift_mask(grid_rows, grid_cols, window, shift_now):
    region = np.zeros((grid_rows, grid_cols), np.int64)
    region_id = 0
    for span_rows in (
        (0, grid_rows - window),
        (grid_rows - window, grid_rows - shift_now),
        (grid_rows - shift_now, grid_rows),
    ):
        for span_cols in (
            (0, grid_cols - window),
            (grid_cols - window, grid_cols - shift_now),
            (grid_cols - shift_now, grid_cols),
        ):
            region[span_rows[0] : span_rows[1], span_cols[0] : span_cols[1]] = region_id
            region_id += 1
    blocks = region.reshape(grid_rows // window, window, grid_cols // window, window).transpose(
        0, 2, 1, 3
    )
    blocks = blocks.reshape(-1, window * window)
    return np.where(blocks[:, :, None] == blocks[:, None, :], 0.0, -100.0).astype(np.float32)


def window_order(shift_now):
    order = np.zeros((ROWS, 2 * HALF), np.float32)
    for win in range(WIN_COLS):
        for row in range(WIN):
            for col in range(WIN):
                source_col = (win * WIN + col + shift_now) % GRID_W
                source = (row // SHIFT) * HALF + (row % SHIFT) * GRID_W + source_col
                order[win * PAD + row * WIN + col, source] = 1.0
    return order


def norm_stats(values):
    row_mean = jnp.mean(values, -1, keepdims=True)
    centred = values - row_mean
    rstd_rows = lax.rsqrt(jnp.mean(centred * centred, -1, keepdims=True) + NORM_EPS)
    return (centred * rstd_rows, rstd_rows)


def norm_back(normed, rstd_rows, grad_normed):
    return rstd_rows * (
        grad_normed
        - jnp.mean(grad_normed, -1, keepdims=True)
        - normed * jnp.mean(grad_normed * normed, -1, keepdims=True)
    )


def dot_nn(left, right):
    return lax.dot_general(left, right, (((1,), (0,)), ((), ())), preferred_element_type=F32)


def dot_nt(left, right):
    return lax.dot_general(left, right, (((1,), (1,)), ((), ())), preferred_element_type=F32)


def dot_tn(left, right):
    return lax.dot_general(left, right, (((0,), (0,)), ((), ())), preferred_element_type=F32)


def row_chunks(body, carry=None):
    def step(index, state):
        return body(pl.ds(pl.multiple_of(index * STEP, STEP), STEP), state)

    return lax.fori_loop(0, ROWS // STEP, step, carry)


def fold8(values):
    return jnp.sum(values.reshape(values.shape[0] // 8, 8, values.shape[1]), 0)


def head_masks():
    lane_head = lax.broadcasted_iota(jnp.int32, (1, 128), 1) // HEAD
    return [(lane_head == head).astype(F32) for head in range(PER)]


def spread_heads(tile, masks):
    return jnp.concatenate([(tile * mask.astype(BF16)) for mask in masks], 0)


def pick_heads(stacked, masks):
    total = stacked[:PAD] * masks[0]
    for head in range(1, PER):
        total = total + stacked[head * PAD : (head + 1) * PAD] * masks[head]
    return total


def group_columns(group):
    return (group // 2) * (3 * TB) + (group % 2) * 128


def weight_views(w_tall, w_wide, v_qkv, v_fc1, v_fc2, block):
    return (
        (w_wide.at[:, block, :, pl.ds(0, 3 * TB)], v_qkv.at[:, block]),
        (w_wide.at[:, block, :, pl.ds(3 * TB, FB)], v_fc1.at[:, block]),
        (w_tall.at[:, block, pl.ds(0, FB)], v_fc2.at[:, block]),
    )


def lanes(start, size):
    return pl.ds(pl.multiple_of(start, 128), size)


def forward_kernel(
    flags,
    recv_a,
    recv_b,
    firsts,
    perm_in,
    perm_out,
    mask,
    vecs,
    bias_qkv,
    bias_fc1,
    bias_pos,
    w_tall,
    w_wide,
    *refs,
):
    (x_all, qkv_all, probs_all, mixed_all, mid_all, rattn_all, rmlp_all, act_all, slope_all) = refs[11:20]
    out_all, hid_all = refs[20:22]
    sends = refs[22:24]
    (
        v_qkv,
        v_proj,
        v_fc1,
        v_fc2,
        v_pos,
        rin,
        xf,
        xb,
        rattn,
        qkv,
        probs,
        mixed,
        mid,
        rmlp,
        act,
        slope,
        total,
        final,
        outb,
        outs,
        sem_w,
        sem_in,
        sem_out,
        sem_h,
    ) = refs[24:]
    valid = flags[0]
    slot = flags[1]
    is_first = flags[2]
    is_last = flags[3]

    @pl.when(valid == 1)
    def _():
        def w_copy(kind, block):
            source, target = weight_views(w_tall, w_wide, v_qkv, v_fc1, v_fc2, block)[kind]
            return pltpu.make_async_copy(source, target, sem_w.at[kind * BLOCKS + block])

        def proj_copy():
            return pltpu.make_async_copy(
                w_tall.at[:, :, pl.ds(FB, TB)], v_proj, sem_w.at[3 * BLOCKS]
            )

        def pos_copy():
            return pltpu.make_async_copy(bias_pos, v_pos, sem_w.at[3 * BLOCKS + 1])

        @pl.when(is_first == 1)
        def _():
            pltpu.make_async_copy(
                firsts.at[slot, 0], rin.at[pl.ds(0, HALF)], sem_in.at[0]
            ).start()
            pltpu.make_async_copy(
                firsts.at[slot, 1], rin.at[pl.ds(HALF, HALF)], sem_in.at[1]
            ).start()

        @pl.when(is_first == 0)
        def _():
            pltpu.make_async_copy(recv_a, rin.at[pl.ds(0, HALF)], sem_in.at[0]).start()
            pltpu.make_async_copy(recv_b, rin.at[pl.ds(HALF, HALF)], sem_in.at[1]).start()

        for block in range(BLOCKS):
            w_copy(0, block).start()
        pltpu.make_async_copy(recv_a, rin.at[pl.ds(0, HALF)], sem_in.at[0]).wait()
        pltpu.make_async_copy(recv_b, rin.at[pl.ds(HALF, HALF)], sem_in.at[1]).wait()

        xf[...] = dot_nn(perm_in[...], rin[...])

        def first_norm(rows, state):
            values = xf[rows, :]
            hat, _ = norm_stats(values)
            rattn[rows, :] = (hat * vecs[0:1, :] + vecs[2:3, :]).astype(BF16)
            xb[rows, :] = values.astype(BF16)
            return state

        row_chunks(first_norm)
        saves = [
            pltpu.make_async_copy(rattn, rattn_all.at[slot], sem_out.at[0]),
            pltpu.make_async_copy(xb, x_all.at[slot], sem_out.at[1]),
        ]
        saves[0].start()
        saves[1].start()
        qkv[pl.ds(ROWS, 16), :] = jnp.zeros((16, 3 * D), BF16)

        pos_copy().start()
        proj_copy().start()

        def qkv_block(block, state):
            w_copy(0, block).wait()
            w_copy(1, block).start()
            out = dot_nn(rattn[:, :DB], v_qkv[0, block])
            out = out + dot_nn(rattn[:, DB:], v_qkv[1, block])
            columns = lanes(block * 3 * TB, 3 * TB)
            qkv[pl.ds(0, ROWS), columns] = (out + bias_qkv[:, columns]).astype(BF16)
            return state

        lax.fori_loop(0, BLOCKS, qkv_block, None)
        save_qkv = pltpu.make_async_copy(
            qkv.at[pl.ds(0, ROWS)], qkv_all.at[slot], sem_out.at[2]
        )
        save_qkv.start()
        for block in range(BLOCKS):
            w_copy(2, block).start()
        pos_copy().wait()
        masks = head_masks()

        def attend(win, group):
            base = pl.multiple_of(win * PAD, 16)
            column = group_columns(group)
            query = qkv[pl.ds(base, PAD), lanes(column, 128)]
            key = qkv[pl.ds(base, KEYS), lanes(column + TB, 128)]
            value = qkv[pl.ds(base, KEYS), lanes(column + 2 * TB, 128)]
            scores = dot_nt(spread_heads(query, masks), key)
            scores = scores * HEAD**-0.5 + v_pos[group]
            scores = scores + jnp.concatenate([mask[win]] * PER, 0)
            top = jnp.max(scores, -1, keepdims=True)
            powers = jnp.exp(scores - top)
            low = (powers * (1.0 / jnp.sum(powers, -1, keepdims=True))).astype(BF16)
            probs[win * GROUPS + group] = low
            mixed[pl.ds(base, PAD), lanes(group * 128, 128)] = pick_heads(
                dot_nn(low, value), masks
            ).astype(BF16)

        def attend_window(win, state):
            for group in range(GROUPS):
                attend(win, group)
            return state

        lax.fori_loop(0, WIN_COLS, attend_window, None)
        saves.append(pltpu.make_async_copy(probs, probs_all.at[slot], sem_out.at[3]))
        saves[-1].start()
        saves.append(pltpu.make_async_copy(mixed, mixed_all.at[slot], sem_out.at[4]))
        saves[-1].start()
        proj_copy().wait()
        for own in range(OWN):
            columns = slice(own * DB, (own + 1) * DB)
            out = xf[:, columns] + vecs[4:5, columns]
            for block in range(BLOCKS):
                out = out + dot_nn(mixed[:, block * TB : (block + 1) * TB], v_proj[own, block])
            mid[:, columns] = out
        saves.append(pltpu.make_async_copy(mid, mid_all.at[slot], sem_out.at[5]))
        saves[-1].start()

        def second_norm(rows, state):
            hat, _ = norm_stats(mid[rows, :])
            rmlp[rows, :] = (hat * vecs[1:2, :] + vecs[3:4, :]).astype(BF16)
            total[rows, :] = mid[rows, :] + vecs[5:6, :]
            return state

        row_chunks(second_norm)
        saves.append(pltpu.make_async_copy(rmlp, rmlp_all.at[slot], sem_out.at[6]))
        saves[-1].start()

        def hidden_saves(block):
            columns = lanes(block * FB, FB)
            return [
                pltpu.make_async_copy(
                    source.at[:, columns], target.at[slot, :, columns], sem_h.at[kind * BLOCKS + block]
                )
                for kind, (source, target) in enumerate(((act, act_all), (slope, slope_all)))
            ]

        def hidden_block(block, state):
            w_copy(1, block).wait()
            columns = lanes(block * FB, FB)
            pre = dot_nn(rmlp[:, :DB], v_fc1[0, block]) + dot_nn(rmlp[:, DB:], v_fc1[1, block])
            pre = pre + bias_fc1[:, columns]
            chance = 0.5 + 0.5 * lax.erf(pre * np.float32(0.5**0.5))
            slope[:, columns] = (
                chance + pre * (np.float32((2 * np.pi) ** -0.5) * jnp.exp(-0.5 * pre * pre))
            ).astype(BF16)
            act[:, columns] = (pre * chance).astype(BF16)
            for save in hidden_saves(block):
                save.start()
            w_copy(2, block).wait()
            for own in range(OWN):
                half = slice(own * DB, (own + 1) * DB)
                total[:, half] += dot_nn(act[:, columns], v_fc2[own, block])
            return state

        lax.fori_loop(0, BLOCKS, hidden_block, None)

        def finish(rows, state):
            values = total[rows, :]
            hat, _ = norm_stats(values)
            shown = jnp.where(is_last == 1, hat * vecs[6:7, :] + vecs[7:8, :], values)
            outb[rows, :] = shown.astype(BF16)
            return state

        row_chunks(finish)
        save_out = pltpu.make_async_copy(total, out_all.at[slot], sem_out.at[9])

        @pl.when(is_last == 1)
        def _():
            save_out.start()

        outs[...] = dot_nn(perm_out[...], outb[...]).astype(BF16)
        for half in range(2):
            rows = pl.ds(half * HALF, HALF)
            saves.append(
                pltpu.make_async_copy(outs.at[rows], sends[half], sem_out.at[10 + half])
            )
            saves[-1].start()
            saves.append(
                pltpu.make_async_copy(outs.at[rows], hid_all.at[slot, half], sem_out.at[12 + half])
            )
            saves[-1].start()
        save_qkv.wait()
        for block in range(BLOCKS):
            saves.extend(hidden_saves(block))
        for save in saves:
            save.wait()

        @pl.when(is_last == 1)
        def _():
            save_out.wait()


def backward_kernel(
    flags,
    recv_a,
    recv_b,
    cots,
    perm_in,
    perm_out,
    vecs,
    w_tall,
    w_wide,
    probs_all,
    mid_all,
    out_all,
    *refs,
):
    x_all, qkv_all, slope_all, dbm_all, dx_all, sums_all, dpos_all = refs[7:14]
    sends = refs[14:16]
    (
        v_qkv,
        v_proj,
        v_fc1,
        v_fc2,
        rin,
        rcot,
        xb,
        qkv,
        probs,
        mid,
        last,
        slope,
        grad,
        back,
        dbm,
        dba,
        dmix,
        dqkv,
        dpos,
        sums,
        outs,
        sem_w,
        sem_in,
        sem_out,
        sem_h,
    ) = refs[16:]
    valid = flags[0]
    slot = flags[1]
    is_last = flags[3]

    @pl.when(valid == 1)
    def _():
        def w_copy(kind, block):
            source, target = weight_views(w_tall, w_wide, v_qkv, v_fc1, v_fc2, block)[2 - kind]
            return pltpu.make_async_copy(source, target, sem_w.at[kind * BLOCKS + block])

        def proj_copy():
            return pltpu.make_async_copy(
                w_tall.at[:, :, pl.ds(FB, TB)], v_proj, sem_w.at[3 * BLOCKS]
            )

        def load(index):
            source, target = (
                (cots.at[slot, 0], rcot.at[pl.ds(0, HALF)]),
                (cots.at[slot, 1], rcot.at[pl.ds(HALF, HALF)]),
                (recv_a, rin.at[pl.ds(0, HALF)]),
                (recv_b, rin.at[pl.ds(HALF, HALF)]),
                (out_all.at[slot], last),
                (slope_all.at[slot], slope),
                (mid_all.at[slot], mid),
                (qkv_all.at[slot], qkv.at[pl.ds(0, ROWS)]),
                (probs_all.at[slot], probs),
                (x_all.at[slot], xb),
                (dpos_all, dpos),
            )[index]
            return pltpu.make_async_copy(source, target, sem_in.at[index])

        for index in range(4):
            load(index).start()

        @pl.when(is_last == 1)
        def _():
            load(4).start()

        w_copy(0, 0).start()
        load(5).start()
        w_copy(1, 0).start()
        for index in range(4):
            load(index).wait()
        sums[...] = jnp.zeros_like(sums)
        grad[...] = dot_nn(perm_in[...], rcot[...])

        @pl.when(is_last == 1)
        def _():
            load(4).wait()

            def final_norm(rows, state):
                cot = grad[rows, :]
                hat, rstd = norm_stats(last[rows, :])
                grad[rows, :] = norm_back(hat, rstd, cot * vecs[6:7, :])
                return (state[0] + fold8(cot * hat), state[1] + fold8(cot))

            zero = jnp.zeros((8, D), F32)
            gain, shift = row_chunks(final_norm, (zero, zero))
            sums[6:7, :] = jnp.sum(gain, 0, keepdims=True)
            sums[7:8, :] = jnp.sum(shift, 0, keepdims=True)

        @pl.when(is_last == 0)
        def _():
            grad[...] += dot_nn(perm_in[...], rin[...])

        def enter(rows, state):
            values = grad[rows, :]
            dbm[rows, :] = values.astype(BF16)
            back[rows, :] = jnp.zeros((STEP, D), F32)
            return state + fold8(values)

        out_sum = row_chunks(enter, jnp.zeros((8, D), F32))
        sums[5:6, :] = jnp.sum(out_sum, 0, keepdims=True)
        saves = [pltpu.make_async_copy(dbm, dbm_all.at[slot], sem_out.at[0])]
        saves[0].start()
        load(5).wait()

        def hidden_save(block):
            columns = lanes(block * FB, FB)
            return pltpu.make_async_copy(
                slope.at[:, columns], slope_all.at[slot, :, columns], sem_h.at[block]
            )

        def hidden_block(block, state):
            columns = lanes(block * FB, FB)
            w_copy(0, block).wait()

            @pl.when(block < BLOCKS - 1)
            def _():
                w_copy(0, block + 1).start()
                w_copy(1, block + 1).start()

            @pl.when(block == BLOCKS - 1)
            def _():
                load(6).start()
                proj_copy().start()
                load(7).start()
                load(8).start()

            dact = dot_nt(dbm[:, :DB], v_fc2[0, block]) + dot_nt(dbm[:, DB:], v_fc2[1, block])
            dpre = (dact * slope[:, columns].astype(F32)).astype(BF16)
            slope[:, columns] = dpre
            hidden_save(block).start()
            sums[pl.ds(8 + block, 1), :] = jnp.sum(dpre.astype(F32), 0, keepdims=True)
            w_copy(1, block).wait()
            for own in range(OWN):
                half = slice(own * DB, (own + 1) * DB)
                back[:, half] += dot_nt(slope[:, columns], v_fc1[own, block])
            return state

        lax.fori_loop(0, BLOCKS, hidden_block, None)
        for block in range(BLOCKS):
            w_copy(2, block).start()
        load(9).start()

        @pl.when(slot > 0)
        def _():
            load(10).start()

        load(6).wait()

        def mlp_norm(rows, state):
            hat, rstd = norm_stats(mid[rows, :])
            ready = back[rows, :]
            values = grad[rows, :] + norm_back(hat, rstd, ready * vecs[1:2, :])
            grad[rows, :] = values
            dba[rows, :] = values.astype(BF16)
            back[rows, :] = jnp.zeros((STEP, D), F32)
            return (state[0] + fold8(ready * hat), state[1] + fold8(ready), state[2] + fold8(values))

        zero = jnp.zeros((8, D), F32)
        gain, shift, out_sum = row_chunks(mlp_norm, (zero, zero, zero))
        sums[1:2, :] = jnp.sum(gain, 0, keepdims=True)
        sums[3:4, :] = jnp.sum(shift, 0, keepdims=True)
        sums[4:5, :] = jnp.sum(out_sum, 0, keepdims=True)
        load(9).wait()
        saves.append(pltpu.make_async_copy(dba, x_all.at[slot], sem_out.at[2]))
        saves[-1].start()
        proj_copy().wait()
        for block in range(BLOCKS):
            out = dot_nt(dba[:, :DB], v_proj[0, block]) + dot_nt(dba[:, DB:], v_proj[1, block])
            dmix[:, block * TB : (block + 1) * TB] = out.astype(BF16)
        load(7).wait()
        load(8).wait()

        @pl.when(slot > 0)
        def _():
            load(10).wait()

        @pl.when(slot == 0)
        def _():
            dpos[...] = jnp.zeros_like(dpos)

        qkv[pl.ds(ROWS, 16), :] = jnp.zeros((16, 3 * D), BF16)
        masks = head_masks()

        def attend_back(group, state):
            column = group_columns(group)
            for win in range(WIN_COLS):
                base = win * PAD
                query = qkv[pl.ds(base, PAD), lanes(column, 128)]
                key = qkv[pl.ds(base, KEYS), lanes(column + TB, 128)]
                value = qkv[pl.ds(base, KEYS), lanes(column + 2 * TB, 128)]
                low = probs[win * GROUPS + group]
                dout = spread_heads(dmix[pl.ds(base, PAD), lanes(group * 128, 128)], masks)
                dprob = dot_nt(dout, value)
                weight = low.astype(F32)
                dscore = weight * (dprob - jnp.sum(dprob * weight, -1, keepdims=True))
                dscore = dscore.astype(BF16)
                dpos[group] += dscore.astype(F32)
                dquery = pick_heads(dot_nn(dscore, key), masks) * HEAD**-0.5
                dkey = dot_tn(dscore, spread_heads(query, masks)) * HEAD**-0.5
                dvalue = dot_tn(low, dout)
                dqkv[pl.ds(base, PAD), lanes(column, 128)] = dquery.astype(BF16)
                dqkv[pl.ds(base, PAD), lanes(column + TB, 128)] = dkey[:PAD].astype(BF16)
                dqkv[pl.ds(base, PAD), lanes(column + 2 * TB, 128)] = dvalue[:PAD].astype(BF16)
            return state

        def attend_back_pair(pair, state):
            return attend_back(2 * pair + 1, attend_back(2 * pair, state))

        lax.fori_loop(0, GROUPS // 2, attend_back_pair, None)
        saves.append(pltpu.make_async_copy(dqkv, qkv_all.at[slot], sem_out.at[3]))
        saves[-1].start()
        saves.append(pltpu.make_async_copy(dpos, dpos_all, sem_out.at[4]))
        saves[-1].start()

        def ready_block(block, state):
            columns = lanes(block * 3 * TB, 3 * TB)
            w_copy(2, block).wait()
            for own in range(OWN):
                half = slice(own * DB, (own + 1) * DB)
                back[:, half] += dot_nt(dqkv[:, columns], v_qkv[own, block])
            return state

        lax.fori_loop(0, BLOCKS, ready_block, None)
        for part in range(3):
            columns = slice(part * D, (part + 1) * D)
            sums[12 + part : 13 + part, :] = jnp.sum(dqkv[:, columns].astype(F32), 0, keepdims=True)

        def attn_norm(rows, state):
            hat, rstd = norm_stats(xb[rows, :].astype(F32))
            ready = back[rows, :]
            values = grad[rows, :] + norm_back(hat, rstd, ready * vecs[0:1, :])
            xb[rows, :] = values.astype(BF16)
            return (state[0] + fold8(ready * hat), state[1] + fold8(ready))

        gain, shift = row_chunks(attn_norm, (zero, zero))
        sums[0:1, :] = jnp.sum(gain, 0, keepdims=True)
        sums[2:3, :] = jnp.sum(shift, 0, keepdims=True)
        saves.append(pltpu.make_async_copy(sums, sums_all.at[slot], sem_out.at[5]))
        saves[-1].start()
        outs[...] = dot_nn(perm_out[...], xb[...]).astype(BF16)
        for half in range(2):
            rows = pl.ds(half * HALF, HALF)
            saves.append(
                pltpu.make_async_copy(outs.at[rows], sends[half], sem_out.at[6 + half])
            )
            saves[-1].start()
            saves.append(
                pltpu.make_async_copy(outs.at[rows], dx_all.at[slot, half], sem_out.at[8 + half])
            )
            saves[-1].start()
        for block in range(BLOCKS):
            saves.append(hidden_save(block))
        for save in saves:
            save.wait()


def any_specs(count):
    return [pl.BlockSpec(memory_space=pl.ANY)] * count


def vmem_specs(count):
    return [pl.BlockSpec(memory_space=pltpu.VMEM)] * count


def shapes_of(arrays):
    return [jax.ShapeDtypeStruct(array.shape, array.dtype) for array in arrays]


WEIGHT_SCRATCH = [
    pltpu.VMEM((OWN, BLOCKS, DB, 3 * TB), BF16),
    pltpu.VMEM((OWN, BLOCKS, TB, DB), BF16),
    pltpu.VMEM((OWN, BLOCKS, DB, FB), BF16),
    pltpu.VMEM((OWN, BLOCKS, FB, DB), BF16),
]


def layer_forward(flags, recv_a, recv_b, firsts, tables, weights, stacks):
    inputs = (flags, recv_a, recv_b, firsts) + tuple(tables) + tuple(weights) + tuple(stacks)
    first_stack = len(inputs) - len(stacks)
    wide = lambda dtype: pltpu.VMEM((ROWS, D), dtype)
    results = pl.pallas_call(
        forward_kernel,
        out_shape=shapes_of(stacks) + [jax.ShapeDtypeStruct((HALF, D), BF16)] * 2,
        in_specs=[pl.BlockSpec(memory_space=pltpu.SMEM)]
        + any_specs(3)
        + vmem_specs(6)
        + any_specs(3 + len(stacks)),
        out_specs=any_specs(len(stacks) + 2),
        scratch_shapes=WEIGHT_SCRATCH
        + [
            pltpu.VMEM((GROUPS, STACK, KEYS), F32),
            pltpu.VMEM((2 * HALF, D), BF16),
            wide(F32),
            wide(BF16),
            wide(BF16),
            pltpu.VMEM((ROWS + 16, 3 * D), BF16),
            pltpu.VMEM((WIN_COLS * GROUPS, STACK, KEYS), BF16),
            wide(BF16),
            wide(F32),
            wide(BF16),
            pltpu.VMEM((ROWS, FF), BF16),
            pltpu.VMEM((ROWS, FF), BF16),
            wide(F32),
            wide(F32),
            wide(BF16),
            pltpu.VMEM((2 * HALF, D), BF16),
            pltpu.SemaphoreType.DMA((3 * BLOCKS + 2,)),
            pltpu.SemaphoreType.DMA((2,)),
            pltpu.SemaphoreType.DMA((14,)),
            pltpu.SemaphoreType.DMA((2 * BLOCKS,)),
        ],
        input_output_aliases={first_stack + index: index for index in range(len(stacks))},
        compiler_params=pltpu.CompilerParams(vmem_limit_bytes=VMEM_BYTES),
        cost_estimate=pl.CostEstimate(
            flops=24 * ROWS * D * D, bytes_accessed=40 * 1024 * 1024, transcendentals=ROWS * FF
        ),
        name="layer_forward",
    )(*inputs)
    return results[-2:], tuple(results[:-2])


def layer_backward(flags, recv_a, recv_b, cots, tables, weights, saved, stacks):
    inputs = (
        (flags, recv_a, recv_b, cots) + tuple(tables) + tuple(weights) + tuple(saved) + tuple(stacks)
    )
    first_stack = len(inputs) - len(stacks)
    wide = lambda dtype: pltpu.VMEM((ROWS, D), dtype)
    results = pl.pallas_call(
        backward_kernel,
        out_shape=shapes_of(stacks) + [jax.ShapeDtypeStruct((HALF, D), BF16)] * 2,
        in_specs=[pl.BlockSpec(memory_space=pltpu.SMEM)]
        + any_specs(3)
        + vmem_specs(3)
        + any_specs(2 + len(saved) + len(stacks)),
        out_specs=any_specs(len(stacks) + 2),
        scratch_shapes=WEIGHT_SCRATCH
        + [
            pltpu.VMEM((2 * HALF, D), BF16),
            pltpu.VMEM((2 * HALF, D), BF16),
            wide(BF16),
            pltpu.VMEM((ROWS + 16, 3 * D), BF16),
            pltpu.VMEM((WIN_COLS * GROUPS, STACK, KEYS), BF16),
            wide(F32),
            wide(F32),
            pltpu.VMEM((ROWS, FF), BF16),
            wide(F32),
            wide(F32),
            wide(BF16),
            wide(BF16),
            wide(BF16),
            pltpu.VMEM((ROWS, 3 * D), BF16),
            pltpu.VMEM((GROUPS, STACK, KEYS), F32),
            pltpu.VMEM((SUMS, D), F32),
            pltpu.VMEM((2 * HALF, D), BF16),
            pltpu.SemaphoreType.DMA((3 * BLOCKS + 1,)),
            pltpu.SemaphoreType.DMA((11,)),
            pltpu.SemaphoreType.DMA((10,)),
            pltpu.SemaphoreType.DMA((BLOCKS,)),
        ],
        input_output_aliases={first_stack + index: index for index in range(len(stacks))},
        compiler_params=pltpu.CompilerParams(vmem_limit_bytes=VMEM_BYTES),
        cost_estimate=pl.CostEstimate(
            flops=24 * ROWS * D * D, bytes_accessed=50 * 1024 * 1024, transcendentals=0
        ),
        name="layer_backward",
    )(*inputs)
    return results[-2:], tuple(results[:-2])


def on_device(
    raw_pages,
    w_merge,
    merge_gain,
    merge_bias,
    final_gain,
    final_bias,
    w_qkv,
    w_proj,
    w_fc1,
    w_fc2,
    qv_bias,
    fc1_bias,
    rel_table,
    ln_gain,
    ln_bias,
    out_bias,
    cotangent,
):
    section_now = lax.axis_index("pipe")
    section_count = lax.axis_size("pipe")
    dp_now = lax.axis_index("dp")
    dp_count = lax.axis_size("dp")
    tensor_now = lax.axis_index("tensor")
    tensor_count = lax.axis_size("tensor")
    copies = tensor_count // WIN_ROWS
    unit_now = tensor_now // copies
    all_axes = ("pipe", "dp", "tensor")
    group_axes = ("dp", "tensor")
    is_first = section_now == 0
    is_last = section_now == section_count - 1
    is_odd = section_now % 2 == 1
    owned, _, rows_here, merge_in = raw_pages.shape
    micro_count = cotangent.shape[1]
    own_width = D // dp_count

    def section_pairs(sections, step, moves):
        pairs = []
        for section in sections:
            for tensor in range(tensor_count):
                target = (tensor + copies * moves[section % 2]) % tensor_count
                pairs.append(
                    (section * tensor_count + tensor, (section + step) * tensor_count + target)
                )
        return pairs

    def odd_pairs(move):
        return [
            (
                section * tensor_count + tensor,
                section * tensor_count + (tensor + copies * move) % tensor_count,
            )
            for section in range(1, section_count, 2)
            for tensor in range(tensor_count)
        ]

    def hop(halves, sections, step):
        axes = ("pipe", "tensor")
        to_a = lax.ppermute(halves[1], axes, section_pairs(sections, step, (0, 1)))
        to_b = lax.ppermute(halves[0], axes, section_pairs(sections, step, (-1, 0)))
        return to_a, to_b

    def shares_summed(values, axis):
        count = lax.axis_size(axis)
        index = lax.axis_index(axis)
        blocks = values.reshape((count, values.shape[0] // count) + values.shape[1:])
        total = lax.dynamic_index_in_dim(blocks, index, 0, keepdims=False).astype(F32)
        for step in range(1, count):
            block = lax.dynamic_index_in_dim(blocks, (index + step) % count, 0, keepdims=False)
            pairs = [(source, (source + step) % count) for source in range(count)]
            total = total + lax.ppermute(block, axis, pairs).astype(F32)
        return total

    def summed(values, axis):
        count = lax.axis_size(axis)
        step = 1
        while step < count:
            pairs = [(source, source ^ step) for source in range(count)]
            values = values + lax.ppermute(values, axis, pairs)
            step *= 2
        return values

    def whole_unit(rows, axis):
        if copies == 1:
            return rows
        rows = lax.all_gather(rows, "tensor", axis=axis, tiled=True)
        return lax.dynamic_slice_in_dim(rows, unit_now * UNIT, UNIT, axis)

    def own_part(rows, axis):
        if copies == 1:
            return rows
        return lax.dynamic_slice_in_dim(
            rows, (tensor_now % copies) * rows_here, rows_here, axis
        )

    def gather_rows(values, axes):
        size = values.shape[0]
        tile = 8 * 128
        rows = jnp.pad(values, (0, -size % tile)).reshape(-1, 128)
        rows = lax.all_gather(rows, axes, axis=0, tiled=True)
        return rows.reshape(-1, size + -size % tile)[:, :size]

    def to_halves(rows):
        rows = rows.reshape(rows.shape[:-2] + (2, LINES, D))
        pads = [(0, 0)] * (rows.ndim - 2) + [(0, HALF - LINES), (0, 0)]
        return jnp.pad(rows, pads)

    def from_halves(halves):
        rows = halves[..., :LINES, :]
        return rows.reshape(rows.shape[:-3] + (UNIT, D))

    share = w_merge.shape[0]
    fshare = final_gain.shape[0]
    small = jnp.concatenate((merge_gain, merge_bias, final_gain, final_bias))
    small = jnp.pad(small, (0, 8 * D - small.shape[0])).reshape(8, D)
    packed = jnp.concatenate((w_merge, small)).astype(BF16)
    tall_rows = (w_fc2.shape[1], w_proj.shape[1], packed.size // own_width)
    tall = jnp.concatenate(
        (w_fc2[0].astype(BF16), w_proj[0].astype(BF16), packed.reshape(-1, own_width))
    )
    wide = jnp.concatenate(
        (w_qkv[0].astype(BF16).reshape(own_width, -1), w_fc1[0].astype(BF16)), 1
    )
    tall = lax.all_gather(tall, group_axes, axis=0)
    wide = lax.all_gather(wide, group_axes, axis=0)
    packed = tall[:, tall_rows[0] + tall_rows[1] :].reshape((-1,) + packed.shape)
    tall = tall.reshape((dp_count, tensor_count) + tall.shape[1:])
    wide = wide.reshape((dp_count, tensor_count) + wide.shape[1:])
    if (dp_count, tensor_count) != (OWN, BLOCKS):
        fc2_full = tall[:, :, : tall_rows[0]].transpose(1, 2, 0, 3)
        fc2_full = fc2_full.reshape(BLOCKS, FB, OWN, DB).transpose(2, 0, 1, 3)
        proj_full = tall[:, :, tall_rows[0] : tall_rows[0] + tall_rows[1]].transpose(1, 2, 0, 3)
        proj_full = proj_full.reshape(BLOCKS, TB, OWN, DB).transpose(2, 0, 1, 3)
        tall = jnp.concatenate((fc2_full, proj_full), 2)
        qkv_width = 3 * D // tensor_count
        qkv_full = wide[..., :qkv_width].reshape(dp_count, tensor_count, own_width, 3, -1)
        qkv_full = qkv_full.transpose(0, 2, 3, 1, 4).reshape(OWN, DB, 3, BLOCKS, TB)
        qkv_full = qkv_full.transpose(0, 3, 1, 2, 4).reshape(OWN, BLOCKS, DB, 3 * TB)
        fc1_full = wide[..., qkv_width:].transpose(0, 2, 1, 3)
        fc1_full = fc1_full.reshape(OWN, DB, BLOCKS, FB).transpose(0, 2, 1, 3)
        wide = jnp.concatenate((qkv_full, fc1_full), 3)
    weights = (tall, wide)

    parts = [packed]
    for step in range(1, section_count):
        pairs = [(source, (source + step) % section_count) for source in range(section_count)]
        parts.append(lax.ppermute(packed, "pipe", pairs))
    parts = parts[::-1]
    packed = lax.dynamic_slice_in_dim(
        jnp.concatenate(parts + parts[:-1]),
        (section_count - 1 - section_now) * packed.shape[0],
        section_count * packed.shape[0],
    )
    merge_weight = packed[:, :share].reshape(merge_in, D)
    small_all = packed[:, share]
    merge_scale = small_all[:, :share].reshape(-1).astype(F32)
    merge_shift = small_all[:, share : 2 * share].reshape(-1).astype(F32)
    final_scale = small_all[:, 2 * share : 2 * share + fshare].reshape(-1).astype(F32)
    final_shift = small_all[:, 2 * share + fshare : 2 * (share + fshare)].reshape(-1).astype(F32)

    heads_here = rel_table.shape[2]
    head_set = jnp.concatenate((qv_bias[0].reshape(-1), rel_table[0].reshape(-1)))
    head_set = gather_rows(head_set, "tensor")
    qv_all = head_set[:, : qv_bias.shape[1] * qv_bias.shape[2]].reshape(tensor_count, 2, -1)
    qv_all = qv_all.transpose(1, 0, 2).reshape(2, BLOCKS, TB)
    bias_qkv = jnp.stack((qv_all[0], jnp.zeros_like(qv_all[0]), qv_all[1]), 1).reshape(1, 3 * D)
    table_all = head_set[:, qv_bias.shape[1] * qv_bias.shape[2] :]
    table_all = table_all.reshape(tensor_count, 2 * WIN - 1, 2 * WIN - 1, heads_here)
    table_all = table_all.transpose(0, 3, 1, 2).reshape(D // HEAD, 2 * WIN - 1, 2 * WIN - 1)
    offsets = jnp.asarray(rel_parts(WIN))
    spread = jnp.einsum("huv,vy->huy", table_all, offsets, precision=lax.Precision.HIGHEST)
    spread = jnp.einsum("huy,ux->hxy", spread, offsets, precision=lax.Precision.HIGHEST)
    spread = spread.reshape(D // HEAD, WIN, WIN, WIN, WIN).transpose(0, 1, 3, 2, 4)
    spread = spread.reshape(D // HEAD, WIN * WIN, WIN * WIN)
    bias_pos = jnp.pad(spread, ((0, 0), (0, PAD - WIN * WIN), (0, 0)))
    bias_pos = jnp.pad(
        bias_pos, ((0, 0), (0, 0), (0, KEYS - WIN * WIN)), constant_values=-1e30
    ).reshape(GROUPS, STACK, KEYS)

    mask_all = np.zeros((WIN_ROWS, WIN_COLS, PAD, KEYS), np.float32)
    mask_all[:, :, : WIN * WIN, : WIN * WIN] = shift_mask(
        WIN * WIN_ROWS, GRID_W, WIN, SHIFT
    ).reshape(WIN_ROWS, WIN_COLS, WIN * WIN, WIN * WIN)
    mask_here = lax.dynamic_index_in_dim(jnp.asarray(mask_all, BF16), unit_now, 0, keepdims=False)
    mask_here = mask_here.astype(F32) * is_odd.astype(F32)
    orders = np.stack((window_order(0), window_order(SHIFT)))
    parity = section_now % 2
    perm_in = lax.dynamic_index_in_dim(jnp.asarray(orders, BF16), parity, 0, keepdims=False)
    perm_out = lax.dynamic_index_in_dim(
        jnp.asarray(orders.transpose(0, 2, 1), BF16), parity, 0, keepdims=False
    )
    vecs = jnp.concatenate(
        (ln_gain[0], ln_bias[0], out_bias[0], final_scale[None], final_shift[None])
    )
    forward_tables = (perm_in, perm_out, mask_here, vecs, bias_qkv, fc1_bias, bias_pos)
    backward_tables = (perm_in, perm_out, vecs)

    raw_rows = raw_pages.reshape(owned * rows_here, merge_in).astype(F32)
    raw_hat, raw_rstd = norm_stats(raw_rows)
    merged_in = (raw_hat * merge_scale + merge_shift).astype(BF16)
    merged = dot_nn(merged_in, merge_weight).astype(BF16).reshape(owned, rows_here, D)
    merged = to_halves(whole_unit(merged, 1))
    first_list = [merged]
    for section in range(1, section_count):
        first_list.append(lax.ppermute(merged, "pipe", [(section, 0)]))
    firsts = jnp.concatenate(first_list, 0)

    cots = to_halves(whole_unit(cotangent[0, :, 0], 1))
    cots_next = lax.ppermute(cots[:, 0], ("pipe", "tensor"), odd_pairs(-1))
    cots = jnp.where(is_odd, jnp.stack((cots[:, 1], cots_next), 1), cots)

    tick_count = micro_count + 2 * (section_count - 1)

    def flags_at(start, tick_now):
        slot_now = tick_now - 2 * start
        is_valid = (slot_now >= 0) & (slot_now < micro_count)
        slot = jnp.clip(slot_now, 0, micro_count - 1)
        return jnp.stack([flag.astype(jnp.int32) for flag in (is_valid, slot, is_first, is_last)])

    def stacks_of(*kinds):
        return pl.pallas_call(
            lambda *refs: None,
            out_shape=[jax.ShapeDtypeStruct(shape, dtype) for shape, dtype in kinds],
            out_specs=any_specs(len(kinds)),
        )()

    def of_micro(shape, dtype):
        return ((micro_count,) + shape, dtype)

    *stacks, empty_a, empty_b = stacks_of(
        of_micro((ROWS, D), BF16),
        of_micro((ROWS, 3 * D), BF16),
        of_micro((WIN_COLS * GROUPS, STACK, KEYS), BF16),
        of_micro((ROWS, D), BF16),
        of_micro((ROWS, D), F32),
        of_micro((ROWS, D), BF16),
        of_micro((ROWS, D), BF16),
        of_micro((ROWS, FF), BF16),
        of_micro((ROWS, FF), BF16),
        of_micro((ROWS, D), F32),
        of_micro((2, HALF, D), BF16),
        ((HALF, D), BF16),
        ((HALF, D), BF16),
    )
    recv = (empty_a, empty_b)
    for tick_now in range(tick_count):
        coming = recv
        if tick_now > 0:
            coming = hop(outgoing, range(section_count - 1), 1)
        outgoing, stacks = layer_forward(
            flags_at(section_now, tick_now), *recv, firsts, forward_tables, weights, stacks
        )
        recv = coming
    (
        x_all,
        qkv_all,
        probs_all,
        mixed_all,
        mid_all,
        rattn_all,
        rmlp_all,
        act_all,
        slope_all,
        out_all,
        hid_all,
    ) = stacks
    hid_before = lax.ppermute(hid_all[:, 1], ("pipe", "tensor"), odd_pairs(1))

    stacks = (
        x_all,
        qkv_all,
        slope_all,
        *stacks_of(
            of_micro((ROWS, D), BF16),
            of_micro((2, HALF, D), BF16),
            of_micro((SUMS, D), F32),
            ((GROUPS, STACK, KEYS), F32),
        ),
    )
    recv = (empty_a, empty_b)
    for tick_now in range(tick_count):
        coming = recv
        if tick_now > 0:
            coming = hop(outgoing, range(1, section_count), -1)
        flags = flags_at(section_count - 1 - section_now, tick_now)
        if tick_now == tick_count // 2:
            flags, hid_before = lax.optimization_barrier((flags, hid_before))
        outgoing, stacks = layer_backward(
            flags,
            *recv,
            cots,
            backward_tables,
            weights,
            (probs_all, mid_all, out_all),
            stacks,
        )
        recv = coming
    dba_all, dqkv_all, dpre_all, dbm_all, dx_all, sums_all, dpos = stacks
    shown = jnp.where(is_odd, jnp.stack((hid_before, hid_all[:, 0]), 1), hid_all)
    shown = own_part(from_halves(shown), 1)

    def weight_gradient(left, right):
        left = left.reshape(micro_count * ROWS, -1)
        right = right.reshape(micro_count * ROWS, D)

        def part(target):
            return dot_tn(
                left, lax.dynamic_slice_in_dim(right, target * own_width, own_width, 1)
            )

        total = None
        for step in range(1, dp_count):
            pairs = [(index, (index + step) % dp_count) for index in range(dp_count)]
            moved = lax.ppermute(
                part((dp_now + step) % dp_count).astype(BF16), "dp", pairs
            ).astype(F32)
            total = moved if total is None else total + moved
        mine = part(dp_now)
        total = mine if total is None else mine + total
        return total / copies

    def over_tensor(total):
        return lax.psum_scatter(total.astype(BF16), "tensor", scatter_dimension=0, tiled=True)

    g_proj = weight_gradient(mixed_all, dba_all).astype(BF16)
    g_proj, act_all, dbm_all, dpre_all, rmlp_all, dqkv_all, rattn_all = lax.optimization_barrier(
        (g_proj, act_all, dbm_all, dpre_all, rmlp_all, dqkv_all, rattn_all)
    )
    g_proj = over_tensor(g_proj).astype(F32)
    g_fc2 = over_tensor(weight_gradient(act_all, dbm_all)).astype(F32)
    g_fc1 = over_tensor(weight_gradient(dpre_all, rmlp_all)).astype(F32).T
    g_qkv = weight_gradient(dqkv_all, rattn_all)
    if copies > 1:
        g_qkv = g_qkv.reshape(BLOCKS, 3, copies, TB // copies, own_width)
        g_qkv = g_qkv.transpose(0, 2, 1, 3, 4).reshape(3 * D, own_width)
    g_qkv = over_tensor(g_qkv).astype(F32).T.reshape(own_width, 3, D // tensor_count)

    own_grads = dx_all[:owned]
    for section in range(1, section_count):
        moved = lax.ppermute(
            dx_all[section * owned : (section + 1) * owned], "pipe", [(0, section)]
        )
        own_grads = jnp.where(section_now == section, moved, own_grads)
    grad_merged = own_part(from_halves(own_grads), 1).reshape(owned * rows_here, D)
    g_merge = dot_tn(merged_in, grad_merged)
    g_merge = g_merge.reshape(section_count, dp_count, tensor_count, share, D)
    g_merge = shares_summed(g_merge.transpose(1, 0, 2, 3, 4).astype(BF16), "dp")[0]
    g_merge = shares_summed(g_merge.astype(BF16), "pipe")[0]
    g_merge = shares_summed(g_merge.astype(BF16), "tensor")[0]
    grad_unit = dot_nt(grad_merged, merge_weight)
    merge_sums = jnp.stack((jnp.sum(grad_unit * raw_hat, 0), jnp.sum(grad_unit, 0)))
    grad_raw = norm_back(raw_hat, raw_rstd, grad_unit * merge_scale)
    grad_raw = grad_raw.reshape(raw_pages.shape).astype(BF16)

    sums = jnp.sum(sums_all, 0) / copies
    dpos = dpos.reshape(D // HEAD, PAD, KEYS)[:, : WIN * WIN, : WIN * WIN]
    dpos = dpos.reshape(D // HEAD, WIN, WIN, WIN, WIN).transpose(0, 1, 3, 2, 4)
    dpos = dpos.reshape(D // HEAD, WIN * WIN, WIN * WIN) / copies
    dtable = jnp.einsum("hxy,vy->hxv", dpos, offsets, precision=lax.Precision.HIGHEST)
    dtable = jnp.einsum("hxv,ux->huv", dtable, offsets, precision=lax.Precision.HIGHEST)
    final_sums = sums[6:8] * is_last.astype(F32)
    every = jnp.concatenate((merge_sums.reshape(-1), final_sums.reshape(-1)))
    vector = jnp.concatenate((every, sums.reshape(-1), dtable.reshape(-1)))
    size = vector.shape[0]
    vector = jnp.pad(vector, (0, -size % D)).reshape(-1, 128)
    for axis in group_axes:
        vector = summed(vector, axis)
    edge_rows = every.shape[0] // 128
    edge = summed(vector[:edge_rows], "pipe").reshape(-1)
    local_sums = vector[edge_rows:].reshape(-1)
    sums = local_sums[: SUMS * D].reshape(SUMS, D)
    dtable = local_sums[SUMS * D : SUMS * D + dtable.size].reshape(tensor_count, heads_here, -1)
    g_table = lax.dynamic_index_in_dim(dtable, tensor_now, 0, keepdims=False).T
    dqv = sums[12:15].reshape(BLOCKS, 3, TB)[:, 0::2].transpose(1, 0, 2).reshape(2, D)
    g_qv = lax.dynamic_slice_in_dim(
        dqv, tensor_now * (D // tensor_count), D // tensor_count, 1
    )
    place = (section_now * dp_count + dp_now) * tensor_count + tensor_now
    edge_parts = []
    start = 0
    for size, width in ((merge_in, share), (merge_in, share), (D, fshare), (D, fshare)):
        edge_parts.append(lax.dynamic_slice_in_dim(edge, start + place * width, width))
        start += size
    return (
        shown[None, :, None],
        grad_raw,
        g_merge,
        *edge_parts,
        g_qkv[None],
        g_proj[None],
        g_fc1[None],
        g_fc2[None],
        g_qv[None],
        sums[8:12].reshape(1, FF),
        g_table[None],
        sums[0:2][None],
        sums[2:4][None],
        sums[4:6][None],
    )


def solution(mesh):
    return jax.shard_map(
        on_device,
        mesh=mesh,
        in_specs=(
            P("pipe", "dp", "tensor", None),
            P(("pipe", "dp", "tensor"), None),
            P(("pipe", "dp", "tensor")),
            P(("pipe", "dp", "tensor")),
            P(("pipe", "dp", "tensor")),
            P(("pipe", "dp", "tensor")),
            P("pipe", "dp", None, "tensor"),
            P("pipe", "tensor", "dp"),
            P("pipe", "dp", "tensor"),
            P("pipe", "tensor", "dp"),
            P("pipe", None, "tensor"),
            P("pipe", None),
            P("pipe", None, "tensor"),
            P("pipe", None, None),
            P("pipe", None, None),
            P("pipe", None, None),
            P("pipe", None, "dp", "tensor", None),
        ),
        out_specs=(
            P("pipe", None, "dp", "tensor", None),
            P("pipe", "dp", "tensor", None),
            P(("pipe", "dp", "tensor"), None),
            P(("pipe", "dp", "tensor")),
            P(("pipe", "dp", "tensor")),
            P(("pipe", "dp", "tensor")),
            P(("pipe", "dp", "tensor")),
            P("pipe", "dp", None, "tensor"),
            P("pipe", "tensor", "dp"),
            P("pipe", "dp", "tensor"),
            P("pipe", "tensor", "dp"),
            P("pipe", None, "tensor"),
            P("pipe", None),
            P("pipe", None, "tensor"),
            P("pipe", None, None),
            P("pipe", None, None),
            P("pipe", None, None),
        ),
        check_vma=False,
    )
```

```python
import functools

import jax
import jax.numpy as jnp
import numpy as np
from jax import lax
from jax.experimental import pallas as pl
from jax.experimental.pallas import tpu as pltpu
from jax.sharding import PartitionSpec as P

D = 1024
HEAD = 32
FF = 4096
WIN = 10
SHIFT = 5
WIN_ROWS = 4
WIN_COLS = 3
NORM_EPS = 1e-05

GRID_W = WIN * WIN_COLS
UNIT = WIN * GRID_W
LINES = SHIFT * GRID_W
HALF = 160
PAD = 112
KEYS = 128
ROWS = WIN_COLS * PAD
PER = 128 // HEAD
GROUPS = D // 128
STACK = PER * PAD
QKV_AT, PROJ_AT, FC1_AT, FC2_AT, BLOCK_ROWS = 0, 768, 1024, 2048, 3072
OWN = 2
BLOCKS = 4
DB = D // OWN
TB = D // BLOCKS
FB = FF // BLOCKS
STEP = PAD
SUMS = 16
VMEM_BYTES = 60 * 1024 * 1024

F32 = jnp.float32
BF16 = jnp.bfloat16


def rel_parts(window):
    offsets = np.arange(window)[:, None] - np.arange(window)[None, :] + window - 1
    return (offsets.reshape(-1)[None, :] == np.arange(2 * window - 1)[:, None]).astype(np.float32)


def shift_mask(grid_rows, grid_cols, window, shift_now):
    region = np.zeros((grid_rows, grid_cols), np.int64)
    region_id = 0
    for span_rows in (
        (0, grid_rows - window),
        (grid_rows - window, grid_rows - shift_now),
        (grid_rows - shift_now, grid_rows),
    ):
        for span_cols in (
            (0, grid_cols - window),
            (grid_cols - window, grid_cols - shift_now),
            (grid_cols - shift_now, grid_cols),
        ):
            region[span_rows[0] : span_rows[1], span_cols[0] : span_cols[1]] = region_id
            region_id += 1
    blocks = region.reshape(grid_rows // window, window, grid_cols // window, window).transpose(
        0, 2, 1, 3
    )
    blocks = blocks.reshape(-1, window * window)
    return np.where(blocks[:, :, None] == blocks[:, None, :], 0.0, -100.0).astype(np.float32)


def window_order(shift_now):
    order = np.zeros((ROWS, 2 * HALF), np.float32)
    for win in range(WIN_COLS):
        for row in range(WIN):
            for col in range(WIN):
                source_col = (win * WIN + col + shift_now) % GRID_W
                source = (row // SHIFT) * HALF + (row % SHIFT) * GRID_W + source_col
                order[win * PAD + row * WIN + col, source] = 1.0
    return order


def norm_stats(values):
    row_mean = jnp.mean(values, -1, keepdims=True)
    centred = values - row_mean
    rstd_rows = lax.rsqrt(jnp.mean(centred * centred, -1, keepdims=True) + NORM_EPS)
    return (centred * rstd_rows, rstd_rows)


def norm_back(normed, rstd_rows, grad_normed):
    return rstd_rows * (
        grad_normed
        - jnp.mean(grad_normed, -1, keepdims=True)
        - normed * jnp.mean(grad_normed * normed, -1, keepdims=True)
    )


def dot_nn(left, right):
    return lax.dot_general(left, right, (((1,), (0,)), ((), ())), preferred_element_type=F32)


def dot_nt(left, right):
    return lax.dot_general(left, right, (((1,), (1,)), ((), ())), preferred_element_type=F32)


def dot_tn(left, right):
    return lax.dot_general(left, right, (((0,), (0,)), ((), ())), preferred_element_type=F32)


def row_chunks(body, carry=None):
    def step(index, state):
        return body(pl.ds(pl.multiple_of(index * STEP, STEP), STEP), state)

    return lax.fori_loop(0, ROWS // STEP, step, carry)


def fold8(values):
    return jnp.sum(values.reshape(values.shape[0] // 8, 8, values.shape[1]), 0)


def head_masks():
    lane_head = lax.broadcasted_iota(jnp.int32, (1, 128), 1) // HEAD
    return [(lane_head == head).astype(F32) for head in range(PER)]


def spread_heads(tile, masks):
    return jnp.concatenate([(tile * mask.astype(BF16)) for mask in masks], 0)


def pick_heads(stacked, masks):
    total = stacked[:PAD] * masks[0]
    for head in range(1, PER):
        total = total + stacked[head * PAD : (head + 1) * PAD] * masks[head]
    return total


def group_columns(group):
    return (group // 2) * (3 * TB) + (group % 2) * 128


class Copies:
    def __init__(self, copies):
        self.copies = copies

    def start(self):
        for copy in self.copies:
            copy.start()

    def wait(self):
        for copy in self.copies:
            copy.wait()


def weight_copies(w_all, targets, sems, block):
    v_qkv, v_proj, v_fc1, v_fc2 = targets
    half = DB // 2
    moves = {
        "qkv": (
            (v_qkv, (0, DB), (0, DB), 0, 0),
            (v_qkv, (0, half), (DB, half), QKV_AT + DB, 0),
            (v_qkv, (half, half), (DB, half), QKV_AT + DB, half),
        ),
        "proj": ((v_proj, (0, TB), (0, DB), PROJ_AT, 0),),
        "fc1": ((v_fc1, (0, DB), (0, DB), FC1_AT, 0), (v_fc1, (0, DB), (DB, DB), FC1_AT + DB, 0)),
        "fc2": ((v_fc2, (0, FB), (0, DB), FC2_AT, 0),),
    }
    starts = {"qkv": 0, "proj": 3, "fc1": 4, "fc2": 6}

    def copies(kind):
        result = []
        for index, (target, rows, columns, row, column) in enumerate(moves[kind]):
            result.append(
                pltpu.make_async_copy(
                    w_all.at[:, block, pl.ds(row, rows[1]), pl.ds(column, columns[1])],
                    target.at[:, block, pl.ds(*rows), pl.ds(*columns)],
                    sems.at[(starts[kind] + index) * BLOCKS + block],
                )
            )
        return Copies(result)

    return copies


def lanes(start, size):
    return pl.ds(pl.multiple_of(start, 128), size)


def forward_kernel(
    flags,
    recv_a,
    recv_b,
    firsts,
    perm_in,
    perm_out,
    mask,
    vecs,
    bias_qkv,
    bias_fc1,
    bias_pos,
    w_all,
    *refs,
):
    (x_all, qkv_all, probs_all, mixed_all, mid_all, rattn_all, rmlp_all, act_all, slope_all) = refs[11:20]
    out_all, hid_all = refs[20:22]
    sends = refs[22:24]
    (
        v_qkv,
        v_proj,
        v_fc1,
        v_fc2,
        v_pos,
        rin,
        xf,
        xb,
        rattn,
        qkv,
        probs,
        mixed,
        mid,
        rmlp,
        act,
        slope,
        total,
        final,
        outb,
        outs,
        sem_w,
        sem_in,
        sem_out,
        sem_h,
    ) = refs[24:]
    valid = flags[0]
    slot = flags[1]
    is_first = flags[2]
    is_last = flags[3]

    @pl.when(valid == 1)
    def _():
        targets = (v_qkv, v_proj, v_fc1, v_fc2)

        def w_copy(kind, block):
            return weight_copies(w_all, targets, sem_w, block)(("qkv", "fc1", "fc2")[kind])

        def proj_copy():
            return Copies(
                [weight_copies(w_all, targets, sem_w, block)("proj").copies[0] for block in range(BLOCKS)]
            )

        def pos_copy():
            return pltpu.make_async_copy(bias_pos, v_pos, sem_w.at[7 * BLOCKS])

        @pl.when(is_first == 1)
        def _():
            pltpu.make_async_copy(
                firsts.at[slot, 0], rin.at[pl.ds(0, HALF)], sem_in.at[0]
            ).start()
            pltpu.make_async_copy(
                firsts.at[slot, 1], rin.at[pl.ds(HALF, HALF)], sem_in.at[1]
            ).start()

        @pl.when(is_first == 0)
        def _():
            pltpu.make_async_copy(recv_a, rin.at[pl.ds(0, HALF)], sem_in.at[0]).start()
            pltpu.make_async_copy(recv_b, rin.at[pl.ds(HALF, HALF)], sem_in.at[1]).start()

        for block in range(BLOCKS):
            w_copy(0, block).start()
        pltpu.make_async_copy(recv_a, rin.at[pl.ds(0, HALF)], sem_in.at[0]).wait()
        pltpu.make_async_copy(recv_b, rin.at[pl.ds(HALF, HALF)], sem_in.at[1]).wait()

        xf[...] = dot_nn(perm_in[...], rin[...])

        def first_norm(rows, state):
            values = xf[rows, :]
            hat, _ = norm_stats(values)
            rattn[rows, :] = (hat * vecs[0:1, :] + vecs[2:3, :]).astype(BF16)
            xb[rows, :] = values.astype(BF16)
            return state

        row_chunks(first_norm)
        saves = [
            pltpu.make_async_copy(rattn, rattn_all.at[slot], sem_out.at[0]),
            pltpu.make_async_copy(xb, x_all.at[slot], sem_out.at[1]),
        ]
        saves[0].start()
        saves[1].start()
        qkv[pl.ds(ROWS, 16), :] = jnp.zeros((16, 3 * D), BF16)

        pos_copy().start()
        proj_copy().start()

        def qkv_block(block, state):
            w_copy(0, block).wait()
            w_copy(1, block).start()
            out = dot_nn(rattn[...], v_qkv[:, block].reshape(D, 3 * TB))
            columns = lanes(block * 3 * TB, 3 * TB)
            qkv[pl.ds(0, ROWS), columns] = (out + bias_qkv[:, columns]).astype(BF16)
            return state

        lax.fori_loop(0, BLOCKS, qkv_block, None)
        save_qkv = pltpu.make_async_copy(
            qkv.at[pl.ds(0, ROWS)], qkv_all.at[slot], sem_out.at[2]
        )
        save_qkv.start()
        for block in range(BLOCKS):
            w_copy(2, block).start()
        pos_copy().wait()
        masks = head_masks()

        def attend(win, group):
            base = pl.multiple_of(win * PAD, 16)
            column = group_columns(group)
            query = qkv[pl.ds(base, PAD), lanes(column, 128)]
            key = qkv[pl.ds(base, KEYS), lanes(column + TB, 128)]
            value = qkv[pl.ds(base, KEYS), lanes(column + 2 * TB, 128)]
            scores = dot_nt(spread_heads(query, masks), key)
            scores = scores * HEAD**-0.5 + v_pos[group]
            scores = scores + jnp.concatenate([mask[win]] * PER, 0)
            top = jnp.max(scores, -1, keepdims=True)
            powers = jnp.exp(scores - top)
            low = (powers * (1.0 / jnp.sum(powers, -1, keepdims=True))).astype(BF16)
            probs[win * GROUPS + group] = low
            mixed[pl.ds(base, PAD), lanes(group * 128, 128)] = pick_heads(
                dot_nn(low, value), masks
            ).astype(BF16)

        def attend_window(win, state):
            for group in range(GROUPS):
                attend(win, group)
            return state

        lax.fori_loop(0, WIN_COLS, attend_window, None)
        saves.append(pltpu.make_async_copy(probs, probs_all.at[slot], sem_out.at[3]))
        saves[-1].start()
        saves.append(pltpu.make_async_copy(mixed, mixed_all.at[slot], sem_out.at[4]))
        saves[-1].start()
        proj_copy().wait()
        for own in range(OWN):
            columns = slice(own * DB, (own + 1) * DB)
            out = dot_nn(mixed[...], v_proj[own].reshape(D, DB))
            mid[:, columns] = xf[:, columns] + vecs[4:5, columns] + out
        saves.append(pltpu.make_async_copy(mid, mid_all.at[slot], sem_out.at[5]))
        saves[-1].start()

        def second_norm(rows, state):
            hat, _ = norm_stats(mid[rows, :])
            rmlp[rows, :] = (hat * vecs[1:2, :] + vecs[3:4, :]).astype(BF16)
            total[rows, :] = mid[rows, :] + vecs[5:6, :]
            return state

        row_chunks(second_norm)
        saves.append(pltpu.make_async_copy(rmlp, rmlp_all.at[slot], sem_out.at[6]))
        saves[-1].start()

        def hidden_saves(block):
            columns = lanes(block * FB, FB)
            return [
                pltpu.make_async_copy(
                    source.at[:, columns], target.at[slot, :, columns], sem_h.at[kind * BLOCKS + block]
                )
                for kind, (source, target) in enumerate(((act, act_all), (slope, slope_all)))
            ]

        def hidden_block(block, state):
            w_copy(1, block).wait()
            columns = lanes(block * FB, FB)
            pre = dot_nn(rmlp[...], v_fc1[:, block].reshape(D, FB))
            pre = pre + bias_fc1[:, columns]
            chance = 0.5 + 0.5 * lax.erf(pre * np.float32(0.5**0.5))
            slope[:, columns] = (
                chance + pre * (np.float32((2 * np.pi) ** -0.5) * jnp.exp(-0.5 * pre * pre))
            ).astype(BF16)
            act[:, columns] = (pre * chance).astype(BF16)
            for save in hidden_saves(block):
                save.start()
            return state

        lax.fori_loop(0, BLOCKS, hidden_block, None)
        for block in range(BLOCKS):
            w_copy(2, block).wait()
        for own in range(OWN):
            half = slice(own * DB, (own + 1) * DB)
            total[:, half] += dot_nn(act[...], v_fc2[own].reshape(FF, DB))

        def finish(rows, state):
            hat, _ = norm_stats(total[rows, :])
            outb[rows, :] = (hat * vecs[6:7, :] + vecs[7:8, :]).astype(BF16)
            return state

        @pl.when(is_last == 1)
        def _():
            row_chunks(finish)

        @pl.when(is_last == 0)
        def _():
            outb[...] = total[...].astype(BF16)

        save_out = pltpu.make_async_copy(total, out_all.at[slot], sem_out.at[9])

        @pl.when(is_last == 1)
        def _():
            save_out.start()

        outs[...] = dot_nn(perm_out[...], outb[...]).astype(BF16)
        for half in range(2):
            rows = pl.ds(half * HALF, HALF)
            saves.append(
                pltpu.make_async_copy(outs.at[rows], sends[half], sem_out.at[10 + half])
            )
            saves[-1].start()
            saves.append(
                pltpu.make_async_copy(outs.at[rows], hid_all.at[slot, half], sem_out.at[12 + half])
            )
            saves[-1].start()
        save_qkv.wait()
        for block in range(BLOCKS):
            saves.extend(hidden_saves(block))
        for save in saves:
            save.wait()

        @pl.when(is_last == 1)
        def _():
            save_out.wait()


def backward_kernel(
    flags,
    recv_a,
    recv_b,
    cots,
    cots_next,
    perm_in,
    perm_out,
    vecs,
    w_all,
    probs_all,
    mid_all,
    out_all,
    *refs,
):
    x_all, qkv_all, slope_all, dbm_all, dx_all, sums_all, dpos_all = refs[7:14]
    sends = refs[14:16]
    (
        v_qkv,
        v_proj,
        v_fc1,
        v_fc2,
        rin,
        rcot,
        xb,
        qkv,
        probs,
        mid,
        last,
        slope,
        grad,
        back,
        dbm,
        dba,
        dmix,
        dqkv,
        dpos,
        sums,
        outs,
        sem_w,
        sem_in,
        sem_out,
        sem_h,
    ) = refs[16:]
    valid = flags[0]
    slot = flags[1]
    is_last = flags[3]

    @pl.when(valid == 1)
    def _():
        targets = (v_qkv, v_proj, v_fc1, v_fc2)

        def w_copy(kind, block):
            return weight_copies(w_all, targets, sem_w, block)(("fc2", "fc1", "qkv")[kind])

        def proj_copy():
            return Copies(
                [weight_copies(w_all, targets, sem_w, block)("proj").copies[0] for block in range(BLOCKS)]
            )

        def load(index):
            source, target = (
                (cots.at[slot, 0], rcot.at[pl.ds(0, HALF)]),
                (cots.at[slot, 1], rcot.at[pl.ds(HALF, HALF)]),
                (recv_a, rin.at[pl.ds(0, HALF)]),
                (recv_b, rin.at[pl.ds(HALF, HALF)]),
                (out_all.at[slot], last),
                (slope_all.at[slot], slope),
                (mid_all.at[slot], mid),
                (qkv_all.at[slot], qkv.at[pl.ds(0, ROWS)]),
                (probs_all.at[slot], probs),
                (x_all.at[slot], xb),
                (dpos_all, dpos),
            )[index]
            return pltpu.make_async_copy(source, target, sem_in.at[index])

        @pl.when(flags[4] == 0)
        def _():
            load(0).start()
            load(1).start()

        @pl.when(flags[4] == 1)
        def _():
            for half, source in enumerate((cots.at[slot, 1], cots_next.at[slot])):
                pltpu.make_async_copy(
                    source, rcot.at[pl.ds(half * HALF, HALF)], sem_in.at[half]
                ).start()

        load(2).start()
        load(3).start()

        @pl.when(is_last == 1)
        def _():
            load(4).start()

        w_copy(0, 0).start()
        load(5).start()
        w_copy(1, 0).start()
        for index in range(4):
            load(index).wait()
        sums[...] = jnp.zeros_like(sums)
        grad[...] = dot_nn(perm_in[...], rcot[...])

        @pl.when(is_last == 1)
        def _():
            load(4).wait()

            def final_norm(rows, state):
                cot = grad[rows, :]
                hat, rstd = norm_stats(last[rows, :])
                grad[rows, :] = norm_back(hat, rstd, cot * vecs[6:7, :])
                return (state[0] + fold8(cot * hat), state[1] + fold8(cot))

            zero = jnp.zeros((8, D), F32)
            gain, shift = row_chunks(final_norm, (zero, zero))
            sums[6:7, :] = jnp.sum(gain, 0, keepdims=True)
            sums[7:8, :] = jnp.sum(shift, 0, keepdims=True)

        @pl.when(is_last == 0)
        def _():
            grad[...] += dot_nn(perm_in[...], rin[...])

        def enter(rows, state):
            values = grad[rows, :]
            dbm[rows, :] = values.astype(BF16)
            back[rows, :] = jnp.zeros((STEP, D), F32)
            return state + fold8(values)

        out_sum = row_chunks(enter, jnp.zeros((8, D), F32))
        sums[5:6, :] = jnp.sum(out_sum, 0, keepdims=True)
        saves = [pltpu.make_async_copy(dbm, dbm_all.at[slot], sem_out.at[0])]
        saves[0].start()
        load(5).wait()

        def hidden_save(block):
            columns = lanes(block * FB, FB)
            return pltpu.make_async_copy(
                slope.at[:, columns], slope_all.at[slot, :, columns], sem_h.at[block]
            )

        def hidden_block(block, state):
            columns = lanes(block * FB, FB)
            w_copy(0, block).wait()

            @pl.when(block < BLOCKS - 1)
            def _():
                w_copy(0, block + 1).start()
                w_copy(1, block + 1).start()

            @pl.when(block == BLOCKS - 1)
            def _():
                load(6).start()
                proj_copy().start()
                load(7).start()
                load(8).start()

            dact = dot_nt(dbm[:, :DB], v_fc2[0, block]) + dot_nt(dbm[:, DB:], v_fc2[1, block])
            dpre = (dact * slope[:, columns].astype(F32)).astype(BF16)
            slope[:, columns] = dpre
            hidden_save(block).start()
            sums[pl.ds(8 + block, 1), :] = jnp.sum(dpre.astype(F32), 0, keepdims=True)
            w_copy(1, block).wait()
            for own in range(OWN):
                half = slice(own * DB, (own + 1) * DB)
                back[:, half] += dot_nt(slope[:, columns], v_fc1[own, block])
            return state

        lax.fori_loop(0, BLOCKS, hidden_block, None)
        for block in range(BLOCKS):
            w_copy(2, block).start()
        load(9).start()

        @pl.when(slot > 0)
        def _():
            load(10).start()

        load(6).wait()

        def mlp_norm(rows, state):
            hat, rstd = norm_stats(mid[rows, :])
            ready = back[rows, :]
            values = grad[rows, :] + norm_back(hat, rstd, ready * vecs[1:2, :])
            grad[rows, :] = values
            dba[rows, :] = values.astype(BF16)
            back[rows, :] = jnp.zeros((STEP, D), F32)
            return (state[0] + fold8(ready * hat), state[1] + fold8(ready), state[2] + fold8(values))

        zero = jnp.zeros((8, D), F32)
        gain, shift, out_sum = row_chunks(mlp_norm, (zero, zero, zero))
        sums[1:2, :] = jnp.sum(gain, 0, keepdims=True)
        sums[3:4, :] = jnp.sum(shift, 0, keepdims=True)
        sums[4:5, :] = jnp.sum(out_sum, 0, keepdims=True)
        load(9).wait()
        saves.append(pltpu.make_async_copy(dba, x_all.at[slot], sem_out.at[2]))
        saves[-1].start()
        proj_copy().wait()
        for block in range(BLOCKS):
            out = dot_nt(dba[:, :DB], v_proj[0, block]) + dot_nt(dba[:, DB:], v_proj[1, block])
            dmix[:, block * TB : (block + 1) * TB] = out.astype(BF16)
        load(7).wait()
        load(8).wait()

        @pl.when(slot > 0)
        def _():
            load(10).wait()

        @pl.when(slot == 0)
        def _():
            dpos[...] = jnp.zeros_like(dpos)

        qkv[pl.ds(ROWS, 16), :] = jnp.zeros((16, 3 * D), BF16)
        masks = head_masks()

        def attend_back(group, state):
            column = group_columns(group)
            for win in range(WIN_COLS):
                base = win * PAD
                query = qkv[pl.ds(base, PAD), lanes(column, 128)]
                key = qkv[pl.ds(base, KEYS), lanes(column + TB, 128)]
                value = qkv[pl.ds(base, KEYS), lanes(column + 2 * TB, 128)]
                low = probs[win * GROUPS + group]
                dout = spread_heads(dmix[pl.ds(base, PAD), lanes(group * 128, 128)], masks)
                dprob = dot_nt(dout, value)
                weight = low.astype(F32)
                dscore = weight * (dprob - jnp.sum(dprob * weight, -1, keepdims=True))
                dscore = dscore.astype(BF16)
                dpos[group] += dscore.astype(F32)
                dquery = pick_heads(dot_nn(dscore, key), masks) * HEAD**-0.5
                dkey = dot_tn(dscore, spread_heads(query, masks)) * HEAD**-0.5
                dvalue = dot_tn(low, dout)
                dqkv[pl.ds(base, PAD), lanes(column, 128)] = dquery.astype(BF16)
                dqkv[pl.ds(base, PAD), lanes(column + TB, 128)] = dkey[:PAD].astype(BF16)
                dqkv[pl.ds(base, PAD), lanes(column + 2 * TB, 128)] = dvalue[:PAD].astype(BF16)
            return state

        def attend_back_pair(pair, state):
            return attend_back(2 * pair + 1, attend_back(2 * pair, state))

        lax.fori_loop(0, GROUPS // 2, attend_back_pair, None)
        saves.append(pltpu.make_async_copy(dqkv, qkv_all.at[slot], sem_out.at[3]))
        saves[-1].start()
        saves.append(pltpu.make_async_copy(dpos, dpos_all, sem_out.at[4]))
        saves[-1].start()

        def ready_block(block, state):
            columns = lanes(block * 3 * TB, 3 * TB)
            w_copy(2, block).wait()
            for own in range(OWN):
                half = slice(own * DB, (own + 1) * DB)
                back[:, half] += dot_nt(dqkv[:, columns], v_qkv[own, block])
            return state

        lax.fori_loop(0, BLOCKS, ready_block, None)
        for part in range(3):
            columns = slice(part * D, (part + 1) * D)
            sums[12 + part : 13 + part, :] = jnp.sum(dqkv[:, columns].astype(F32), 0, keepdims=True)

        def attn_norm(rows, state):
            hat, rstd = norm_stats(xb[rows, :].astype(F32))
            ready = back[rows, :]
            values = grad[rows, :] + norm_back(hat, rstd, ready * vecs[0:1, :])
            xb[rows, :] = values.astype(BF16)
            return (state[0] + fold8(ready * hat), state[1] + fold8(ready))

        gain, shift = row_chunks(attn_norm, (zero, zero))
        sums[0:1, :] = jnp.sum(gain, 0, keepdims=True)
        sums[2:3, :] = jnp.sum(shift, 0, keepdims=True)
        saves.append(pltpu.make_async_copy(sums, sums_all.at[slot], sem_out.at[5]))
        saves[-1].start()
        outs[...] = dot_nn(perm_out[...], xb[...]).astype(BF16)
        for half in range(2):
            rows = pl.ds(half * HALF, HALF)
            saves.append(
                pltpu.make_async_copy(outs.at[rows], sends[half], sem_out.at[6 + half])
            )
            saves[-1].start()
            saves.append(
                pltpu.make_async_copy(outs.at[rows], dx_all.at[slot, half], sem_out.at[8 + half])
            )
            saves[-1].start()
        for block in range(BLOCKS):
            saves.append(hidden_save(block))
        for save in saves:
            save.wait()


def any_specs(count):
    return [pl.BlockSpec(memory_space=pl.ANY)] * count


def vmem_specs(count):
    return [pl.BlockSpec(memory_space=pltpu.VMEM)] * count


def shapes_of(arrays):
    return [jax.ShapeDtypeStruct(array.shape, array.dtype) for array in arrays]


WEIGHT_SCRATCH = [
    pltpu.VMEM((OWN, BLOCKS, DB, 3 * TB), BF16),
    pltpu.VMEM((OWN, BLOCKS, TB, DB), BF16),
    pltpu.VMEM((OWN, BLOCKS, DB, FB), BF16),
    pltpu.VMEM((OWN, BLOCKS, FB, DB), BF16),
]


def layer_forward(flags, recv_a, recv_b, firsts, tables, weights, stacks):
    inputs = (flags, recv_a, recv_b, firsts) + tuple(tables) + (weights,) + tuple(stacks)
    first_stack = len(inputs) - len(stacks)
    wide = lambda dtype: pltpu.VMEM((ROWS, D), dtype)
    results = pl.pallas_call(
        forward_kernel,
        out_shape=shapes_of(stacks) + [jax.ShapeDtypeStruct((HALF, D), BF16)] * 2,
        in_specs=[pl.BlockSpec(memory_space=pltpu.SMEM)]
        + any_specs(3)
        + vmem_specs(6)
        + any_specs(2 + len(stacks)),
        out_specs=any_specs(len(stacks) + 2),
        scratch_shapes=WEIGHT_SCRATCH
        + [
            pltpu.VMEM((GROUPS, STACK, KEYS), F32),
            pltpu.VMEM((2 * HALF, D), BF16),
            wide(F32),
            wide(BF16),
            wide(BF16),
            pltpu.VMEM((ROWS + 16, 3 * D), BF16),
            pltpu.VMEM((WIN_COLS * GROUPS, STACK, KEYS), BF16),
            wide(BF16),
            wide(F32),
            wide(BF16),
            pltpu.VMEM((ROWS, FF), BF16),
            pltpu.VMEM((ROWS, FF), BF16),
            wide(F32),
            wide(F32),
            wide(BF16),
            pltpu.VMEM((2 * HALF, D), BF16),
            pltpu.SemaphoreType.DMA((7 * BLOCKS + 1,)),
            pltpu.SemaphoreType.DMA((2,)),
            pltpu.SemaphoreType.DMA((14,)),
            pltpu.SemaphoreType.DMA((2 * BLOCKS,)),
        ],
        input_output_aliases={first_stack + index: index for index in range(len(stacks))},
        compiler_params=pltpu.CompilerParams(vmem_limit_bytes=VMEM_BYTES),
        cost_estimate=pl.CostEstimate(
            flops=24 * ROWS * D * D, bytes_accessed=40 * 1024 * 1024, transcendentals=ROWS * FF
        ),
        name="layer_forward",
    )(*inputs)
    return results[-2:], tuple(results[:-2])


def layer_backward(flags, recv_a, recv_b, cots, cots_next, tables, weights, saved, stacks):
    inputs = (
        (flags, recv_a, recv_b, cots, cots_next)
        + tuple(tables)
        + (weights,)
        + tuple(saved)
        + tuple(stacks)
    )
    first_stack = len(inputs) - len(stacks)
    wide = lambda dtype: pltpu.VMEM((ROWS, D), dtype)
    results = pl.pallas_call(
        backward_kernel,
        out_shape=shapes_of(stacks) + [jax.ShapeDtypeStruct((HALF, D), BF16)] * 2,
        in_specs=[pl.BlockSpec(memory_space=pltpu.SMEM)]
        + any_specs(4)
        + vmem_specs(3)
        + any_specs(1 + len(saved) + len(stacks)),
        out_specs=any_specs(len(stacks) + 2),
        scratch_shapes=WEIGHT_SCRATCH
        + [
            pltpu.VMEM((2 * HALF, D), BF16),
            pltpu.VMEM((2 * HALF, D), BF16),
            wide(BF16),
            pltpu.VMEM((ROWS + 16, 3 * D), BF16),
            pltpu.VMEM((WIN_COLS * GROUPS, STACK, KEYS), BF16),
            wide(F32),
            wide(F32),
            pltpu.VMEM((ROWS, FF), BF16),
            wide(F32),
            wide(F32),
            wide(BF16),
            wide(BF16),
            wide(BF16),
            pltpu.VMEM((ROWS, 3 * D), BF16),
            pltpu.VMEM((GROUPS, STACK, KEYS), F32),
            pltpu.VMEM((SUMS, D), F32),
            pltpu.VMEM((2 * HALF, D), BF16),
            pltpu.SemaphoreType.DMA((7 * BLOCKS,)),
            pltpu.SemaphoreType.DMA((11,)),
            pltpu.SemaphoreType.DMA((10,)),
            pltpu.SemaphoreType.DMA((BLOCKS,)),
        ],
        input_output_aliases={first_stack + index: index for index in range(len(stacks))},
        compiler_params=pltpu.CompilerParams(vmem_limit_bytes=VMEM_BYTES),
        cost_estimate=pl.CostEstimate(
            flops=24 * ROWS * D * D, bytes_accessed=50 * 1024 * 1024, transcendentals=0
        ),
        name="layer_backward",
    )(*inputs)
    return results[-2:], tuple(results[:-2])


def on_device(
    raw_pages,
    w_merge,
    merge_gain,
    merge_bias,
    final_gain,
    final_bias,
    w_qkv,
    w_proj,
    w_fc1,
    w_fc2,
    qv_bias,
    fc1_bias,
    rel_table,
    ln_gain,
    ln_bias,
    out_bias,
    cotangent,
):
    section_now = lax.axis_index("pipe")
    section_count = lax.axis_size("pipe")
    dp_now = lax.axis_index("dp")
    dp_count = lax.axis_size("dp")
    tensor_now = lax.axis_index("tensor")
    tensor_count = lax.axis_size("tensor")
    copies = tensor_count // WIN_ROWS
    unit_now = tensor_now // copies
    all_axes = ("pipe", "dp", "tensor")
    group_axes = ("dp", "tensor")
    is_first = section_now == 0
    is_last = section_now == section_count - 1
    is_odd = section_now % 2 == 1
    owned, _, rows_here, merge_in = raw_pages.shape
    micro_count = cotangent.shape[1]
    own_width = D // dp_count

    def section_pairs(sections, step, moves):
        pairs = []
        for section in sections:
            for tensor in range(tensor_count):
                target = (tensor + copies * moves[section % 2]) % tensor_count
                pairs.append(
                    (section * tensor_count + tensor, (section + step) * tensor_count + target)
                )
        return pairs

    def odd_pairs(move):
        return [
            (
                section * tensor_count + tensor,
                section * tensor_count + (tensor + copies * move) % tensor_count,
            )
            for section in range(1, section_count, 2)
            for tensor in range(tensor_count)
        ]

    def hop(halves, sections, step):
        axes = ("pipe", "tensor")
        to_a = lax.ppermute(halves[1], axes, section_pairs(sections, step, (0, 1)))
        to_b = lax.ppermute(halves[0], axes, section_pairs(sections, step, (-1, 0)))
        return to_a, to_b

    def shares_summed(values, axis):
        count = lax.axis_size(axis)
        index = lax.axis_index(axis)
        blocks = values.reshape((count, values.shape[0] // count) + values.shape[1:])
        total = lax.dynamic_index_in_dim(blocks, index, 0, keepdims=False).astype(F32)
        for step in range(1, count):
            block = lax.dynamic_index_in_dim(blocks, (index + step) % count, 0, keepdims=False)
            pairs = [(source, (source + step) % count) for source in range(count)]
            total = total + lax.ppermute(block, axis, pairs).astype(F32)
        return total

    def summed(values, axis):
        count = lax.axis_size(axis)
        step = 1
        while step < count:
            pairs = [(source, source ^ step) for source in range(count)]
            values = values + lax.ppermute(values, axis, pairs)
            step *= 2
        return values

    def whole_unit(rows, axis):
        if copies == 1:
            return rows
        rows = lax.all_gather(rows, "tensor", axis=axis, tiled=True)
        return lax.dynamic_slice_in_dim(rows, unit_now * UNIT, UNIT, axis)

    def own_part(rows, axis):
        if copies == 1:
            return rows
        return lax.dynamic_slice_in_dim(
            rows, (tensor_now % copies) * rows_here, rows_here, axis
        )

    def gather_rows(values, axes):
        size = values.shape[0]
        tile = 8 * 128
        rows = jnp.pad(values, (0, -size % tile)).reshape(-1, 128)
        rows = lax.all_gather(rows, axes, axis=0, tiled=True)
        return rows.reshape(-1, size + -size % tile)[:, :size]

    def to_halves(rows):
        rows = rows.reshape(rows.shape[:-2] + (2, LINES, D))
        pads = [(0, 0)] * (rows.ndim - 2) + [(0, HALF - LINES), (0, 0)]
        return jnp.pad(rows, pads)

    def from_halves(halves):
        rows = halves[..., :LINES, :]
        return rows.reshape(rows.shape[:-3] + (UNIT, D))

    def stacks_of(*kinds, after=()):
        return pl.pallas_call(
            lambda *refs: None,
            out_shape=[jax.ShapeDtypeStruct(shape, dtype) for shape, dtype in kinds],
            in_specs=any_specs(len(after)),
            out_specs=any_specs(len(kinds)),
        )(*after)

    lined = (dp_count, tensor_count) == (OWN, BLOCKS)

    def block_rows(qkv, proj, fc1, fc2):
        half = DB // 2
        tail = (qkv[..., :half, DB:], qkv[..., half:, DB:])
        rows = (qkv[..., :DB], jnp.concatenate(tail, -1), proj, fc1[..., :DB], fc1[..., DB:], fc2)
        return jnp.concatenate(rows, -2)

    shards = [
        weight.astype(BF16)
        for weight in (w_qkv[0].reshape(own_width, -1), w_proj[0], w_fc1[0], w_fc2[0])
    ]
    if lined:
        weights = lax.all_gather(block_rows(*shards), group_axes, axis=0)
        weights = weights.reshape(OWN, BLOCKS, BLOCK_ROWS, DB)
    else:
        split = (dp_count, tensor_count)
        qkv_full, proj_full, fc1_full, fc2_full = [
            lax.all_gather(shard, group_axes, axis=0).reshape(split + shard.shape)
            for shard in shards
        ]
        qkv_full = qkv_full.reshape(split + (own_width, 3, -1)).transpose(0, 2, 3, 1, 4)
        qkv_full = qkv_full.reshape(OWN, DB, 3, BLOCKS, TB).transpose(0, 3, 1, 2, 4)
        qkv_full = qkv_full.reshape(OWN, BLOCKS, DB, 3 * TB)
        fc1_full = fc1_full.transpose(0, 2, 1, 3).reshape(OWN, DB, BLOCKS, FB)
        fc1_full = fc1_full.transpose(0, 2, 1, 3)
        proj_full, fc2_full = [
            full.transpose(1, 2, 0, 3).reshape(BLOCKS, -1, OWN, DB).transpose(2, 0, 1, 3)
            for full in (proj_full, fc2_full)
        ]
        weights = block_rows(qkv_full, proj_full, fc1_full, fc2_full)

    share = w_merge.shape[0]
    fshare = final_gain.shape[0]
    small = jnp.concatenate((merge_gain, merge_bias, final_gain, final_bias))
    small = jnp.pad(small, (0, 8 * D - small.shape[0])).reshape(8, D)
    packed = jnp.concatenate((w_merge, small)).astype(BF16)

    def passed_round(block, axis):
        count = lax.axis_size(axis)
        index = lax.axis_index(axis)
        parts = [block]
        for step in range(1, count):
            pairs = [(source, (source + step) % count) for source in range(count)]
            parts.append(lax.ppermute(block, axis, pairs))
        parts = parts[::-1]
        return lax.dynamic_slice_in_dim(jnp.stack(parts + parts[:-1]), count - 1 - index, count)

    packed_shape = packed.shape
    packed = passed_round(passed_round(packed, "tensor"), "dp")
    packed = packed.reshape((-1,) + packed_shape)

    packed = passed_round(packed, "pipe").reshape((-1,) + packed_shape)
    merge_weight = packed[:, :share].reshape(merge_in, D)
    small_all = packed[:, share]
    merge_scale = small_all[:, :share].reshape(-1).astype(F32)
    merge_shift = small_all[:, share : 2 * share].reshape(-1).astype(F32)
    final_scale = small_all[:, 2 * share : 2 * share + fshare].reshape(-1).astype(F32)
    final_shift = small_all[:, 2 * share + fshare : 2 * (share + fshare)].reshape(-1).astype(F32)

    mask_all = np.zeros((WIN_ROWS, WIN_COLS, PAD, KEYS), np.float32)
    mask_all[:, :, : WIN * WIN, : WIN * WIN] = shift_mask(
        WIN * WIN_ROWS, GRID_W, WIN, SHIFT
    ).reshape(WIN_ROWS, WIN_COLS, WIN * WIN, WIN * WIN)
    mask_here = lax.dynamic_index_in_dim(jnp.asarray(mask_all, BF16), unit_now, 0, keepdims=False)
    mask_here = mask_here.astype(F32) * is_odd.astype(F32)
    orders = np.stack((window_order(0), window_order(SHIFT)))
    parity = section_now % 2
    perm_in = lax.dynamic_index_in_dim(jnp.asarray(orders, BF16), parity, 0, keepdims=False)
    perm_out = lax.dynamic_index_in_dim(
        jnp.asarray(orders.transpose(0, 2, 1), BF16), parity, 0, keepdims=False
    )
    raw_rows = raw_pages.reshape(owned * rows_here, merge_in).astype(F32)
    raw_hat, raw_rstd = norm_stats(raw_rows)
    merged_in = (raw_hat * merge_scale + merge_shift).astype(BF16)
    merged = dot_nn(merged_in, merge_weight).astype(BF16).reshape(owned, rows_here, D)
    merged = to_halves(whole_unit(merged, 1))
    merged, qv_bias, rel_table = lax.optimization_barrier((merged, qv_bias, rel_table))
    cots = to_halves(whole_unit(cotangent[0, :, 0], 1))
    weights, cots_first = lax.optimization_barrier((weights, cots[:, 0]))
    first_list = [merged]
    for section in range(1, section_count):
        first_list.append(lax.ppermute(merged, "pipe", [(section, 0)]))
    firsts = jnp.concatenate(first_list, 0)

    heads_here = rel_table.shape[2]
    head_set = jnp.concatenate((qv_bias[0].reshape(-1), rel_table[0].reshape(-1)))
    head_set = gather_rows(head_set, "tensor")
    qv_all = head_set[:, : qv_bias.shape[1] * qv_bias.shape[2]].reshape(tensor_count, 2, -1)
    qv_all = qv_all.transpose(1, 0, 2).reshape(2, BLOCKS, TB)
    bias_qkv = jnp.stack((qv_all[0], jnp.zeros_like(qv_all[0]), qv_all[1]), 1).reshape(1, 3 * D)
    table_all = head_set[:, qv_bias.shape[1] * qv_bias.shape[2] :]
    table_all = table_all.reshape(tensor_count, 2 * WIN - 1, 2 * WIN - 1, heads_here)
    table_all = table_all.transpose(0, 3, 1, 2).reshape(D // HEAD, 2 * WIN - 1, 2 * WIN - 1)
    offsets = jnp.asarray(rel_parts(WIN))
    spread = jnp.einsum("huv,vy->huy", table_all, offsets, precision=lax.Precision.HIGHEST)
    spread = jnp.einsum("huy,ux->hxy", spread, offsets, precision=lax.Precision.HIGHEST)
    spread = spread.reshape(D // HEAD, WIN, WIN, WIN, WIN).transpose(0, 1, 3, 2, 4)
    spread = spread.reshape(D // HEAD, WIN * WIN, WIN * WIN)
    bias_pos = jnp.pad(spread, ((0, 0), (0, PAD - WIN * WIN), (0, 0)))
    bias_pos = jnp.pad(
        bias_pos, ((0, 0), (0, 0), (0, KEYS - WIN * WIN)), constant_values=-1e30
    )
    bias_pos = bias_pos.reshape(GROUPS, STACK, KEYS)

    vecs = jnp.concatenate(
        (ln_gain[0], ln_bias[0], out_bias[0], final_scale[None], final_shift[None])
    )
    forward_tables = (perm_in, perm_out, mask_here, vecs, bias_qkv, fc1_bias, bias_pos)
    backward_tables = (perm_in, perm_out, vecs)

    cots_next = lax.ppermute(cots_first, ("pipe", "tensor"), odd_pairs(-1))

    tick_count = micro_count + 2 * (section_count - 1)

    def flags_at(start, tick_now):
        slot_now = tick_now - 2 * start
        is_valid = (slot_now >= 0) & (slot_now < micro_count)
        slot = jnp.clip(slot_now, 0, micro_count - 1)
        return jnp.stack([flag.astype(jnp.int32) for flag in (is_valid, slot, is_first, is_last, is_odd)])

    def of_micro(shape, dtype):
        return ((micro_count,) + shape, dtype)

    *stacks, empty_a, empty_b = stacks_of(
        of_micro((ROWS, D), BF16),
        of_micro((ROWS, 3 * D), BF16),
        of_micro((WIN_COLS * GROUPS, STACK, KEYS), BF16),
        of_micro((ROWS, D), BF16),
        of_micro((ROWS, D), F32),
        of_micro((ROWS, D), BF16),
        of_micro((ROWS, D), BF16),
        of_micro((ROWS, FF), BF16),
        of_micro((ROWS, FF), BF16),
        of_micro((ROWS, D), F32),
        of_micro((2, HALF, D), BF16),
        ((HALF, D), BF16),
        ((HALF, D), BF16),
        after=() if lined else (weights,),
    )
    recv = (empty_a, empty_b)
    for tick_now in range(tick_count):
        coming = recv
        if tick_now > 0:
            coming = hop(outgoing, range(section_count - 1), 1)
        flags = flags_at(section_now, tick_now)
        if tick_now == 2:
            flags, cots_next = lax.optimization_barrier((flags, cots_next))
        outgoing, stacks = layer_forward(
            flags, *recv, firsts, forward_tables, weights, stacks
        )
        recv = coming
    (
        x_all,
        qkv_all,
        probs_all,
        mixed_all,
        mid_all,
        rattn_all,
        rmlp_all,
        act_all,
        slope_all,
        out_all,
        hid_all,
    ) = stacks
    stacks = (
        x_all,
        qkv_all,
        slope_all,
        *stacks_of(
            of_micro((ROWS, D), BF16),
            of_micro((2, HALF, D), BF16),
            of_micro((SUMS, D), F32),
            ((GROUPS, STACK, KEYS), F32),
        ),
    )
    recv = (empty_a, empty_b)
    for tick_now in range(tick_count):
        coming = recv
        if tick_now > 0:
            coming = hop(outgoing, range(1, section_count), -1)
        flags = flags_at(section_count - 1 - section_now, tick_now)
        if tick_now == tick_count - 3:
            flags, hid_before = lax.optimization_barrier((flags, hid_before))
        outgoing, stacks = layer_backward(
            flags,
            *recv,
            cots,
            cots_next,
            backward_tables,
            weights,
            (probs_all, mid_all, out_all),
            stacks,
        )
        recv = coming
        if tick_now == micro_count - 1:
            outgoing, hid_all = lax.optimization_barrier((outgoing, hid_all))
            hid_before = lax.ppermute(hid_all[:, 1], ("pipe", "tensor"), odd_pairs(1))
    dba_all, dqkv_all, dpre_all, dbm_all, dx_all, sums_all, dpos = stacks
    shown = jnp.where(is_odd, jnp.stack((hid_before, hid_all[:, 0]), 1), hid_all)
    shown = own_part(from_halves(shown), 1)

    def weight_gradient(left, right):
        left = left.reshape(micro_count * ROWS, -1)
        right = right.reshape(micro_count * ROWS, D)

        def part(target):
            return dot_tn(
                left, lax.dynamic_slice_in_dim(right, target * own_width, own_width, 1)
            )

        total = None
        for step in range(1, dp_count):
            pairs = [(index, (index + step) % dp_count) for index in range(dp_count)]
            moved = lax.ppermute(
                part((dp_now + step) % dp_count).astype(BF16), "dp", pairs
            ).astype(F32)
            total = moved if total is None else total + moved
        mine = part(dp_now)
        total = mine if total is None else mine + total
        return total / copies

    def over_tensor(*totals):
        totals = [
            total.astype(BF16).reshape(tensor_count, -1, total.shape[1]) for total in totals
        ]
        rows = [total.shape[1] for total in totals]
        total = jnp.concatenate(totals, 1)
        total = lax.psum_scatter(total, "tensor", scatter_dimension=0).astype(F32)
        return jnp.split(total, np.cumsum(rows)[:-1])

    g_proj = weight_gradient(mixed_all, dba_all)
    g_qkv = weight_gradient(dqkv_all, rattn_all)
    if copies > 1:
        g_qkv = g_qkv.reshape(BLOCKS, 3, copies, TB // copies, own_width)
        g_qkv = g_qkv.transpose(0, 2, 1, 3, 4).reshape(3 * D, own_width)
    g_proj, g_qkv, act_all, dbm_all, dpre_all, rmlp_all, dx_all = lax.optimization_barrier(
        (g_proj, g_qkv, act_all, dbm_all, dpre_all, rmlp_all, dx_all)
    )
    g_proj, g_qkv = over_tensor(g_proj, g_qkv)
    g_fc2 = weight_gradient(act_all, dbm_all)
    g_fc2, g_fc1 = over_tensor(g_fc2, weight_gradient(dpre_all, rmlp_all))
    g_fc1 = g_fc1.T
    g_qkv = g_qkv.T.reshape(own_width, 3, D // tensor_count)

    own_grads = dx_all[:owned]
    for section in range(1, section_count):
        moved = lax.ppermute(
            dx_all[section * owned : (section + 1) * owned], "pipe", [(0, section)]
        )
        own_grads = jnp.where(section_now == section, moved, own_grads)
    grad_merged = own_part(from_halves(own_grads), 1).reshape(owned * rows_here, D)
    g_merge = dot_tn(merged_in, grad_merged)
    g_merge = g_merge.reshape(section_count, dp_count, tensor_count, share, D)
    g_merge = shares_summed(g_merge.transpose(1, 0, 2, 3, 4).astype(BF16), "dp")[0]
    g_merge = shares_summed(g_merge.astype(BF16), "pipe")[0]
    g_merge = shares_summed(g_merge.astype(BF16), "tensor")[0]
    grad_unit = dot_nt(grad_merged, merge_weight)
    merge_sums = jnp.stack((jnp.sum(grad_unit * raw_hat, 0), jnp.sum(grad_unit, 0)))
    grad_raw = norm_back(raw_hat, raw_rstd, grad_unit * merge_scale)
    grad_raw = grad_raw.reshape(raw_pages.shape).astype(BF16)

    sums = jnp.sum(sums_all, 0) / copies
    dpos = dpos.reshape(D // HEAD, PAD, KEYS)[:, : WIN * WIN, : WIN * WIN]
    dpos = dpos.reshape(D // HEAD, WIN, WIN, WIN, WIN).transpose(0, 1, 3, 2, 4)
    dpos = dpos.reshape(D // HEAD, WIN * WIN, WIN * WIN) / copies
    dtable = jnp.einsum("hxy,vy->hxv", dpos, offsets, precision=lax.Precision.HIGHEST)
    dtable = jnp.einsum("hxv,ux->huv", dtable, offsets, precision=lax.Precision.HIGHEST)
    final_sums = sums[6:8] * is_last.astype(F32)
    every = jnp.concatenate((merge_sums.reshape(-1), final_sums.reshape(-1)))
    vector = jnp.concatenate((every, sums.reshape(-1), dtable.reshape(-1)))
    size = vector.shape[0]
    vector = jnp.pad(vector, (0, -size % D)).reshape(-1, 128)
    for axis in group_axes:
        vector = summed(vector, axis)
    edge_rows = every.shape[0] // 128
    edge = summed(vector[:edge_rows], "pipe").reshape(-1)
    local_sums = vector[edge_rows:].reshape(-1)
    sums = local_sums[: SUMS * D].reshape(SUMS, D)
    dtable = local_sums[SUMS * D : SUMS * D + dtable.size].reshape(tensor_count, heads_here, -1)
    g_table = lax.dynamic_index_in_dim(dtable, tensor_now, 0, keepdims=False).T
    dqv = sums[12:15].reshape(BLOCKS, 3, TB)[:, 0::2].transpose(1, 0, 2).reshape(2, D)
    g_qv = lax.dynamic_slice_in_dim(
        dqv, tensor_now * (D // tensor_count), D // tensor_count, 1
    )
    place = (section_now * dp_count + dp_now) * tensor_count + tensor_now
    edge_parts = []
    start = 0
    for size, width in ((merge_in, share), (merge_in, share), (D, fshare), (D, fshare)):
        edge_parts.append(lax.dynamic_slice_in_dim(edge, start + place * width, width))
        start += size
    return (
        shown[None, :, None],
        grad_raw,
        g_merge,
        *edge_parts,
        g_qkv[None],
        g_proj[None],
        g_fc1[None],
        g_fc2[None],
        g_qv[None],
        sums[8:12].reshape(1, FF),
        g_table[None],
        sums[0:2][None],
        sums[2:4][None],
        sums[4:6][None],
    )


def solution(mesh):
    return jax.shard_map(
        on_device,
        mesh=mesh,
        in_specs=(
            P("pipe", "dp", "tensor", None),
            P(("pipe", "dp", "tensor"), None),
            P(("pipe", "dp", "tensor")),
            P(("pipe", "dp", "tensor")),
            P(("pipe", "dp", "tensor")),
            P(("pipe", "dp", "tensor")),
            P("pipe", "dp", None, "tensor"),
            P("pipe", "tensor", "dp"),
            P("pipe", "dp", "tensor"),
            P("pipe", "tensor", "dp"),
            P("pipe", None, "tensor"),
            P("pipe", None),
            P("pipe", None, "tensor"),
            P("pipe", None, None),
            P("pipe", None, None),
            P("pipe", None, None),
            P("pipe", None, "dp", "tensor", None),
        ),
        out_specs=(
            P("pipe", None, "dp", "tensor", None),
            P("pipe", "dp", "tensor", None),
            P(("pipe", "dp", "tensor"), None),
            P(("pipe", "dp", "tensor")),
            P(("pipe", "dp", "tensor")),
            P(("pipe", "dp", "tensor")),
            P(("pipe", "dp", "tensor")),
            P("pipe", "dp", None, "tensor"),
            P("pipe", "tensor", "dp"),
            P("pipe", "dp", "tensor"),
            P("pipe", "tensor", "dp"),
            P("pipe", None, "tensor"),
            P("pipe", None),
            P("pipe", None, "tensor"),
            P("pipe", None, None),
            P("pipe", None, None),
            P("pipe", None, None),
        ),
        check_vma=False,
    )
```

```python
import functools

import jax
import jax.numpy as jnp
import numpy as np
from jax import lax
from jax.experimental import pallas as pl
from jax.experimental.pallas import tpu as pltpu
from jax.sharding import PartitionSpec as P

D = 1024
HEAD = 32
FF = 4096
WIN = 10
SHIFT = 5
WIN_ROWS = 4
WIN_COLS = 3
NORM_EPS = 1e-05

GRID_W = WIN * WIN_COLS
UNIT = WIN * GRID_W
LINES = SHIFT * GRID_W
HALF = 160
PAD = 112
KEYS = 128
ROWS = WIN_COLS * PAD
PER = 128 // HEAD
GROUPS = D // 128
STACK = PER * PAD
QKV_AT, PROJ_AT, FC1_AT, FC2_AT, BLOCK_ROWS = 0, 768, 1024, 2048, 3072
OWN = 2
BLOCKS = 4
DB = D // OWN
TB = D // BLOCKS
FB = FF // BLOCKS
STEP = PAD
SUMS = 16
VMEM_BYTES = 60 * 1024 * 1024

F32 = jnp.float32
BF16 = jnp.bfloat16


def rel_parts(window):
    offsets = np.arange(window)[:, None] - np.arange(window)[None, :] + window - 1
    return (offsets.reshape(-1)[None, :] == np.arange(2 * window - 1)[:, None]).astype(np.float32)


def shift_mask(grid_rows, grid_cols, window, shift_now):
    region = np.zeros((grid_rows, grid_cols), np.int64)
    region_id = 0
    for span_rows in (
        (0, grid_rows - window),
        (grid_rows - window, grid_rows - shift_now),
        (grid_rows - shift_now, grid_rows),
    ):
        for span_cols in (
            (0, grid_cols - window),
            (grid_cols - window, grid_cols - shift_now),
            (grid_cols - shift_now, grid_cols),
        ):
            region[span_rows[0] : span_rows[1], span_cols[0] : span_cols[1]] = region_id
            region_id += 1
    blocks = region.reshape(grid_rows // window, window, grid_cols // window, window).transpose(
        0, 2, 1, 3
    )
    blocks = blocks.reshape(-1, window * window)
    return np.where(blocks[:, :, None] == blocks[:, None, :], 0.0, -100.0).astype(np.float32)


def window_order(shift_now):
    order = np.zeros((ROWS, 2 * HALF), np.float32)
    for win in range(WIN_COLS):
        for row in range(WIN):
            for col in range(WIN):
                source_col = (win * WIN + col + shift_now) % GRID_W
                source = (row // SHIFT) * HALF + (row % SHIFT) * GRID_W + source_col
                order[win * PAD + row * WIN + col, source] = 1.0
    return order


def norm_stats(values):
    row_mean = jnp.mean(values, -1, keepdims=True)
    centred = values - row_mean
    rstd_rows = lax.rsqrt(jnp.mean(centred * centred, -1, keepdims=True) + NORM_EPS)
    return (centred * rstd_rows, rstd_rows)


def norm_back(normed, rstd_rows, grad_normed):
    return rstd_rows * (
        grad_normed
        - jnp.mean(grad_normed, -1, keepdims=True)
        - normed * jnp.mean(grad_normed * normed, -1, keepdims=True)
    )


def dot_nn(left, right):
    return lax.dot_general(left, right, (((1,), (0,)), ((), ())), preferred_element_type=F32)


def dot_nt(left, right):
    return lax.dot_general(left, right, (((1,), (1,)), ((), ())), preferred_element_type=F32)


def dot_tn(left, right):
    return lax.dot_general(left, right, (((0,), (0,)), ((), ())), preferred_element_type=F32)


def row_chunks(body, carry=None):
    def step(index, state):
        return body(pl.ds(pl.multiple_of(index * STEP, STEP), STEP), state)

    return lax.fori_loop(0, ROWS // STEP, step, carry)


def fold8(values):
    return jnp.sum(values.reshape(values.shape[0] // 8, 8, values.shape[1]), 0)


def head_masks():
    lane_head = lax.broadcasted_iota(jnp.int32, (1, 128), 1) // HEAD
    return [(lane_head == head).astype(F32) for head in range(PER)]


def spread_heads(tile, masks):
    return jnp.concatenate([(tile * mask.astype(BF16)) for mask in masks], 0)


def pick_heads(stacked, masks):
    total = stacked[:PAD] * masks[0]
    for head in range(1, PER):
        total = total + stacked[head * PAD : (head + 1) * PAD] * masks[head]
    return total


def group_columns(group):
    return (group // 2) * (3 * TB) + (group % 2) * 128


class Copies:
    def __init__(self, copies):
        self.copies = copies

    def start(self):
        for copy in self.copies:
            copy.start()

    def wait(self):
        for copy in self.copies:
            copy.wait()


def weight_copies(w_all, targets, sems, block):
    v_qkv, v_proj, v_fc1, v_fc2 = targets
    half = DB // 2
    moves = {
        "qkv": (
            (v_qkv, (0, DB), (0, DB), 0, 0),
            (v_qkv, (0, half), (DB, half), QKV_AT + DB, 0),
            (v_qkv, (half, half), (DB, half), QKV_AT + DB, half),
        ),
        "proj": ((v_proj, (0, TB), (0, DB), PROJ_AT, 0),),
        "fc1": ((v_fc1, (0, DB), (0, DB), FC1_AT, 0), (v_fc1, (0, DB), (DB, DB), FC1_AT + DB, 0)),
        "fc2": ((v_fc2, (0, FB), (0, DB), FC2_AT, 0),),
    }
    starts = {"qkv": 0, "proj": 3, "fc1": 4, "fc2": 6}

    def copies(kind):
        result = []
        for index, (target, rows, columns, row, column) in enumerate(moves[kind]):
            result.append(
                pltpu.make_async_copy(
                    w_all.at[:, block, pl.ds(row, rows[1]), pl.ds(column, columns[1])],
                    target.at[:, block, pl.ds(*rows), pl.ds(*columns)],
                    sems.at[(starts[kind] + index) * BLOCKS + block],
                )
            )
        return Copies(result)

    return copies


def lanes(start, size):
    return pl.ds(pl.multiple_of(start, 128), size)


def forward_kernel(
    flags,
    recv_a,
    recv_b,
    firsts,
    perm_in,
    perm_out,
    mask,
    vecs,
    bias_qkv,
    bias_fc1,
    bias_pos,
    w_all,
    *refs,
):
    (x_all, qkv_all, probs_all, mixed_all, mid_all, rattn_all, rmlp_all, act_all, slope_all) = refs[11:20]
    out_all, hid_all = refs[20:22]
    sends = refs[22:24]
    (
        v_qkv,
        v_proj,
        v_fc1,
        v_fc2,
        v_pos,
        rin,
        xf,
        xb,
        rattn,
        qkv,
        probs,
        mixed,
        mid,
        rmlp,
        act,
        slope,
        total,
        final,
        outb,
        outs,
        sem_w,
        sem_in,
        sem_out,
        sem_h,
    ) = refs[24:]
    valid = flags[0]
    slot = flags[1]
    is_first = flags[2]
    is_last = flags[3]

    @pl.when(valid == 1)
    def _():
        targets = (v_qkv, v_proj, v_fc1, v_fc2)

        def w_copy(kind, block):
            return weight_copies(w_all, targets, sem_w, block)(("qkv", "fc1", "fc2")[kind])

        def proj_copy():
            return Copies(
                [weight_copies(w_all, targets, sem_w, block)("proj").copies[0] for block in range(BLOCKS)]
            )

        def pos_copy():
            return pltpu.make_async_copy(bias_pos, v_pos, sem_w.at[7 * BLOCKS])

        @pl.when(is_first == 1)
        def _():
            pltpu.make_async_copy(
                firsts.at[slot, 0], rin.at[pl.ds(0, HALF)], sem_in.at[0]
            ).start()
            pltpu.make_async_copy(
                firsts.at[slot, 1], rin.at[pl.ds(HALF, HALF)], sem_in.at[1]
            ).start()

        @pl.when(is_first == 0)
        def _():
            pltpu.make_async_copy(recv_a, rin.at[pl.ds(0, HALF)], sem_in.at[0]).start()
            pltpu.make_async_copy(recv_b, rin.at[pl.ds(HALF, HALF)], sem_in.at[1]).start()

        for block in range(BLOCKS):
            w_copy(0, block).start()
        pltpu.make_async_copy(recv_a, rin.at[pl.ds(0, HALF)], sem_in.at[0]).wait()
        pltpu.make_async_copy(recv_b, rin.at[pl.ds(HALF, HALF)], sem_in.at[1]).wait()

        xf[...] = dot_nn(perm_in[...], rin[...])

        def first_norm(rows, state):
            values = xf[rows, :]
            hat, _ = norm_stats(values)
            rattn[rows, :] = (hat * vecs[0:1, :] + vecs[2:3, :]).astype(BF16)
            xb[rows, :] = values.astype(BF16)
            return state

        row_chunks(first_norm)
        saves = [
            pltpu.make_async_copy(rattn, rattn_all.at[slot], sem_out.at[0]),
            pltpu.make_async_copy(xb, x_all.at[slot], sem_out.at[1]),
        ]
        saves[0].start()
        saves[1].start()
        qkv[pl.ds(ROWS, 16), :] = jnp.zeros((16, 3 * D), BF16)

        pos_copy().start()
        proj_copy().start()

        def qkv_block(block, state):
            w_copy(0, block).wait()
            w_copy(1, block).start()
            out = dot_nn(rattn[...], v_qkv[:, block].reshape(D, 3 * TB))
            columns = lanes(block * 3 * TB, 3 * TB)
            qkv[pl.ds(0, ROWS), columns] = (out + bias_qkv[:, columns]).astype(BF16)
            return state

        lax.fori_loop(0, BLOCKS, qkv_block, None)
        save_qkv = pltpu.make_async_copy(
            qkv.at[pl.ds(0, ROWS)], qkv_all.at[slot], sem_out.at[2]
        )
        save_qkv.start()
        for block in range(BLOCKS):
            w_copy(2, block).start()
        pos_copy().wait()
        masks = head_masks()

        def attend(win, group):
            base = pl.multiple_of(win * PAD, 16)
            column = group_columns(group)
            query = qkv[pl.ds(base, PAD), lanes(column, 128)]
            key = qkv[pl.ds(base, KEYS), lanes(column + TB, 128)]
            value = qkv[pl.ds(base, KEYS), lanes(column + 2 * TB, 128)]
            scores = dot_nt(spread_heads(query, masks), key)
            scores = scores * HEAD**-0.5 + v_pos[group]
            scores = scores + jnp.concatenate([mask[win]] * PER, 0)
            top = jnp.max(scores, -1, keepdims=True)
            powers = jnp.exp(scores - top)
            low = (powers * (1.0 / jnp.sum(powers, -1, keepdims=True))).astype(BF16)
            probs[win * GROUPS + group] = low
            mixed[pl.ds(base, PAD), lanes(group * 128, 128)] = pick_heads(
                dot_nn(low, value), masks
            ).astype(BF16)

        def attend_window(win, state):
            for group in range(GROUPS):
                attend(win, group)
            return state

        lax.fori_loop(0, WIN_COLS, attend_window, None)
        saves.append(pltpu.make_async_copy(probs, probs_all.at[slot], sem_out.at[3]))
        saves[-1].start()
        saves.append(pltpu.make_async_copy(mixed, mixed_all.at[slot], sem_out.at[4]))
        saves[-1].start()
        proj_copy().wait()
        for own in range(OWN):
            columns = slice(own * DB, (own + 1) * DB)
            out = dot_nn(mixed[...], v_proj[own].reshape(D, DB))
            mid[:, columns] = xf[:, columns] + vecs[4:5, columns] + out
        saves.append(pltpu.make_async_copy(mid, mid_all.at[slot], sem_out.at[5]))
        saves[-1].start()

        def second_norm(rows, state):
            hat, _ = norm_stats(mid[rows, :])
            rmlp[rows, :] = (hat * vecs[1:2, :] + vecs[3:4, :]).astype(BF16)
            total[rows, :] = mid[rows, :] + vecs[5:6, :]
            return state

        row_chunks(second_norm)
        saves.append(pltpu.make_async_copy(rmlp, rmlp_all.at[slot], sem_out.at[6]))
        saves[-1].start()

        def hidden_saves(block):
            columns = lanes(block * FB, FB)
            return [
                pltpu.make_async_copy(
                    source.at[:, columns], target.at[slot, :, columns], sem_h.at[kind * BLOCKS + block]
                )
                for kind, (source, target) in enumerate(((act, act_all), (slope, slope_all)))
            ]

        def hidden_block(block, state):
            w_copy(1, block).wait()
            columns = lanes(block * FB, FB)
            pre = dot_nn(rmlp[...], v_fc1[:, block].reshape(D, FB))
            pre = pre + bias_fc1[:, columns]
            chance = 0.5 + 0.5 * lax.erf(pre * np.float32(0.5**0.5))
            slope[:, columns] = (
                chance + pre * (np.float32((2 * np.pi) ** -0.5) * jnp.exp(-0.5 * pre * pre))
            ).astype(BF16)
            act[:, columns] = (pre * chance).astype(BF16)
            for save in hidden_saves(block):
                save.start()
            return state

        lax.fori_loop(0, BLOCKS, hidden_block, None)
        for block in range(BLOCKS):
            w_copy(2, block).wait()
        for own in range(OWN):
            half = slice(own * DB, (own + 1) * DB)
            total[:, half] += dot_nn(act[...], v_fc2[own].reshape(FF, DB))

        def finish(rows, state):
            hat, _ = norm_stats(total[rows, :])
            outb[rows, :] = (hat * vecs[6:7, :] + vecs[7:8, :]).astype(BF16)
            return state

        @pl.when(is_last == 1)
        def _():
            row_chunks(finish)

        @pl.when(is_last == 0)
        def _():
            outb[...] = total[...].astype(BF16)

        save_out = pltpu.make_async_copy(total, out_all.at[slot], sem_out.at[9])

        @pl.when(is_last == 1)
        def _():
            save_out.start()

        outs[...] = dot_nn(perm_out[...], outb[...]).astype(BF16)
        for half in range(2):
            rows = pl.ds(half * HALF, HALF)
            saves.append(
                pltpu.make_async_copy(outs.at[rows], sends[half], sem_out.at[10 + half])
            )
            saves[-1].start()
            saves.append(
                pltpu.make_async_copy(outs.at[rows], hid_all.at[slot, half], sem_out.at[12 + half])
            )
            saves[-1].start()
        save_qkv.wait()
        for block in range(BLOCKS):
            saves.extend(hidden_saves(block))
        for save in saves:
            save.wait()

        @pl.when(is_last == 1)
        def _():
            save_out.wait()


def backward_kernel(
    flags,
    recv_a,
    recv_b,
    cots,
    cots_next,
    perm_in,
    perm_out,
    vecs,
    w_all,
    probs_all,
    mid_all,
    out_all,
    *refs,
):
    x_all, qkv_all, slope_all, dbm_all, dx_all, sums_all, dpos_all = refs[7:14]
    sends = refs[14:16]
    (
        v_qkv,
        v_proj,
        v_fc1,
        v_fc2,
        rin,
        rcot,
        xb,
        qkv,
        probs,
        mid,
        last,
        slope,
        grad,
        back,
        dbm,
        dba,
        dmix,
        dqkv,
        dpos,
        sums,
        outs,
        sem_w,
        sem_in,
        sem_out,
        sem_h,
    ) = refs[16:]
    valid = flags[0]
    slot = flags[1]
    is_last = flags[3]

    @pl.when(valid == 1)
    def _():
        targets = (v_qkv, v_proj, v_fc1, v_fc2)

        def w_copy(kind, block):
            return weight_copies(w_all, targets, sem_w, block)(("fc2", "fc1", "qkv")[kind])

        def proj_copy():
            return Copies(
                [weight_copies(w_all, targets, sem_w, block)("proj").copies[0] for block in range(BLOCKS)]
            )

        def load(index):
            source, target = (
                (cots.at[slot, 0], rcot.at[pl.ds(0, HALF)]),
                (cots.at[slot, 1], rcot.at[pl.ds(HALF, HALF)]),
                (recv_a, rin.at[pl.ds(0, HALF)]),
                (recv_b, rin.at[pl.ds(HALF, HALF)]),
                (out_all.at[slot], last),
                (slope_all.at[slot], slope),
                (mid_all.at[slot], mid),
                (qkv_all.at[slot], qkv.at[pl.ds(0, ROWS)]),
                (probs_all.at[slot], probs),
                (x_all.at[slot], xb),
                (dpos_all, dpos),
            )[index]
            return pltpu.make_async_copy(source, target, sem_in.at[index])

        @pl.when(flags[4] == 0)
        def _():
            load(0).start()
            load(1).start()

        @pl.when(flags[4] == 1)
        def _():
            for half, source in enumerate((cots.at[slot, 1], cots_next.at[slot])):
                pltpu.make_async_copy(
                    source, rcot.at[pl.ds(half * HALF, HALF)], sem_in.at[half]
                ).start()

        load(2).start()
        load(3).start()

        @pl.when(is_last == 1)
        def _():
            load(4).start()

        w_copy(0, 0).start()
        load(5).start()
        w_copy(1, 0).start()
        w_copy(0, 1).start()
        w_copy(1, 1).start()
        for index in range(4):
            load(index).wait()
        sums[...] = jnp.zeros_like(sums)
        grad[...] = dot_nn(perm_in[...], rcot[...])

        @pl.when(is_last == 1)
        def _():
            load(4).wait()

            def final_norm(rows, state):
                cot = grad[rows, :]
                hat, rstd = norm_stats(last[rows, :])
                grad[rows, :] = norm_back(hat, rstd, cot * vecs[6:7, :])
                return (state[0] + fold8(cot * hat), state[1] + fold8(cot))

            zero = jnp.zeros((8, D), F32)
            gain, shift = row_chunks(final_norm, (zero, zero))
            sums[6:7, :] = jnp.sum(gain, 0, keepdims=True)
            sums[7:8, :] = jnp.sum(shift, 0, keepdims=True)

        @pl.when(is_last == 0)
        def _():
            grad[...] += dot_nn(perm_in[...], rin[...])

        def enter(rows, state):
            values = grad[rows, :]
            dbm[rows, :] = values.astype(BF16)
            back[rows, :] = jnp.zeros((STEP, D), F32)
            return state + fold8(values)

        out_sum = row_chunks(enter, jnp.zeros((8, D), F32))
        sums[5:6, :] = jnp.sum(out_sum, 0, keepdims=True)
        saves = [pltpu.make_async_copy(dbm, dbm_all.at[slot], sem_out.at[0])]
        saves[0].start()
        load(5).wait()

        def hidden_save(block):
            columns = lanes(block * FB, FB)
            return pltpu.make_async_copy(
                slope.at[:, columns], slope_all.at[slot, :, columns], sem_h.at[block]
            )

        def hidden_block(block, state):
            columns = lanes(block * FB, FB)
            w_copy(0, block).wait()

            @pl.when(block < BLOCKS - 2)
            def _():
                w_copy(0, block + 2).start()
                w_copy(1, block + 2).start()

            @pl.when(block == BLOCKS - 2)
            def _():
                load(6).start()
                proj_copy().start()
                load(7).start()
                load(8).start()

            dact = dot_nt(dbm[:, :DB], v_fc2[0, block]) + dot_nt(dbm[:, DB:], v_fc2[1, block])
            dpre = (dact * slope[:, columns].astype(F32)).astype(BF16)
            slope[:, columns] = dpre
            hidden_save(block).start()
            sums[pl.ds(8 + block, 1), :] = jnp.sum(dpre.astype(F32), 0, keepdims=True)
            w_copy(1, block).wait()
            for own in range(OWN):
                half = slice(own * DB, (own + 1) * DB)
                back[:, half] += dot_nt(slope[:, columns], v_fc1[own, block])
            return state

        lax.fori_loop(0, BLOCKS, hidden_block, None)
        for block in range(BLOCKS):
            w_copy(2, block).start()
        load(9).start()

        @pl.when(slot > 0)
        def _():
            load(10).start()

        load(6).wait()

        def mlp_norm(rows, state):
            hat, rstd = norm_stats(mid[rows, :])
            ready = back[rows, :]
            values = grad[rows, :] + norm_back(hat, rstd, ready * vecs[1:2, :])
            grad[rows, :] = values
            dba[rows, :] = values.astype(BF16)
            back[rows, :] = jnp.zeros((STEP, D), F32)
            return (state[0] + fold8(ready * hat), state[1] + fold8(ready), state[2] + fold8(values))

        zero = jnp.zeros((8, D), F32)
        gain, shift, out_sum = row_chunks(mlp_norm, (zero, zero, zero))
        sums[1:2, :] = jnp.sum(gain, 0, keepdims=True)
        sums[3:4, :] = jnp.sum(shift, 0, keepdims=True)
        sums[4:5, :] = jnp.sum(out_sum, 0, keepdims=True)
        load(9).wait()
        saves.append(pltpu.make_async_copy(dba, x_all.at[slot], sem_out.at[2]))
        saves[-1].start()
        proj_copy().wait()
        for block in range(BLOCKS):
            out = dot_nt(dba[:, :DB], v_proj[0, block]) + dot_nt(dba[:, DB:], v_proj[1, block])
            dmix[:, block * TB : (block + 1) * TB] = out.astype(BF16)
        load(7).wait()
        load(8).wait()

        @pl.when(slot > 0)
        def _():
            load(10).wait()

        @pl.when(slot == 0)
        def _():
            dpos[...] = jnp.zeros_like(dpos)

        qkv[pl.ds(ROWS, 16), :] = jnp.zeros((16, 3 * D), BF16)
        masks = head_masks()

        def attend_back(group, state):
            column = group_columns(group)
            for win in range(WIN_COLS):
                base = win * PAD
                query = qkv[pl.ds(base, PAD), lanes(column, 128)]
                key = qkv[pl.ds(base, KEYS), lanes(column + TB, 128)]
                value = qkv[pl.ds(base, KEYS), lanes(column + 2 * TB, 128)]
                low = probs[win * GROUPS + group]
                dout = spread_heads(dmix[pl.ds(base, PAD), lanes(group * 128, 128)], masks)
                dprob = dot_nt(dout, value)
                weight = low.astype(F32)
                dscore = weight * (dprob - jnp.sum(dprob * weight, -1, keepdims=True))
                dscore = dscore.astype(BF16)
                dpos[group] += dscore.astype(F32)
                dquery = pick_heads(dot_nn(dscore, key), masks) * HEAD**-0.5
                dkey = dot_tn(dscore, spread_heads(query, masks)) * HEAD**-0.5
                dvalue = dot_tn(low, dout)
                dqkv[pl.ds(base, PAD), lanes(column, 128)] = dquery.astype(BF16)
                dqkv[pl.ds(base, PAD), lanes(column + TB, 128)] = dkey[:PAD].astype(BF16)
                dqkv[pl.ds(base, PAD), lanes(column + 2 * TB, 128)] = dvalue[:PAD].astype(BF16)
            return state

        def attend_back_pair(pair, state):
            return attend_back(2 * pair + 1, attend_back(2 * pair, state))

        lax.fori_loop(0, GROUPS // 2, attend_back_pair, None)
        saves.append(pltpu.make_async_copy(dqkv, qkv_all.at[slot], sem_out.at[3]))
        saves[-1].start()
        saves.append(pltpu.make_async_copy(dpos, dpos_all, sem_out.at[4]))
        saves[-1].start()

        def ready_block(block, state):
            columns = lanes(block * 3 * TB, 3 * TB)
            w_copy(2, block).wait()
            for own in range(OWN):
                half = slice(own * DB, (own + 1) * DB)
                back[:, half] += dot_nt(dqkv[:, columns], v_qkv[own, block])
            return state

        lax.fori_loop(0, BLOCKS, ready_block, None)
        for part in range(3):
            columns = slice(part * D, (part + 1) * D)
            sums[12 + part : 13 + part, :] = jnp.sum(dqkv[:, columns].astype(F32), 0, keepdims=True)

        def attn_norm(rows, state):
            hat, rstd = norm_stats(xb[rows, :].astype(F32))
            ready = back[rows, :]
            values = grad[rows, :] + norm_back(hat, rstd, ready * vecs[0:1, :])
            xb[rows, :] = values.astype(BF16)
            return (state[0] + fold8(ready * hat), state[1] + fold8(ready))

        gain, shift = row_chunks(attn_norm, (zero, zero))
        sums[0:1, :] = jnp.sum(gain, 0, keepdims=True)
        sums[2:3, :] = jnp.sum(shift, 0, keepdims=True)
        saves.append(pltpu.make_async_copy(sums, sums_all.at[slot], sem_out.at[5]))
        saves[-1].start()
        outs[...] = dot_nn(perm_out[...], xb[...]).astype(BF16)
        for half in range(2):
            rows = pl.ds(half * HALF, HALF)
            saves.append(
                pltpu.make_async_copy(outs.at[rows], sends[half], sem_out.at[6 + half])
            )
            saves[-1].start()
            saves.append(
                pltpu.make_async_copy(outs.at[rows], dx_all.at[slot, half], sem_out.at[8 + half])
            )
            saves[-1].start()
        for block in range(BLOCKS):
            saves.append(hidden_save(block))
        for save in saves:
            save.wait()


def any_specs(count):
    return [pl.BlockSpec(memory_space=pl.ANY)] * count


def vmem_specs(count):
    return [pl.BlockSpec(memory_space=pltpu.VMEM)] * count


def shapes_of(arrays):
    return [jax.ShapeDtypeStruct(array.shape, array.dtype) for array in arrays]


WEIGHT_SCRATCH = [
    pltpu.VMEM((OWN, BLOCKS, DB, 3 * TB), BF16),
    pltpu.VMEM((OWN, BLOCKS, TB, DB), BF16),
    pltpu.VMEM((OWN, BLOCKS, DB, FB), BF16),
    pltpu.VMEM((OWN, BLOCKS, FB, DB), BF16),
]


def layer_forward(flags, recv_a, recv_b, firsts, tables, weights, stacks):
    inputs = (flags, recv_a, recv_b, firsts) + tuple(tables) + (weights,) + tuple(stacks)
    first_stack = len(inputs) - len(stacks)
    wide = lambda dtype: pltpu.VMEM((ROWS, D), dtype)
    results = pl.pallas_call(
        forward_kernel,
        out_shape=shapes_of(stacks) + [jax.ShapeDtypeStruct((HALF, D), BF16)] * 2,
        in_specs=[pl.BlockSpec(memory_space=pltpu.SMEM)]
        + any_specs(3)
        + vmem_specs(6)
        + any_specs(2 + len(stacks)),
        out_specs=any_specs(len(stacks) + 2),
        scratch_shapes=WEIGHT_SCRATCH
        + [
            pltpu.VMEM((GROUPS, STACK, KEYS), F32),
            pltpu.VMEM((2 * HALF, D), BF16),
            wide(F32),
            wide(BF16),
            wide(BF16),
            pltpu.VMEM((ROWS + 16, 3 * D), BF16),
            pltpu.VMEM((WIN_COLS * GROUPS, STACK, KEYS), BF16),
            wide(BF16),
            wide(F32),
            wide(BF16),
            pltpu.VMEM((ROWS, FF), BF16),
            pltpu.VMEM((ROWS, FF), BF16),
            wide(F32),
            wide(F32),
            wide(BF16),
            pltpu.VMEM((2 * HALF, D), BF16),
            pltpu.SemaphoreType.DMA((7 * BLOCKS + 1,)),
            pltpu.SemaphoreType.DMA((2,)),
            pltpu.SemaphoreType.DMA((14,)),
            pltpu.SemaphoreType.DMA((2 * BLOCKS,)),
        ],
        input_output_aliases={first_stack + index: index for index in range(len(stacks))},
        compiler_params=pltpu.CompilerParams(vmem_limit_bytes=VMEM_BYTES),
        cost_estimate=pl.CostEstimate(
            flops=24 * ROWS * D * D, bytes_accessed=40 * 1024 * 1024, transcendentals=ROWS * FF
        ),
        name="layer_forward",
    )(*inputs)
    return results[-2:], tuple(results[:-2])


def layer_backward(flags, recv_a, recv_b, cots, cots_next, tables, weights, saved, stacks):
    inputs = (
        (flags, recv_a, recv_b, cots, cots_next)
        + tuple(tables)
        + (weights,)
        + tuple(saved)
        + tuple(stacks)
    )
    first_stack = len(inputs) - len(stacks)
    wide = lambda dtype: pltpu.VMEM((ROWS, D), dtype)
    results = pl.pallas_call(
        backward_kernel,
        out_shape=shapes_of(stacks) + [jax.ShapeDtypeStruct((HALF, D), BF16)] * 2,
        in_specs=[pl.BlockSpec(memory_space=pltpu.SMEM)]
        + any_specs(4)
        + vmem_specs(3)
        + any_specs(1 + len(saved) + len(stacks)),
        out_specs=any_specs(len(stacks) + 2),
        scratch_shapes=WEIGHT_SCRATCH
        + [
            pltpu.VMEM((2 * HALF, D), BF16),
            pltpu.VMEM((2 * HALF, D), BF16),
            wide(BF16),
            pltpu.VMEM((ROWS + 16, 3 * D), BF16),
            pltpu.VMEM((WIN_COLS * GROUPS, STACK, KEYS), BF16),
            wide(F32),
            wide(F32),
            pltpu.VMEM((ROWS, FF), BF16),
            wide(F32),
            wide(F32),
            wide(BF16),
            wide(BF16),
            wide(BF16),
            pltpu.VMEM((ROWS, 3 * D), BF16),
            pltpu.VMEM((GROUPS, STACK, KEYS), F32),
            pltpu.VMEM((SUMS, D), F32),
            pltpu.VMEM((2 * HALF, D), BF16),
            pltpu.SemaphoreType.DMA((7 * BLOCKS,)),
            pltpu.SemaphoreType.DMA((11,)),
            pltpu.SemaphoreType.DMA((10,)),
            pltpu.SemaphoreType.DMA((BLOCKS,)),
        ],
        input_output_aliases={first_stack + index: index for index in range(len(stacks))},
        compiler_params=pltpu.CompilerParams(vmem_limit_bytes=VMEM_BYTES),
        cost_estimate=pl.CostEstimate(
            flops=24 * ROWS * D * D, bytes_accessed=50 * 1024 * 1024, transcendentals=0
        ),
        name="layer_backward",
    )(*inputs)
    return results[-2:], tuple(results[:-2])


def on_device(
    raw_pages,
    w_merge,
    merge_gain,
    merge_bias,
    final_gain,
    final_bias,
    w_qkv,
    w_proj,
    w_fc1,
    w_fc2,
    qv_bias,
    fc1_bias,
    rel_table,
    ln_gain,
    ln_bias,
    out_bias,
    cotangent,
):
    section_now = lax.axis_index("pipe")
    section_count = lax.axis_size("pipe")
    dp_now = lax.axis_index("dp")
    dp_count = lax.axis_size("dp")
    tensor_now = lax.axis_index("tensor")
    tensor_count = lax.axis_size("tensor")
    copies = tensor_count // WIN_ROWS
    unit_now = tensor_now // copies
    all_axes = ("pipe", "dp", "tensor")
    group_axes = ("dp", "tensor")
    is_first = section_now == 0
    is_last = section_now == section_count - 1
    is_odd = section_now % 2 == 1
    owned, _, rows_here, merge_in = raw_pages.shape
    micro_count = cotangent.shape[1]
    own_width = D // dp_count

    def section_pairs(sections, step, moves):
        pairs = []
        for section in sections:
            for tensor in range(tensor_count):
                target = (tensor + copies * moves[section % 2]) % tensor_count
                pairs.append(
                    (section * tensor_count + tensor, (section + step) * tensor_count + target)
                )
        return pairs

    def odd_pairs(move):
        return [
            (
                section * tensor_count + tensor,
                section * tensor_count + (tensor + copies * move) % tensor_count,
            )
            for section in range(1, section_count, 2)
            for tensor in range(tensor_count)
        ]

    def hop(halves, sections, step):
        axes = ("pipe", "tensor")
        to_a = lax.ppermute(halves[1], axes, section_pairs(sections, step, (0, 1)))
        to_b = lax.ppermute(halves[0], axes, section_pairs(sections, step, (-1, 0)))
        return to_a, to_b

    def shares_summed(values, axis):
        count = lax.axis_size(axis)
        index = lax.axis_index(axis)
        blocks = values.reshape((count, values.shape[0] // count) + values.shape[1:])
        total = lax.dynamic_index_in_dim(blocks, index, 0, keepdims=False).astype(F32)
        for step in range(1, count):
            block = lax.dynamic_index_in_dim(blocks, (index + step) % count, 0, keepdims=False)
            pairs = [(source, (source + step) % count) for source in range(count)]
            total = total + lax.ppermute(block, axis, pairs).astype(F32)
        return total

    def summed(values, axis):
        count = lax.axis_size(axis)
        step = 1
        while step < count:
            pairs = [(source, source ^ step) for source in range(count)]
            values = values + lax.ppermute(values, axis, pairs)
            step *= 2
        return values

    def whole_unit(rows, axis):
        if copies == 1:
            return rows
        rows = lax.all_gather(rows, "tensor", axis=axis, tiled=True)
        return lax.dynamic_slice_in_dim(rows, unit_now * UNIT, UNIT, axis)

    def own_part(rows, axis):
        if copies == 1:
            return rows
        return lax.dynamic_slice_in_dim(
            rows, (tensor_now % copies) * rows_here, rows_here, axis
        )

    def gather_rows(values, axes):
        size = values.shape[0]
        tile = 8 * 128
        rows = jnp.pad(values, (0, -size % tile)).reshape(-1, 128)
        rows = lax.all_gather(rows, axes, axis=0, tiled=True)
        return rows.reshape(-1, size + -size % tile)[:, :size]

    def to_halves(rows):
        rows = rows.reshape(rows.shape[:-2] + (2, LINES, D))
        pads = [(0, 0)] * (rows.ndim - 2) + [(0, HALF - LINES), (0, 0)]
        return jnp.pad(rows, pads)

    def from_halves(halves):
        rows = halves[..., :LINES, :]
        return rows.reshape(rows.shape[:-3] + (UNIT, D))

    def stacks_of(*kinds, after=()):
        return pl.pallas_call(
            lambda *refs: None,
            out_shape=[jax.ShapeDtypeStruct(shape, dtype) for shape, dtype in kinds],
            in_specs=any_specs(len(after)),
            out_specs=any_specs(len(kinds)),
        )(*after)

    lined = (dp_count, tensor_count) == (OWN, BLOCKS)

    def block_rows(qkv, proj, fc1, fc2):
        half = DB // 2
        tail = (qkv[..., :half, DB:], qkv[..., half:, DB:])
        rows = (qkv[..., :DB], jnp.concatenate(tail, -1), proj, fc1[..., :DB], fc1[..., DB:], fc2)
        return jnp.concatenate(rows, -2)

    shards = [
        weight.astype(BF16)
        for weight in (w_qkv[0].reshape(own_width, -1), w_proj[0], w_fc1[0], w_fc2[0])
    ]
    if lined:
        weights = lax.all_gather(block_rows(*shards), group_axes, axis=0)
        weights = weights.reshape(OWN, BLOCKS, BLOCK_ROWS, DB)
    else:
        split = (dp_count, tensor_count)
        qkv_full, proj_full, fc1_full, fc2_full = [
            lax.all_gather(shard, group_axes, axis=0).reshape(split + shard.shape)
            for shard in shards
        ]
        qkv_full = qkv_full.reshape(split + (own_width, 3, -1)).transpose(0, 2, 3, 1, 4)
        qkv_full = qkv_full.reshape(OWN, DB, 3, BLOCKS, TB).transpose(0, 3, 1, 2, 4)
        qkv_full = qkv_full.reshape(OWN, BLOCKS, DB, 3 * TB)
        fc1_full = fc1_full.transpose(0, 2, 1, 3).reshape(OWN, DB, BLOCKS, FB)
        fc1_full = fc1_full.transpose(0, 2, 1, 3)
        proj_full, fc2_full = [
            full.transpose(1, 2, 0, 3).reshape(BLOCKS, -1, OWN, DB).transpose(2, 0, 1, 3)
            for full in (proj_full, fc2_full)
        ]
        weights = block_rows(qkv_full, proj_full, fc1_full, fc2_full)

    share = w_merge.shape[0]
    fshare = final_gain.shape[0]
    small = jnp.concatenate((merge_gain, merge_bias, final_gain, final_bias))
    small = jnp.pad(small, (0, 8 * D - small.shape[0])).reshape(8, D)
    packed = jnp.concatenate((w_merge, small)).astype(BF16)

    def passed_round(block, axis):
        count = lax.axis_size(axis)
        index = lax.axis_index(axis)
        parts = [block]
        for step in range(1, count):
            pairs = [(source, (source + step) % count) for source in range(count)]
            parts.append(lax.ppermute(block, axis, pairs))
        parts = parts[::-1]
        return lax.dynamic_slice_in_dim(jnp.stack(parts + parts[:-1]), count - 1 - index, count)

    packed_shape = packed.shape
    packed = passed_round(passed_round(packed, "tensor"), "dp")
    packed = packed.reshape((-1,) + packed_shape)

    packed = passed_round(packed, "pipe").reshape((-1,) + packed_shape)
    merge_weight = packed[:, :share].reshape(merge_in, D)
    small_all = packed[:, share]
    merge_scale = small_all[:, :share].reshape(-1).astype(F32)
    merge_shift = small_all[:, share : 2 * share].reshape(-1).astype(F32)
    final_scale = small_all[:, 2 * share : 2 * share + fshare].reshape(-1).astype(F32)
    final_shift = small_all[:, 2 * share + fshare : 2 * (share + fshare)].reshape(-1).astype(F32)

    mask_all = np.zeros((WIN_ROWS, WIN_COLS, PAD, KEYS), np.float32)
    mask_all[:, :, : WIN * WIN, : WIN * WIN] = shift_mask(
        WIN * WIN_ROWS, GRID_W, WIN, SHIFT
    ).reshape(WIN_ROWS, WIN_COLS, WIN * WIN, WIN * WIN)
    mask_here = lax.dynamic_index_in_dim(jnp.asarray(mask_all, BF16), unit_now, 0, keepdims=False)
    mask_here = mask_here.astype(F32) * is_odd.astype(F32)
    orders = np.stack((window_order(0), window_order(SHIFT)))
    parity = section_now % 2
    perm_in = lax.dynamic_index_in_dim(jnp.asarray(orders, BF16), parity, 0, keepdims=False)
    perm_out = lax.dynamic_index_in_dim(
        jnp.asarray(orders.transpose(0, 2, 1), BF16), parity, 0, keepdims=False
    )
    raw_rows = raw_pages.reshape(owned * rows_here, merge_in).astype(F32)
    raw_hat, raw_rstd = norm_stats(raw_rows)
    merged_in = (raw_hat * merge_scale + merge_shift).astype(BF16)
    merged = dot_nn(merged_in, merge_weight).astype(BF16).reshape(owned, rows_here, D)
    merged = to_halves(whole_unit(merged, 1))
    merged, qv_bias, rel_table = lax.optimization_barrier((merged, qv_bias, rel_table))
    cots = to_halves(whole_unit(cotangent[0, :, 0], 1))
    weights, cots_first = lax.optimization_barrier((weights, cots[:, 0]))
    first_list = [merged]
    for section in range(1, section_count):
        first_list.append(lax.ppermute(merged, "pipe", [(section, 0)]))
    firsts = jnp.concatenate(first_list, 0)

    heads_here = rel_table.shape[2]
    head_set = jnp.concatenate((qv_bias[0].reshape(-1), rel_table[0].reshape(-1)))
    head_set = gather_rows(head_set, "tensor")
    qv_all = head_set[:, : qv_bias.shape[1] * qv_bias.shape[2]].reshape(tensor_count, 2, -1)
    qv_all = qv_all.transpose(1, 0, 2).reshape(2, BLOCKS, TB)
    bias_qkv = jnp.stack((qv_all[0], jnp.zeros_like(qv_all[0]), qv_all[1]), 1).reshape(1, 3 * D)
    table_all = head_set[:, qv_bias.shape[1] * qv_bias.shape[2] :]
    table_all = table_all.reshape(tensor_count, 2 * WIN - 1, 2 * WIN - 1, heads_here)
    table_all = table_all.transpose(0, 3, 1, 2).reshape(D // HEAD, 2 * WIN - 1, 2 * WIN - 1)
    offsets = jnp.asarray(rel_parts(WIN))
    spread = jnp.einsum("huv,vy->huy", table_all, offsets, precision=lax.Precision.HIGHEST)
    spread = jnp.einsum("huy,ux->hxy", spread, offsets, precision=lax.Precision.HIGHEST)
    spread = spread.reshape(D // HEAD, WIN, WIN, WIN, WIN).transpose(0, 1, 3, 2, 4)
    spread = spread.reshape(D // HEAD, WIN * WIN, WIN * WIN)
    bias_pos = jnp.pad(spread, ((0, 0), (0, PAD - WIN * WIN), (0, 0)))
    bias_pos = jnp.pad(
        bias_pos, ((0, 0), (0, 0), (0, KEYS - WIN * WIN)), constant_values=-1e30
    )
    bias_pos = bias_pos.reshape(GROUPS, STACK, KEYS)

    vecs = jnp.concatenate(
        (ln_gain[0], ln_bias[0], out_bias[0], final_scale[None], final_shift[None])
    )
    forward_tables = (perm_in, perm_out, mask_here, vecs, bias_qkv, fc1_bias, bias_pos)
    backward_tables = (perm_in, perm_out, vecs)

    cots_next = lax.ppermute(cots_first, ("pipe", "tensor"), odd_pairs(-1))

    tick_count = micro_count + 2 * (section_count - 1)

    def flags_at(start, tick_now):
        slot_now = tick_now - 2 * start
        is_valid = (slot_now >= 0) & (slot_now < micro_count)
        slot = jnp.clip(slot_now, 0, micro_count - 1)
        return jnp.stack([flag.astype(jnp.int32) for flag in (is_valid, slot, is_first, is_last, is_odd)])

    def of_micro(shape, dtype):
        return ((micro_count,) + shape, dtype)

    *stacks, empty_a, empty_b = stacks_of(
        of_micro((ROWS, D), BF16),
        of_micro((ROWS, 3 * D), BF16),
        of_micro((WIN_COLS * GROUPS, STACK, KEYS), BF16),
        of_micro((ROWS, D), BF16),
        of_micro((ROWS, D), F32),
        of_micro((ROWS, D), BF16),
        of_micro((ROWS, D), BF16),
        of_micro((ROWS, FF), BF16),
        of_micro((ROWS, FF), BF16),
        of_micro((ROWS, D), F32),
        of_micro((2, HALF, D), BF16),
        ((HALF, D), BF16),
        ((HALF, D), BF16),
        after=() if lined else (weights,),
    )
    recv = (empty_a, empty_b)
    for tick_now in range(tick_count):
        coming = recv
        if tick_now > 0:
            coming = hop(outgoing, range(section_count - 1), 1)
        flags = flags_at(section_now, tick_now)
        if tick_now == 2:
            flags, cots_next = lax.optimization_barrier((flags, cots_next))
        outgoing, stacks = layer_forward(
            flags, *recv, firsts, forward_tables, weights, stacks
        )
        recv = coming
    (
        x_all,
        qkv_all,
        probs_all,
        mixed_all,
        mid_all,
        rattn_all,
        rmlp_all,
        act_all,
        slope_all,
        out_all,
        hid_all,
    ) = stacks
    stacks = (
        x_all,
        qkv_all,
        slope_all,
        *stacks_of(
            of_micro((ROWS, D), BF16),
            of_micro((2, HALF, D), BF16),
            of_micro((SUMS, D), F32),
            ((GROUPS, STACK, KEYS), F32),
        ),
    )
    recv = (empty_a, empty_b)
    for tick_now in range(tick_count):
        coming = recv
        if tick_now > 0:
            coming = hop(outgoing, range(1, section_count), -1)
        flags = flags_at(section_count - 1 - section_now, tick_now)
        if tick_now == tick_count - 3:
            flags, hid_before = lax.optimization_barrier((flags, hid_before))
        outgoing, stacks = layer_backward(
            flags,
            *recv,
            cots,
            cots_next,
            backward_tables,
            weights,
            (probs_all, mid_all, out_all),
            stacks,
        )
        recv = coming
        if tick_now == micro_count - 1:
            outgoing, hid_all = lax.optimization_barrier((outgoing, hid_all))
            hid_before = lax.ppermute(hid_all[:, 1], ("pipe", "tensor"), odd_pairs(1))
    dba_all, dqkv_all, dpre_all, dbm_all, dx_all, sums_all, dpos = stacks
    shown = jnp.where(is_odd, jnp.stack((hid_before, hid_all[:, 0]), 1), hid_all)
    shown = own_part(from_halves(shown), 1)

    def weight_gradient(left, right):
        left = left.reshape(micro_count * ROWS, -1)
        right = right.reshape(micro_count * ROWS, D)

        def part(target):
            return dot_tn(
                left, lax.dynamic_slice_in_dim(right, target * own_width, own_width, 1)
            )

        total = None
        for step in range(1, dp_count):
            pairs = [(index, (index + step) % dp_count) for index in range(dp_count)]
            moved = lax.ppermute(
                part((dp_now + step) % dp_count).astype(BF16), "dp", pairs
            ).astype(F32)
            total = moved if total is None else total + moved
        mine = part(dp_now)
        total = mine if total is None else mine + total
        return total / copies

    def over_tensor(*totals):
        totals = [
            total.astype(BF16).reshape(tensor_count, -1, total.shape[1]) for total in totals
        ]
        rows = [total.shape[1] for total in totals]
        total = jnp.concatenate(totals, 1)
        total = lax.psum_scatter(total, "tensor", scatter_dimension=0).astype(F32)
        return jnp.split(total, np.cumsum(rows)[:-1])

    g_proj = weight_gradient(mixed_all, dba_all)
    g_qkv = weight_gradient(dqkv_all, rattn_all)
    if copies > 1:
        g_qkv = g_qkv.reshape(BLOCKS, 3, copies, TB // copies, own_width)
        g_qkv = g_qkv.transpose(0, 2, 1, 3, 4).reshape(3 * D, own_width)
    g_proj, g_qkv, act_all, dbm_all, dpre_all, rmlp_all, dx_all = lax.optimization_barrier(
        (g_proj, g_qkv, act_all, dbm_all, dpre_all, rmlp_all, dx_all)
    )
    g_proj, g_qkv = over_tensor(g_proj, g_qkv)
    g_fc2 = weight_gradient(act_all, dbm_all)
    g_fc2, g_fc1 = over_tensor(g_fc2, weight_gradient(dpre_all, rmlp_all))
    g_fc1 = g_fc1.T
    g_qkv = g_qkv.T.reshape(own_width, 3, D // tensor_count)

    own_grads = dx_all[:owned]
    for section in range(1, section_count):
        moved = lax.ppermute(
            dx_all[section * owned : (section + 1) * owned], "pipe", [(0, section)]
        )
        own_grads = jnp.where(section_now == section, moved, own_grads)
    own_grads, g_proj, g_qkv = lax.optimization_barrier((own_grads, g_proj, g_qkv))
    grad_merged = own_part(from_halves(own_grads), 1).reshape(owned * rows_here, D)
    g_merge = dot_tn(merged_in, grad_merged).astype(BF16)
    g_merge, dpos = lax.optimization_barrier((g_merge, dpos))
    g_merge = g_merge.reshape(section_count, dp_count, tensor_count, share, D)
    g_merge = shares_summed(g_merge.transpose(1, 0, 2, 3, 4), "dp")[0]
    g_merge = shares_summed(g_merge.astype(BF16), "pipe")[0]
    g_merge = shares_summed(g_merge.astype(BF16), "tensor")[0]
    grad_unit = dot_nt(grad_merged, merge_weight)
    merge_sums = jnp.stack((jnp.sum(grad_unit * raw_hat, 0), jnp.sum(grad_unit, 0)))
    grad_raw = norm_back(raw_hat, raw_rstd, grad_unit * merge_scale)
    grad_raw = grad_raw.reshape(raw_pages.shape).astype(BF16)

    sums = jnp.sum(sums_all, 0) / copies
    dpos = dpos.reshape(D // HEAD, PAD, KEYS)[:, : WIN * WIN, : WIN * WIN]
    dpos = dpos.reshape(D // HEAD, WIN, WIN, WIN, WIN).transpose(0, 1, 3, 2, 4)
    dpos = dpos.reshape(D // HEAD, WIN * WIN, WIN * WIN) / copies
    dtable = jnp.einsum("hxy,vy->hxv", dpos, offsets, precision=lax.Precision.HIGHEST)
    dtable = jnp.einsum("hxv,ux->huv", dtable, offsets, precision=lax.Precision.HIGHEST)
    final_sums = sums[6:8] * is_last.astype(F32)
    every = jnp.concatenate((merge_sums.reshape(-1), final_sums.reshape(-1)))
    vector = jnp.concatenate((every, sums.reshape(-1), dtable.reshape(-1)))
    size = vector.shape[0]
    vector = jnp.pad(vector, (0, -size % D)).reshape(-1, 128)
    for axis in group_axes:
        vector = summed(vector, axis)
    edge_rows = every.shape[0] // 128
    edge = summed(vector[:edge_rows], "pipe").reshape(-1)
    local_sums = vector[edge_rows:].reshape(-1)
    sums = local_sums[: SUMS * D].reshape(SUMS, D)
    dtable = local_sums[SUMS * D : SUMS * D + dtable.size].reshape(tensor_count, heads_here, -1)
    g_table = lax.dynamic_index_in_dim(dtable, tensor_now, 0, keepdims=False).T
    dqv = sums[12:15].reshape(BLOCKS, 3, TB)[:, 0::2].transpose(1, 0, 2).reshape(2, D)
    g_qv = lax.dynamic_slice_in_dim(
        dqv, tensor_now * (D // tensor_count), D // tensor_count, 1
    )
    place = (section_now * dp_count + dp_now) * tensor_count + tensor_now
    edge_parts = []
    start = 0
    for size, width in ((merge_in, share), (merge_in, share), (D, fshare), (D, fshare)):
        edge_parts.append(lax.dynamic_slice_in_dim(edge, start + place * width, width))
        start += size
    return (
        shown[None, :, None],
        grad_raw,
        g_merge,
        *edge_parts,
        g_qkv[None],
        g_proj[None],
        g_fc1[None],
        g_fc2[None],
        g_qv[None],
        sums[8:12].reshape(1, FF),
        g_table[None],
        sums[0:2][None],
        sums[2:4][None],
        sums[4:6][None],
    )


def solution(mesh):
    return jax.shard_map(
        on_device,
        mesh=mesh,
        in_specs=(
            P("pipe", "dp", "tensor", None),
            P(("pipe", "dp", "tensor"), None),
            P(("pipe", "dp", "tensor")),
            P(("pipe", "dp", "tensor")),
            P(("pipe", "dp", "tensor")),
            P(("pipe", "dp", "tensor")),
            P("pipe", "dp", None, "tensor"),
            P("pipe", "tensor", "dp"),
            P("pipe", "dp", "tensor"),
            P("pipe", "tensor", "dp"),
            P("pipe", None, "tensor"),
            P("pipe", None),
            P("pipe", None, "tensor"),
            P("pipe", None, None),
            P("pipe", None, None),
            P("pipe", None, None),
            P("pipe", None, "dp", "tensor", None),
        ),
        out_specs=(
            P("pipe", None, "dp", "tensor", None),
            P("pipe", "dp", "tensor", None),
            P(("pipe", "dp", "tensor"), None),
            P(("pipe", "dp", "tensor")),
            P(("pipe", "dp", "tensor")),
            P(("pipe", "dp", "tensor")),
            P(("pipe", "dp", "tensor")),
            P("pipe", "dp", None, "tensor"),
            P("pipe", "tensor", "dp"),
            P("pipe", "dp", "tensor"),
            P("pipe", "tensor", "dp"),
            P("pipe", None, "tensor"),
            P("pipe", None),
            P("pipe", None, "tensor"),
            P("pipe", None, None),
            P("pipe", None, None),
            P("pipe", None, None),
        ),
        check_vma=False,
    )
```

```python
import functools

import jax
import jax.numpy as jnp
import numpy as np
from jax import lax
from jax.experimental import pallas as pl
from jax.experimental.pallas import tpu as pltpu
from jax.sharding import PartitionSpec as P

D = 1024
HEAD = 32
FF = 4096
WIN = 10
SHIFT = 5
WIN_ROWS = 4
WIN_COLS = 3
NORM_EPS = 1e-05

GRID_W = WIN * WIN_COLS
UNIT = WIN * GRID_W
LINES = SHIFT * GRID_W
HALF = 160
PAD = 112
KEYS = 128
ROWS = WIN_COLS * PAD
PER = 128 // HEAD
GROUPS = D // 128
STACK = PER * PAD
QKV_AT, PROJ_AT, FC1_AT, FC2_AT, BLOCK_ROWS = 0, 768, 1024, 2048, 3072
OWN = 2
BLOCKS = 4
DB = D // OWN
TB = D // BLOCKS
FB = FF // BLOCKS
STEP = PAD
SUMS = 16
VMEM_BYTES = 60 * 1024 * 1024

F32 = jnp.float32
BF16 = jnp.bfloat16


def rel_parts(window):
    offsets = np.arange(window)[:, None] - np.arange(window)[None, :] + window - 1
    return (offsets.reshape(-1)[None, :] == np.arange(2 * window - 1)[:, None]).astype(np.float32)


def shift_mask(grid_rows, grid_cols, window, shift_now):
    region = np.zeros((grid_rows, grid_cols), np.int64)
    region_id = 0
    for span_rows in (
        (0, grid_rows - window),
        (grid_rows - window, grid_rows - shift_now),
        (grid_rows - shift_now, grid_rows),
    ):
        for span_cols in (
            (0, grid_cols - window),
            (grid_cols - window, grid_cols - shift_now),
            (grid_cols - shift_now, grid_cols),
        ):
            region[span_rows[0] : span_rows[1], span_cols[0] : span_cols[1]] = region_id
            region_id += 1
    blocks = region.reshape(grid_rows // window, window, grid_cols // window, window).transpose(
        0, 2, 1, 3
    )
    blocks = blocks.reshape(-1, window * window)
    return np.where(blocks[:, :, None] == blocks[:, None, :], 0.0, -100.0).astype(np.float32)


def window_order(shift_now):
    order = np.zeros((ROWS, 2 * HALF), np.float32)
    for win in range(WIN_COLS):
        for row in range(WIN):
            for col in range(WIN):
                source_col = (win * WIN + col + shift_now) % GRID_W
                source = (row // SHIFT) * HALF + (row % SHIFT) * GRID_W + source_col
                order[win * PAD + row * WIN + col, source] = 1.0
    return order


def norm_stats(values):
    row_mean = jnp.mean(values, -1, keepdims=True)
    centred = values - row_mean
    rstd_rows = lax.rsqrt(jnp.mean(centred * centred, -1, keepdims=True) + NORM_EPS)
    return (centred * rstd_rows, rstd_rows)


def norm_back(normed, rstd_rows, grad_normed):
    return rstd_rows * (
        grad_normed
        - jnp.mean(grad_normed, -1, keepdims=True)
        - normed * jnp.mean(grad_normed * normed, -1, keepdims=True)
    )


def dot_nn(left, right):
    return lax.dot_general(left, right, (((1,), (0,)), ((), ())), preferred_element_type=F32)


def dot_nt(left, right):
    return lax.dot_general(left, right, (((1,), (1,)), ((), ())), preferred_element_type=F32)


def dot_tn(left, right):
    return lax.dot_general(left, right, (((0,), (0,)), ((), ())), preferred_element_type=F32)


def row_chunks(body, carry=None):
    def step(index, state):
        return body(pl.ds(pl.multiple_of(index * STEP, STEP), STEP), state)

    return lax.fori_loop(0, ROWS // STEP, step, carry)


def fold8(values):
    return jnp.sum(values.reshape(values.shape[0] // 8, 8, values.shape[1]), 0)


def head_masks():
    lane_head = lax.broadcasted_iota(jnp.int32, (1, 128), 1) // HEAD
    return [(lane_head == head).astype(F32) for head in range(PER)]


def spread_heads(tile, masks):
    return jnp.concatenate([(tile * mask.astype(BF16)) for mask in masks], 0)


def pick_heads(stacked, masks):
    total = stacked[:PAD] * masks[0]
    for head in range(1, PER):
        total = total + stacked[head * PAD : (head + 1) * PAD] * masks[head]
    return total


def group_columns(group):
    return (group // 2) * (3 * TB) + (group % 2) * 128


class Copies:
    def __init__(self, copies):
        self.copies = copies

    def start(self):
        for copy in self.copies:
            copy.start()

    def wait(self):
        for copy in self.copies:
            copy.wait()


def weight_copies(w_all, targets, sems, block):
    v_qkv, v_proj, v_fc1, v_fc2 = targets
    half = DB // 2
    moves = {
        "qkv": (
            (v_qkv, (0, DB), (0, DB), 0, 0),
            (v_qkv, (0, half), (DB, half), QKV_AT + DB, 0),
            (v_qkv, (half, half), (DB, half), QKV_AT + DB, half),
        ),
        "proj": ((v_proj, (0, TB), (0, DB), PROJ_AT, 0),),
        "fc1": ((v_fc1, (0, DB), (0, DB), FC1_AT, 0), (v_fc1, (0, DB), (DB, DB), FC1_AT + DB, 0)),
        "fc2": ((v_fc2, (0, FB), (0, DB), FC2_AT, 0),),
    }
    starts = {"qkv": 0, "proj": 3, "fc1": 4, "fc2": 6}

    def copies(kind):
        result = []
        for index, (target, rows, columns, row, column) in enumerate(moves[kind]):
            result.append(
                pltpu.make_async_copy(
                    w_all.at[:, block, pl.ds(row, rows[1]), pl.ds(column, columns[1])],
                    target.at[:, block, pl.ds(*rows), pl.ds(*columns)],
                    sems.at[(starts[kind] + index) * BLOCKS + block],
                )
            )
        return Copies(result)

    return copies


def lanes(start, size):
    return pl.ds(pl.multiple_of(start, 128), size)


def forward_kernel(
    flags,
    recv_a,
    recv_b,
    firsts,
    perm_in,
    perm_out,
    mask,
    vecs,
    bias_qkv,
    bias_fc1,
    bias_pos,
    w_all,
    *refs,
):
    (x_all, qkv_all, probs_all, mixed_all, mid_all, rattn_all, rmlp_all, act_all, slope_all) = refs[11:20]
    out_all, hid_all = refs[20:22]
    sends = refs[22:24]
    (
        v_qkv,
        v_proj,
        v_fc1,
        v_fc2,
        v_pos,
        rin,
        xf,
        xb,
        rattn,
        qkv,
        probs,
        mixed,
        mid,
        rmlp,
        act,
        slope,
        total,
        final,
        outb,
        outs,
        sem_w,
        sem_in,
        sem_out,
        sem_h,
    ) = refs[24:]
    valid = flags[0]
    slot = flags[1]
    is_first = flags[2]
    is_last = flags[3]

    @pl.when(valid == 1)
    def _():
        targets = (v_qkv, v_proj, v_fc1, v_fc2)

        def w_copy(kind, block):
            return weight_copies(w_all, targets, sem_w, block)(("qkv", "fc1", "fc2")[kind])

        def proj_copy():
            return Copies(
                [weight_copies(w_all, targets, sem_w, block)("proj").copies[0] for block in range(BLOCKS)]
            )

        def pos_copy():
            return pltpu.make_async_copy(bias_pos, v_pos, sem_w.at[7 * BLOCKS])

        @pl.when(is_first == 1)
        def _():
            pltpu.make_async_copy(
                firsts.at[slot, 0], rin.at[pl.ds(0, HALF)], sem_in.at[0]
            ).start()
            pltpu.make_async_copy(
                firsts.at[slot, 1], rin.at[pl.ds(HALF, HALF)], sem_in.at[1]
            ).start()

        @pl.when(is_first == 0)
        def _():
            pltpu.make_async_copy(recv_a, rin.at[pl.ds(0, HALF)], sem_in.at[0]).start()
            pltpu.make_async_copy(recv_b, rin.at[pl.ds(HALF, HALF)], sem_in.at[1]).start()

        for block in range(BLOCKS):
            w_copy(0, block).start()
        pltpu.make_async_copy(recv_a, rin.at[pl.ds(0, HALF)], sem_in.at[0]).wait()
        pltpu.make_async_copy(recv_b, rin.at[pl.ds(HALF, HALF)], sem_in.at[1]).wait()

        xf[...] = dot_nn(perm_in[...], rin[...])

        def first_norm(rows, state):
            values = xf[rows, :]
            hat, _ = norm_stats(values)
            rattn[rows, :] = (hat * vecs[0:1, :] + vecs[2:3, :]).astype(BF16)
            xb[rows, :] = values.astype(BF16)
            return state

        row_chunks(first_norm)
        saves = [
            pltpu.make_async_copy(rattn, rattn_all.at[slot], sem_out.at[0]),
            pltpu.make_async_copy(xb, x_all.at[slot], sem_out.at[1]),
        ]
        saves[0].start()
        saves[1].start()
        qkv[pl.ds(ROWS, 16), :] = jnp.zeros((16, 3 * D), BF16)

        pos_copy().start()
        proj_copy().start()

        def qkv_block(block, state):
            w_copy(0, block).wait()
            w_copy(1, block).start()
            out = dot_nn(rattn[...], v_qkv[:, block].reshape(D, 3 * TB))
            columns = lanes(block * 3 * TB, 3 * TB)
            qkv[pl.ds(0, ROWS), columns] = (out + bias_qkv[:, columns]).astype(BF16)
            return state

        lax.fori_loop(0, BLOCKS, qkv_block, None)
        save_qkv = pltpu.make_async_copy(
            qkv.at[pl.ds(0, ROWS)], qkv_all.at[slot], sem_out.at[2]
        )
        save_qkv.start()
        for block in range(BLOCKS):
            w_copy(2, block).start()
        pos_copy().wait()
        masks = head_masks()

        def attend(win, group):
            base = pl.multiple_of(win * PAD, 16)
            column = group_columns(group)
            query = qkv[pl.ds(base, PAD), lanes(column, 128)]
            key = qkv[pl.ds(base, KEYS), lanes(column + TB, 128)]
            value = qkv[pl.ds(base, KEYS), lanes(column + 2 * TB, 128)]
            scores = dot_nt(spread_heads(query, masks), key)
            scores = scores * HEAD**-0.5 + v_pos[group]
            scores = scores + jnp.concatenate([mask[win]] * PER, 0)
            top = jnp.max(scores, -1, keepdims=True)
            powers = jnp.exp(scores - top)
            low = (powers * (1.0 / jnp.sum(powers, -1, keepdims=True))).astype(BF16)
            probs[win * GROUPS + group] = low
            mixed[pl.ds(base, PAD), lanes(group * 128, 128)] = pick_heads(
                dot_nn(low, value), masks
            ).astype(BF16)

        def attend_window(win, state):
            for group in range(GROUPS):
                attend(win, group)
            return state

        lax.fori_loop(0, WIN_COLS, attend_window, None)
        saves.append(pltpu.make_async_copy(probs, probs_all.at[slot], sem_out.at[3]))
        saves[-1].start()
        saves.append(pltpu.make_async_copy(mixed, mixed_all.at[slot], sem_out.at[4]))
        saves[-1].start()
        proj_copy().wait()
        for own in range(OWN):
            columns = slice(own * DB, (own + 1) * DB)
            out = dot_nn(mixed[...], v_proj[own].reshape(D, DB))
            mid[:, columns] = xf[:, columns] + vecs[4:5, columns] + out
        saves.append(pltpu.make_async_copy(mid, mid_all.at[slot], sem_out.at[5]))
        saves[-1].start()

        def second_norm(rows, state):
            hat, _ = norm_stats(mid[rows, :])
            rmlp[rows, :] = (hat * vecs[1:2, :] + vecs[3:4, :]).astype(BF16)
            total[rows, :] = mid[rows, :] + vecs[5:6, :]
            return state

        row_chunks(second_norm)
        saves.append(pltpu.make_async_copy(rmlp, rmlp_all.at[slot], sem_out.at[6]))
        saves[-1].start()

        def hidden_saves(block):
            columns = lanes(block * FB, FB)
            return [
                pltpu.make_async_copy(
                    source.at[:, columns], target.at[slot, :, columns], sem_h.at[kind * BLOCKS + block]
                )
                for kind, (source, target) in enumerate(((act, act_all), (slope, slope_all)))
            ]

        def hidden_block(block, state):
            w_copy(1, block).wait()
            columns = lanes(block * FB, FB)
            pre = dot_nn(rmlp[...], v_fc1[:, block].reshape(D, FB))
            pre = pre + bias_fc1[:, columns]
            chance = 0.5 + 0.5 * lax.erf(pre * np.float32(0.5**0.5))
            slope[:, columns] = (
                chance + pre * (np.float32((2 * np.pi) ** -0.5) * jnp.exp(-0.5 * pre * pre))
            ).astype(BF16)
            act[:, columns] = (pre * chance).astype(BF16)
            for save in hidden_saves(block):
                save.start()
            return state

        lax.fori_loop(0, BLOCKS, hidden_block, None)
        for block in range(BLOCKS):
            w_copy(2, block).wait()
        for own in range(OWN):
            half = slice(own * DB, (own + 1) * DB)
            total[:, half] += dot_nn(act[...], v_fc2[own].reshape(FF, DB))

        def finish(rows, state):
            hat, _ = norm_stats(total[rows, :])
            outb[rows, :] = (hat * vecs[6:7, :] + vecs[7:8, :]).astype(BF16)
            return state

        @pl.when(is_last == 1)
        def _():
            row_chunks(finish)

        @pl.when(is_last == 0)
        def _():
            outb[...] = total[...].astype(BF16)

        save_out = pltpu.make_async_copy(total, out_all.at[slot], sem_out.at[9])

        @pl.when(is_last == 1)
        def _():
            save_out.start()

        outs[...] = dot_nn(perm_out[...], outb[...]).astype(BF16)
        for half in range(2):
            rows = pl.ds(half * HALF, HALF)
            saves.append(
                pltpu.make_async_copy(outs.at[rows], sends[half], sem_out.at[10 + half])
            )
            saves[-1].start()
            saves.append(
                pltpu.make_async_copy(outs.at[rows], hid_all.at[slot, half], sem_out.at[12 + half])
            )
            saves[-1].start()
        save_qkv.wait()
        for block in range(BLOCKS):
            saves.extend(hidden_saves(block))
        for save in saves:
            save.wait()

        @pl.when(is_last == 1)
        def _():
            save_out.wait()


def backward_kernel(
    flags,
    recv_a,
    recv_b,
    cots,
    cots_next,
    perm_in,
    perm_out,
    vecs,
    w_all,
    probs_all,
    mid_all,
    out_all,
    *refs,
):
    x_all, qkv_all, slope_all, dbm_all, dx_all, sums_all, dpos_all = refs[7:14]
    sends = refs[14:16]
    (
        v_qkv,
        v_proj,
        v_fc1,
        v_fc2,
        rin,
        rcot,
        xb,
        qkv,
        probs,
        mid,
        last,
        slope,
        grad,
        back,
        dbm,
        dba,
        dmix,
        dqkv,
        dpos,
        sums,
        outs,
        sem_w,
        sem_in,
        sem_out,
        sem_h,
    ) = refs[16:]
    valid = flags[0]
    slot = flags[1]
    is_last = flags[3]

    @pl.when(valid == 1)
    def _():
        targets = (v_qkv, v_proj, v_fc1, v_fc2)

        def w_copy(kind, block):
            return weight_copies(w_all, targets, sem_w, block)(("fc2", "fc1", "qkv")[kind])

        def proj_copy():
            return Copies(
                [weight_copies(w_all, targets, sem_w, block)("proj").copies[0] for block in range(BLOCKS)]
            )

        def load(index):
            source, target = (
                (cots.at[slot, 0], rcot.at[pl.ds(0, HALF)]),
                (cots.at[slot, 1], rcot.at[pl.ds(HALF, HALF)]),
                (recv_a, rin.at[pl.ds(0, HALF)]),
                (recv_b, rin.at[pl.ds(HALF, HALF)]),
                (out_all.at[slot], last),
                (slope_all.at[slot], slope),
                (mid_all.at[slot], mid),
                (qkv_all.at[slot], qkv.at[pl.ds(0, ROWS)]),
                (probs_all.at[slot], probs),
                (x_all.at[slot], xb),
                (dpos_all, dpos),
            )[index]
            return pltpu.make_async_copy(source, target, sem_in.at[index])

        @pl.when(flags[4] == 0)
        def _():
            load(0).start()
            load(1).start()

        @pl.when(flags[4] == 1)
        def _():
            for half, source in enumerate((cots.at[slot, 1], cots_next.at[slot])):
                pltpu.make_async_copy(
                    source, rcot.at[pl.ds(half * HALF, HALF)], sem_in.at[half]
                ).start()

        load(2).start()
        load(3).start()

        @pl.when(is_last == 1)
        def _():
            load(4).start()

        w_copy(0, 0).start()
        load(5).start()
        w_copy(1, 0).start()
        w_copy(0, 1).start()
        w_copy(1, 1).start()
        for index in range(4):
            load(index).wait()
        sums[...] = jnp.zeros_like(sums)
        grad[...] = dot_nn(perm_in[...], rcot[...])

        @pl.when(is_last == 1)
        def _():
            load(4).wait()

            def final_norm(rows, state):
                cot = grad[rows, :]
                hat, rstd = norm_stats(last[rows, :])
                grad[rows, :] = norm_back(hat, rstd, cot * vecs[6:7, :])
                return (state[0] + fold8(cot * hat), state[1] + fold8(cot))

            zero = jnp.zeros((8, D), F32)
            gain, shift = row_chunks(final_norm, (zero, zero))
            sums[6:7, :] = jnp.sum(gain, 0, keepdims=True)
            sums[7:8, :] = jnp.sum(shift, 0, keepdims=True)

        @pl.when(is_last == 0)
        def _():
            grad[...] += dot_nn(perm_in[...], rin[...])

        def enter(rows, state):
            values = grad[rows, :]
            dbm[rows, :] = values.astype(BF16)
            back[rows, :] = jnp.zeros((STEP, D), F32)
            return state + fold8(values)

        out_sum = row_chunks(enter, jnp.zeros((8, D), F32))
        sums[5:6, :] = jnp.sum(out_sum, 0, keepdims=True)
        saves = [pltpu.make_async_copy(dbm, dbm_all.at[slot], sem_out.at[0])]
        saves[0].start()
        load(5).wait()

        def hidden_save(block):
            columns = lanes(block * FB, FB)
            return pltpu.make_async_copy(
                slope.at[:, columns], slope_all.at[slot, :, columns], sem_h.at[block]
            )

        def hidden_block(block, state):
            columns = lanes(block * FB, FB)
            w_copy(0, block).wait()

            @pl.when(block < BLOCKS - 2)
            def _():
                w_copy(0, block + 2).start()
                w_copy(1, block + 2).start()

            @pl.when(block == BLOCKS - 2)
            def _():
                load(6).start()
                proj_copy().start()
                load(7).start()
                load(8).start()

            dact = dot_nt(dbm[:, :DB], v_fc2[0, block]) + dot_nt(dbm[:, DB:], v_fc2[1, block])
            dpre = (dact * slope[:, columns].astype(F32)).astype(BF16)
            slope[:, columns] = dpre
            hidden_save(block).start()
            sums[pl.ds(8 + block, 1), :] = jnp.sum(dpre.astype(F32), 0, keepdims=True)
            w_copy(1, block).wait()
            for own in range(OWN):
                half = slice(own * DB, (own + 1) * DB)
                back[:, half] += dot_nt(slope[:, columns], v_fc1[own, block])
            return state

        lax.fori_loop(0, BLOCKS, hidden_block, None)
        for block in range(BLOCKS):
            w_copy(2, block).start()
        load(9).start()

        @pl.when(slot > 0)
        def _():
            load(10).start()

        load(6).wait()

        def mlp_norm(rows, state):
            hat, rstd = norm_stats(mid[rows, :])
            ready = back[rows, :]
            values = grad[rows, :] + norm_back(hat, rstd, ready * vecs[1:2, :])
            grad[rows, :] = values
            dba[rows, :] = values.astype(BF16)
            back[rows, :] = jnp.zeros((STEP, D), F32)
            return (state[0] + fold8(ready * hat), state[1] + fold8(ready), state[2] + fold8(values))

        zero = jnp.zeros((8, D), F32)
        gain, shift, out_sum = row_chunks(mlp_norm, (zero, zero, zero))
        sums[1:2, :] = jnp.sum(gain, 0, keepdims=True)
        sums[3:4, :] = jnp.sum(shift, 0, keepdims=True)
        sums[4:5, :] = jnp.sum(out_sum, 0, keepdims=True)
        load(9).wait()
        saves.append(pltpu.make_async_copy(dba, x_all.at[slot], sem_out.at[2]))
        saves[-1].start()
        proj_copy().wait()
        for block in range(BLOCKS):
            out = dot_nt(dba[:, :DB], v_proj[0, block]) + dot_nt(dba[:, DB:], v_proj[1, block])
            dmix[:, block * TB : (block + 1) * TB] = out.astype(BF16)
        load(7).wait()
        load(8).wait()

        @pl.when(slot > 0)
        def _():
            load(10).wait()

        @pl.when(slot == 0)
        def _():
            dpos[...] = jnp.zeros_like(dpos)

        qkv[pl.ds(ROWS, 16), :] = jnp.zeros((16, 3 * D), BF16)
        masks = head_masks()

        def attend_back(group, state):
            column = group_columns(group)
            for win in range(WIN_COLS):
                base = win * PAD
                query = qkv[pl.ds(base, PAD), lanes(column, 128)]
                key = qkv[pl.ds(base, KEYS), lanes(column + TB, 128)]
                value = qkv[pl.ds(base, KEYS), lanes(column + 2 * TB, 128)]
                low = probs[win * GROUPS + group]
                dout = spread_heads(dmix[pl.ds(base, PAD), lanes(group * 128, 128)], masks)
                dprob = dot_nt(dout, value)
                weight = low.astype(F32)
                dscore = weight * (dprob - jnp.sum(dprob * weight, -1, keepdims=True))
                dscore = dscore.astype(BF16)
                dpos[group] += dscore.astype(F32)
                dquery = pick_heads(dot_nn(dscore, key), masks) * HEAD**-0.5
                dkey = dot_tn(dscore, spread_heads(query, masks)) * HEAD**-0.5
                dvalue = dot_tn(low, dout)
                dqkv[pl.ds(base, PAD), lanes(column, 128)] = dquery.astype(BF16)
                dqkv[pl.ds(base, PAD), lanes(column + TB, 128)] = dkey[:PAD].astype(BF16)
                dqkv[pl.ds(base, PAD), lanes(column + 2 * TB, 128)] = dvalue[:PAD].astype(BF16)
            return state

        def attend_back_pair(pair, state):
            return attend_back(2 * pair + 1, attend_back(2 * pair, state))

        lax.fori_loop(0, GROUPS // 2, attend_back_pair, None)
        saves.append(pltpu.make_async_copy(dqkv, qkv_all.at[slot], sem_out.at[3]))
        saves[-1].start()
        saves.append(pltpu.make_async_copy(dpos, dpos_all, sem_out.at[4]))
        saves[-1].start()

        def ready_block(block, state):
            columns = lanes(block * 3 * TB, 3 * TB)
            w_copy(2, block).wait()
            for own in range(OWN):
                half = slice(own * DB, (own + 1) * DB)
                back[:, half] += dot_nt(dqkv[:, columns], v_qkv[own, block])
            return state

        lax.fori_loop(0, BLOCKS, ready_block, None)
        for part in range(3):
            columns = slice(part * D, (part + 1) * D)
            sums[12 + part : 13 + part, :] = jnp.sum(dqkv[:, columns].astype(F32), 0, keepdims=True)

        def attn_norm(rows, state):
            hat, rstd = norm_stats(xb[rows, :].astype(F32))
            ready = back[rows, :]
            values = grad[rows, :] + norm_back(hat, rstd, ready * vecs[0:1, :])
            xb[rows, :] = values.astype(BF16)
            return (state[0] + fold8(ready * hat), state[1] + fold8(ready))

        gain, shift = row_chunks(attn_norm, (zero, zero))
        sums[0:1, :] = jnp.sum(gain, 0, keepdims=True)
        sums[2:3, :] = jnp.sum(shift, 0, keepdims=True)
        saves.append(pltpu.make_async_copy(sums, sums_all.at[slot], sem_out.at[5]))
        saves[-1].start()
        outs[...] = dot_nn(perm_out[...], xb[...]).astype(BF16)
        for half in range(2):
            rows = pl.ds(half * HALF, HALF)
            saves.append(
                pltpu.make_async_copy(outs.at[rows], sends[half], sem_out.at[6 + half])
            )
            saves[-1].start()
            saves.append(
                pltpu.make_async_copy(outs.at[rows], dx_all.at[slot, half], sem_out.at[8 + half])
            )
            saves[-1].start()
        for block in range(BLOCKS):
            saves.append(hidden_save(block))
        for save in saves:
            save.wait()


def any_specs(count):
    return [pl.BlockSpec(memory_space=pl.ANY)] * count


def vmem_specs(count):
    return [pl.BlockSpec(memory_space=pltpu.VMEM)] * count


def shapes_of(arrays):
    return [jax.ShapeDtypeStruct(array.shape, array.dtype) for array in arrays]


WEIGHT_SCRATCH = [
    pltpu.VMEM((OWN, BLOCKS, DB, 3 * TB), BF16),
    pltpu.VMEM((OWN, BLOCKS, TB, DB), BF16),
    pltpu.VMEM((OWN, BLOCKS, DB, FB), BF16),
    pltpu.VMEM((OWN, BLOCKS, FB, DB), BF16),
]


def layer_forward(flags, recv_a, recv_b, firsts, tables, weights, stacks):
    inputs = (flags, recv_a, recv_b, firsts) + tuple(tables) + (weights,) + tuple(stacks)
    first_stack = len(inputs) - len(stacks)
    wide = lambda dtype: pltpu.VMEM((ROWS, D), dtype)
    results = pl.pallas_call(
        forward_kernel,
        out_shape=shapes_of(stacks) + [jax.ShapeDtypeStruct((HALF, D), BF16)] * 2,
        in_specs=[pl.BlockSpec(memory_space=pltpu.SMEM)]
        + any_specs(3)
        + vmem_specs(6)
        + any_specs(2 + len(stacks)),
        out_specs=any_specs(len(stacks) + 2),
        scratch_shapes=WEIGHT_SCRATCH
        + [
            pltpu.VMEM((GROUPS, STACK, KEYS), F32),
            pltpu.VMEM((2 * HALF, D), BF16),
            wide(F32),
            wide(BF16),
            wide(BF16),
            pltpu.VMEM((ROWS + 16, 3 * D), BF16),
            pltpu.VMEM((WIN_COLS * GROUPS, STACK, KEYS), BF16),
            wide(BF16),
            wide(F32),
            wide(BF16),
            pltpu.VMEM((ROWS, FF), BF16),
            pltpu.VMEM((ROWS, FF), BF16),
            wide(F32),
            wide(F32),
            wide(BF16),
            pltpu.VMEM((2 * HALF, D), BF16),
            pltpu.SemaphoreType.DMA((7 * BLOCKS + 1,)),
            pltpu.SemaphoreType.DMA((2,)),
            pltpu.SemaphoreType.DMA((14,)),
            pltpu.SemaphoreType.DMA((2 * BLOCKS,)),
        ],
        input_output_aliases={first_stack + index: index for index in range(len(stacks))},
        compiler_params=pltpu.CompilerParams(vmem_limit_bytes=VMEM_BYTES),
        cost_estimate=pl.CostEstimate(
            flops=24 * ROWS * D * D, bytes_accessed=40 * 1024 * 1024, transcendentals=ROWS * FF
        ),
        name="layer_forward",
    )(*inputs)
    return results[-2:], tuple(results[:-2])


def layer_backward(flags, recv_a, recv_b, cots, cots_next, tables, weights, saved, stacks):
    inputs = (
        (flags, recv_a, recv_b, cots, cots_next)
        + tuple(tables)
        + (weights,)
        + tuple(saved)
        + tuple(stacks)
    )
    first_stack = len(inputs) - len(stacks)
    wide = lambda dtype: pltpu.VMEM((ROWS, D), dtype)
    results = pl.pallas_call(
        backward_kernel,
        out_shape=shapes_of(stacks) + [jax.ShapeDtypeStruct((HALF, D), BF16)] * 2,
        in_specs=[pl.BlockSpec(memory_space=pltpu.SMEM)]
        + any_specs(4)
        + vmem_specs(3)
        + any_specs(1 + len(saved) + len(stacks)),
        out_specs=any_specs(len(stacks) + 2),
        scratch_shapes=WEIGHT_SCRATCH
        + [
            pltpu.VMEM((2 * HALF, D), BF16),
            pltpu.VMEM((2 * HALF, D), BF16),
            wide(BF16),
            pltpu.VMEM((ROWS + 16, 3 * D), BF16),
            pltpu.VMEM((WIN_COLS * GROUPS, STACK, KEYS), BF16),
            wide(F32),
            wide(F32),
            pltpu.VMEM((ROWS, FF), BF16),
            wide(F32),
            wide(F32),
            wide(BF16),
            wide(BF16),
            wide(BF16),
            pltpu.VMEM((ROWS, 3 * D), BF16),
            pltpu.VMEM((GROUPS, STACK, KEYS), F32),
            pltpu.VMEM((SUMS, D), F32),
            pltpu.VMEM((2 * HALF, D), BF16),
            pltpu.SemaphoreType.DMA((7 * BLOCKS,)),
            pltpu.SemaphoreType.DMA((11,)),
            pltpu.SemaphoreType.DMA((10,)),
            pltpu.SemaphoreType.DMA((BLOCKS,)),
        ],
        input_output_aliases={first_stack + index: index for index in range(len(stacks))},
        compiler_params=pltpu.CompilerParams(vmem_limit_bytes=VMEM_BYTES),
        cost_estimate=pl.CostEstimate(
            flops=24 * ROWS * D * D, bytes_accessed=50 * 1024 * 1024, transcendentals=0
        ),
        name="layer_backward",
    )(*inputs)
    return results[-2:], tuple(results[:-2])


def on_device(
    raw_pages,
    w_merge,
    merge_gain,
    merge_bias,
    final_gain,
    final_bias,
    w_qkv,
    w_proj,
    w_fc1,
    w_fc2,
    qv_bias,
    fc1_bias,
    rel_table,
    ln_gain,
    ln_bias,
    out_bias,
    cotangent,
):
    section_now = lax.axis_index("pipe")
    section_count = lax.axis_size("pipe")
    dp_now = lax.axis_index("dp")
    dp_count = lax.axis_size("dp")
    tensor_now = lax.axis_index("tensor")
    tensor_count = lax.axis_size("tensor")
    copies = tensor_count // WIN_ROWS
    unit_now = tensor_now // copies
    all_axes = ("pipe", "dp", "tensor")
    group_axes = ("dp", "tensor")
    is_first = section_now == 0
    is_last = section_now == section_count - 1
    is_odd = section_now % 2 == 1
    owned, _, rows_here, merge_in = raw_pages.shape
    micro_count = cotangent.shape[1]
    own_width = D // dp_count

    def section_pairs(sections, step, moves):
        pairs = []
        for section in sections:
            for tensor in range(tensor_count):
                target = (tensor + copies * moves[section % 2]) % tensor_count
                pairs.append(
                    (section * tensor_count + tensor, (section + step) * tensor_count + target)
                )
        return pairs

    def odd_pairs(move):
        return [
            (
                section * tensor_count + tensor,
                section * tensor_count + (tensor + copies * move) % tensor_count,
            )
            for section in range(1, section_count, 2)
            for tensor in range(tensor_count)
        ]

    def hop(halves, sections, step):
        axes = ("pipe", "tensor")
        to_a = lax.ppermute(halves[1], axes, section_pairs(sections, step, (0, 1)))
        to_b = lax.ppermute(halves[0], axes, section_pairs(sections, step, (-1, 0)))
        return to_a, to_b

    def shares_summed(values, axis):
        count = lax.axis_size(axis)
        index = lax.axis_index(axis)
        blocks = values.reshape((count, values.shape[0] // count) + values.shape[1:])
        total = lax.dynamic_index_in_dim(blocks, index, 0, keepdims=False).astype(F32)
        for step in range(1, count):
            block = lax.dynamic_index_in_dim(blocks, (index + step) % count, 0, keepdims=False)
            pairs = [(source, (source + step) % count) for source in range(count)]
            total = total + lax.ppermute(block, axis, pairs).astype(F32)
        return total

    def summed(values, axis):
        count = lax.axis_size(axis)
        step = 1
        while step < count:
            pairs = [(source, source ^ step) for source in range(count)]
            values = values + lax.ppermute(values, axis, pairs)
            step *= 2
        return values

    def whole_unit(rows, axis):
        if copies == 1:
            return rows
        rows = lax.all_gather(rows, "tensor", axis=axis, tiled=True)
        return lax.dynamic_slice_in_dim(rows, unit_now * UNIT, UNIT, axis)

    def own_part(rows, axis):
        if copies == 1:
            return rows
        return lax.dynamic_slice_in_dim(
            rows, (tensor_now % copies) * rows_here, rows_here, axis
        )

    def gather_rows(values, axes):
        size = values.shape[0]
        tile = 8 * 128
        rows = jnp.pad(values, (0, -size % tile)).reshape(-1, 128)
        rows = lax.all_gather(rows, axes, axis=0, tiled=True)
        return rows.reshape(-1, size + -size % tile)[:, :size]

    def to_halves(rows):
        rows = rows.reshape(rows.shape[:-2] + (2, LINES, D))
        pads = [(0, 0)] * (rows.ndim - 2) + [(0, HALF - LINES), (0, 0)]
        return jnp.pad(rows, pads)

    def from_halves(halves):
        rows = halves[..., :LINES, :]
        return rows.reshape(rows.shape[:-3] + (UNIT, D))

    def stacks_of(*kinds, after=()):
        return pl.pallas_call(
            lambda *refs: None,
            out_shape=[jax.ShapeDtypeStruct(shape, dtype) for shape, dtype in kinds],
            in_specs=any_specs(len(after)),
            out_specs=any_specs(len(kinds)),
        )(*after)

    lined = (dp_count, tensor_count) == (OWN, BLOCKS)

    def block_rows(qkv, proj, fc1, fc2):
        half = DB // 2
        tail = (qkv[..., :half, DB:], qkv[..., half:, DB:])
        rows = (qkv[..., :DB], jnp.concatenate(tail, -1), proj, fc1[..., :DB], fc1[..., DB:], fc2)
        return jnp.concatenate(rows, -2)

    shards = [
        weight.astype(BF16)
        for weight in (w_qkv[0].reshape(own_width, -1), w_proj[0], w_fc1[0], w_fc2[0])
    ]
    if lined:
        weights = lax.all_gather(block_rows(*shards), group_axes, axis=0)
        weights = weights.reshape(OWN, BLOCKS, BLOCK_ROWS, DB)
    else:
        split = (dp_count, tensor_count)
        qkv_full, proj_full, fc1_full, fc2_full = [
            lax.all_gather(shard, group_axes, axis=0).reshape(split + shard.shape)
            for shard in shards
        ]
        qkv_full = qkv_full.reshape(split + (own_width, 3, -1)).transpose(0, 2, 3, 1, 4)
        qkv_full = qkv_full.reshape(OWN, DB, 3, BLOCKS, TB).transpose(0, 3, 1, 2, 4)
        qkv_full = qkv_full.reshape(OWN, BLOCKS, DB, 3 * TB)
        fc1_full = fc1_full.transpose(0, 2, 1, 3).reshape(OWN, DB, BLOCKS, FB)
        fc1_full = fc1_full.transpose(0, 2, 1, 3)
        proj_full, fc2_full = [
            full.transpose(1, 2, 0, 3).reshape(BLOCKS, -1, OWN, DB).transpose(2, 0, 1, 3)
            for full in (proj_full, fc2_full)
        ]
        weights = block_rows(qkv_full, proj_full, fc1_full, fc2_full)

    share = w_merge.shape[0]
    fshare = final_gain.shape[0]
    small = jnp.concatenate((merge_gain, merge_bias, final_gain, final_bias))
    small = jnp.pad(small, (0, 8 * D - small.shape[0])).reshape(8, D)
    packed = jnp.concatenate((w_merge, small)).astype(BF16)

    def passed_round(block, axis):
        count = lax.axis_size(axis)
        index = lax.axis_index(axis)
        parts = [block]
        for step in range(1, count):
            pairs = [(source, (source + step) % count) for source in range(count)]
            parts.append(lax.ppermute(block, axis, pairs))
        parts = parts[::-1]
        return lax.dynamic_slice_in_dim(jnp.stack(parts + parts[:-1]), count - 1 - index, count)

    packed_shape = packed.shape
    packed = passed_round(passed_round(packed, "tensor"), "dp")
    packed = packed.reshape((-1,) + packed_shape)

    packed = passed_round(packed, "pipe").reshape((-1,) + packed_shape)
    merge_weight = packed[:, :share].reshape(merge_in, D)
    small_all = packed[:, share]
    merge_scale = small_all[:, :share].reshape(-1).astype(F32)
    merge_shift = small_all[:, share : 2 * share].reshape(-1).astype(F32)
    final_scale = small_all[:, 2 * share : 2 * share + fshare].reshape(-1).astype(F32)
    final_shift = small_all[:, 2 * share + fshare : 2 * (share + fshare)].reshape(-1).astype(F32)

    mask_all = np.zeros((WIN_ROWS, WIN_COLS, PAD, KEYS), np.float32)
    mask_all[:, :, : WIN * WIN, : WIN * WIN] = shift_mask(
        WIN * WIN_ROWS, GRID_W, WIN, SHIFT
    ).reshape(WIN_ROWS, WIN_COLS, WIN * WIN, WIN * WIN)
    mask_here = lax.dynamic_index_in_dim(jnp.asarray(mask_all, BF16), unit_now, 0, keepdims=False)
    mask_here = mask_here.astype(F32) * is_odd.astype(F32)
    orders = np.stack((window_order(0), window_order(SHIFT)))
    parity = section_now % 2
    perm_in = lax.dynamic_index_in_dim(jnp.asarray(orders, BF16), parity, 0, keepdims=False)
    perm_out = lax.dynamic_index_in_dim(
        jnp.asarray(orders.transpose(0, 2, 1), BF16), parity, 0, keepdims=False
    )
    raw_rows = raw_pages.reshape(owned * rows_here, merge_in).astype(F32)
    raw_hat, raw_rstd = norm_stats(raw_rows)
    merged_in = (raw_hat * merge_scale + merge_shift).astype(BF16)
    merged = dot_nn(merged_in, merge_weight).astype(BF16).reshape(owned, rows_here, D)
    merged = to_halves(whole_unit(merged, 1))
    merged, qv_bias, rel_table = lax.optimization_barrier((merged, qv_bias, rel_table))
    cots = to_halves(whole_unit(cotangent[0, :, 0], 1))
    weights, cots_first = lax.optimization_barrier((weights, cots[:, 0]))
    first_list = [merged]
    for section in range(1, section_count):
        first_list.append(lax.ppermute(merged, "pipe", [(section, 0)]))
    firsts = jnp.concatenate(first_list, 0)

    heads_here = rel_table.shape[2]
    head_set = jnp.concatenate((qv_bias[0].reshape(-1), rel_table[0].reshape(-1)))
    head_set = gather_rows(head_set, "tensor")
    qv_all = head_set[:, : qv_bias.shape[1] * qv_bias.shape[2]].reshape(tensor_count, 2, -1)
    qv_all = qv_all.transpose(1, 0, 2).reshape(2, BLOCKS, TB)
    bias_qkv = jnp.stack((qv_all[0], jnp.zeros_like(qv_all[0]), qv_all[1]), 1).reshape(1, 3 * D)
    table_all = head_set[:, qv_bias.shape[1] * qv_bias.shape[2] :]
    table_all = table_all.reshape(tensor_count, 2 * WIN - 1, 2 * WIN - 1, heads_here)
    table_all = table_all.transpose(0, 3, 1, 2).reshape(D // HEAD, 2 * WIN - 1, 2 * WIN - 1)
    offsets = jnp.asarray(rel_parts(WIN))
    spread = jnp.einsum("huv,vy->huy", table_all, offsets, precision=lax.Precision.HIGHEST)
    spread = jnp.einsum("huy,ux->hxy", spread, offsets, precision=lax.Precision.HIGHEST)
    spread = spread.reshape(D // HEAD, WIN, WIN, WIN, WIN).transpose(0, 1, 3, 2, 4)
    spread = spread.reshape(D // HEAD, WIN * WIN, WIN * WIN)
    bias_pos = jnp.pad(spread, ((0, 0), (0, PAD - WIN * WIN), (0, 0)))
    bias_pos = jnp.pad(
        bias_pos, ((0, 0), (0, 0), (0, KEYS - WIN * WIN)), constant_values=-1e30
    )
    bias_pos = bias_pos.reshape(GROUPS, STACK, KEYS)

    vecs = jnp.concatenate(
        (ln_gain[0], ln_bias[0], out_bias[0], final_scale[None], final_shift[None])
    )
    forward_tables = (perm_in, perm_out, mask_here, vecs, bias_qkv, fc1_bias, bias_pos)
    backward_tables = (perm_in, perm_out, vecs)

    cots_next = lax.ppermute(cots_first, ("pipe", "tensor"), odd_pairs(-1))

    tick_count = micro_count + 2 * (section_count - 1)

    def flags_at(start, tick_now):
        slot_now = tick_now - 2 * start
        is_valid = (slot_now >= 0) & (slot_now < micro_count)
        slot = jnp.clip(slot_now, 0, micro_count - 1)
        return jnp.stack([flag.astype(jnp.int32) for flag in (is_valid, slot, is_first, is_last, is_odd)])

    def of_micro(shape, dtype):
        return ((micro_count,) + shape, dtype)

    *stacks, empty_a, empty_b = stacks_of(
        of_micro((ROWS, D), BF16),
        of_micro((ROWS, 3 * D), BF16),
        of_micro((WIN_COLS * GROUPS, STACK, KEYS), BF16),
        of_micro((ROWS, D), BF16),
        of_micro((ROWS, D), F32),
        of_micro((ROWS, D), BF16),
        of_micro((ROWS, D), BF16),
        of_micro((ROWS, FF), BF16),
        of_micro((ROWS, FF), BF16),
        of_micro((ROWS, D), F32),
        of_micro((2, HALF, D), BF16),
        ((HALF, D), BF16),
        ((HALF, D), BF16),
        after=() if lined else (weights,),
    )
    recv = (empty_a, empty_b)
    for tick_now in range(tick_count):
        coming = recv
        if tick_now > 0:
            coming = hop(outgoing, range(section_count - 1), 1)
        flags = flags_at(section_now, tick_now)
        if tick_now == 2:
            flags, cots_next = lax.optimization_barrier((flags, cots_next))
        outgoing, stacks = layer_forward(
            flags, *recv, firsts, forward_tables, weights, stacks
        )
        recv = coming
    (
        x_all,
        qkv_all,
        probs_all,
        mixed_all,
        mid_all,
        rattn_all,
        rmlp_all,
        act_all,
        slope_all,
        out_all,
        hid_all,
    ) = stacks
    stacks = (
        x_all,
        qkv_all,
        slope_all,
        *stacks_of(
            of_micro((ROWS, D), BF16),
            of_micro((2, HALF, D), BF16),
            of_micro((SUMS, D), F32),
            ((GROUPS, STACK, KEYS), F32),
        ),
    )
    recv = (empty_a, empty_b)
    for tick_now in range(tick_count):
        coming = recv
        if tick_now > 0:
            coming = hop(outgoing, range(1, section_count), -1)
        flags = flags_at(section_count - 1 - section_now, tick_now)
        if tick_now == tick_count - 3:
            flags, hid_before = lax.optimization_barrier((flags, hid_before))
        outgoing, stacks = layer_backward(
            flags,
            *recv,
            cots,
            cots_next,
            backward_tables,
            weights,
            (probs_all, mid_all, out_all),
            stacks,
        )
        recv = coming
        if tick_now == micro_count - 1:
            outgoing, hid_all = lax.optimization_barrier((outgoing, hid_all))
            hid_before = lax.ppermute(hid_all[:, 1], ("pipe", "tensor"), odd_pairs(1))
    dba_all, dqkv_all, dpre_all, dbm_all, dx_all, sums_all, dpos = stacks
    shown = jnp.where(is_odd, jnp.stack((hid_before, hid_all[:, 0]), 1), hid_all)
    shown = own_part(from_halves(shown), 1)

    def weight_gradient(left, right):
        left = left.reshape(micro_count * ROWS, -1)
        right = right.reshape(micro_count * ROWS, D)

        def part(target):
            return dot_tn(
                left, lax.dynamic_slice_in_dim(right, target * own_width, own_width, 1)
            )

        total = None
        for step in range(1, dp_count):
            pairs = [(index, (index + step) % dp_count) for index in range(dp_count)]
            moved = lax.ppermute(
                part((dp_now + step) % dp_count).astype(BF16), "dp", pairs
            ).astype(F32)
            total = moved if total is None else total + moved
        mine = part(dp_now)
        total = mine if total is None else mine + total
        return total / copies

    def over_tensor(*totals):
        totals = [
            total.astype(BF16).reshape(tensor_count, -1, total.shape[1]) for total in totals
        ]
        rows = [total.shape[1] for total in totals]
        total = jnp.concatenate(totals, 1)
        total = lax.psum_scatter(total, "tensor", scatter_dimension=0).astype(F32)
        return jnp.split(total, np.cumsum(rows)[:-1])

    g_proj = weight_gradient(mixed_all, dba_all)
    g_qkv = weight_gradient(dqkv_all, rattn_all)
    if copies > 1:
        g_qkv = g_qkv.reshape(BLOCKS, 3, copies, TB // copies, own_width)
        g_qkv = g_qkv.transpose(0, 2, 1, 3, 4).reshape(3 * D, own_width)
    g_proj, g_qkv, act_all, dbm_all, dpre_all, rmlp_all, dx_all = lax.optimization_barrier(
        (g_proj, g_qkv, act_all, dbm_all, dpre_all, rmlp_all, dx_all)
    )
    g_proj, g_qkv = over_tensor(g_proj, g_qkv)
    g_fc2 = weight_gradient(act_all, dbm_all)
    g_fc2, g_fc1 = over_tensor(g_fc2, weight_gradient(dpre_all, rmlp_all))
    g_fc1 = g_fc1.T
    g_qkv = g_qkv.T.reshape(own_width, 3, D // tensor_count)

    own_grads = dx_all[:owned]
    for section in range(1, section_count):
        moved = lax.ppermute(
            dx_all[section * owned : (section + 1) * owned], "pipe", [(0, section)]
        )
        own_grads = jnp.where(section_now == section, moved, own_grads)
    own_grads, g_proj, g_qkv = lax.optimization_barrier((own_grads, g_proj, g_qkv))
    grad_merged = own_part(from_halves(own_grads), 1).reshape(owned * rows_here, D)
    g_merge = dot_tn(merged_in, grad_merged).astype(BF16)
    g_merge = g_merge.reshape(section_count, dp_count, tensor_count, share, D)
    g_merge = shares_summed(g_merge.transpose(1, 0, 2, 3, 4), "dp")[0].astype(BF16)
    g_merge, dpos = lax.optimization_barrier((g_merge, dpos))
    g_merge = shares_summed(g_merge, "pipe")[0]
    g_merge = shares_summed(g_merge.astype(BF16), "tensor")[0]
    grad_unit = dot_nt(grad_merged, merge_weight)
    merge_sums = jnp.stack((jnp.sum(grad_unit * raw_hat, 0), jnp.sum(grad_unit, 0)))
    grad_raw = norm_back(raw_hat, raw_rstd, grad_unit * merge_scale)
    grad_raw = grad_raw.reshape(raw_pages.shape).astype(BF16)

    sums = jnp.sum(sums_all, 0) / copies
    dpos = dpos.reshape(D // HEAD, PAD, KEYS)[:, : WIN * WIN, : WIN * WIN]
    dpos = dpos.reshape(D // HEAD, WIN, WIN, WIN, WIN).transpose(0, 1, 3, 2, 4)
    dpos = dpos.reshape(D // HEAD, WIN * WIN, WIN * WIN) / copies
    dtable = jnp.einsum("hxy,vy->hxv", dpos, offsets, precision=lax.Precision.HIGHEST)
    dtable = jnp.einsum("hxv,ux->huv", dtable, offsets, precision=lax.Precision.HIGHEST)
    final_sums = sums[6:8] * is_last.astype(F32)
    every = jnp.concatenate((merge_sums.reshape(-1), final_sums.reshape(-1)))
    vector = jnp.concatenate((every, sums.reshape(-1), dtable.reshape(-1)))
    size = vector.shape[0]
    vector = jnp.pad(vector, (0, -size % D)).reshape(-1, 128)
    for axis in group_axes:
        vector = summed(vector, axis)
    edge_rows = every.shape[0] // 128
    edge = summed(vector[:edge_rows], "pipe").reshape(-1)
    local_sums = vector[edge_rows:].reshape(-1)
    sums = local_sums[: SUMS * D].reshape(SUMS, D)
    dtable = local_sums[SUMS * D : SUMS * D + dtable.size].reshape(tensor_count, heads_here, -1)
    g_table = lax.dynamic_index_in_dim(dtable, tensor_now, 0, keepdims=False).T
    dqv = sums[12:15].reshape(BLOCKS, 3, TB)[:, 0::2].transpose(1, 0, 2).reshape(2, D)
    g_qv = lax.dynamic_slice_in_dim(
        dqv, tensor_now * (D // tensor_count), D // tensor_count, 1
    )
    place = (section_now * dp_count + dp_now) * tensor_count + tensor_now
    edge_parts = []
    start = 0
    for size, width in ((merge_in, share), (merge_in, share), (D, fshare), (D, fshare)):
        edge_parts.append(lax.dynamic_slice_in_dim(edge, start + place * width, width))
        start += size
    return (
        shown[None, :, None],
        grad_raw,
        g_merge,
        *edge_parts,
        g_qkv[None],
        g_proj[None],
        g_fc1[None],
        g_fc2[None],
        g_qv[None],
        sums[8:12].reshape(1, FF),
        g_table[None],
        sums[0:2][None],
        sums[2:4][None],
        sums[4:6][None],
    )


def solution(mesh):
    return jax.shard_map(
        on_device,
        mesh=mesh,
        in_specs=(
            P("pipe", "dp", "tensor", None),
            P(("pipe", "dp", "tensor"), None),
            P(("pipe", "dp", "tensor")),
            P(("pipe", "dp", "tensor")),
            P(("pipe", "dp", "tensor")),
            P(("pipe", "dp", "tensor")),
            P("pipe", "dp", None, "tensor"),
            P("pipe", "tensor", "dp"),
            P("pipe", "dp", "tensor"),
            P("pipe", "tensor", "dp"),
            P("pipe", None, "tensor"),
            P("pipe", None),
            P("pipe", None, "tensor"),
            P("pipe", None, None),
            P("pipe", None, None),
            P("pipe", None, None),
            P("pipe", None, "dp", "tensor", None),
        ),
        out_specs=(
            P("pipe", None, "dp", "tensor", None),
            P("pipe", "dp", "tensor", None),
            P(("pipe", "dp", "tensor"), None),
            P(("pipe", "dp", "tensor")),
            P(("pipe", "dp", "tensor")),
            P(("pipe", "dp", "tensor")),
            P(("pipe", "dp", "tensor")),
            P("pipe", "dp", None, "tensor"),
            P("pipe", "tensor", "dp"),
            P("pipe", "dp", "tensor"),
            P("pipe", "tensor", "dp"),
            P("pipe", None, "tensor"),
            P("pipe", None),
            P("pipe", None, "tensor"),
            P("pipe", None, None),
            P("pipe", None, None),
            P("pipe", None, None),
        ),
        check_vma=False,
    )
```
